32 devices in a mesh: seg: 4 (over y, x), seq: 2 (over core), chan: 4 (over z).
Axes of the slice: x: 2, y: 2, z: 4, core: 2. Of those that a mesh axis runs over, the one named last changes fastest.
Arguments:
- sequence_elements: bfloat16 [4, 1024, 2048], P('seg', ('seq', 'chan')), may hold values from -6 to 6
- segment_predecessor_entries: float32 [4, 2, 2048], P('seg'), may hold values from -6 to 6
- opening_recurrences: float32 [4, 64, 2048], P('seg'), may hold values from -12 to 12
- first_layernorm_gain: float32 [2048], replicated, may hold values from 0.5 to 1.5
- first_layernorm_shift_term: float32 [2048], replicated, may hold values from -2 to 2
- lag_blend_coefficients: float32 [2048, 6], replicated, may hold values from 0 to 1
- lag_narrowing_factor: bfloat16 [2048, 160], replicated, may hold values from -0.125 to 0.125
- lag_widening_factors: bfloat16 [2048, 160], replicated, may hold values from -1 to 1
- fading_exponent_baseline: float32 [2048], replicated, as said below
- fading_narrowing_factor: bfloat16 [2048, 64], replicated, may hold values from -0.125 to 0.125
- fading_widening_factor: bfloat16 [2048, 64], replicated, may hold values from -0.75 to 0.75
- present_reward: float32 [2048], replicated, may hold values from -3 to 3
- acceptor_projection: bfloat16 [2048, 2048], P('seg'), may hold values from -0.125 to 0.125
- address_projection: bfloat16 [2048, 2048], P('seg'), may hold values from -0.125 to 0.125
- content_projection: bfloat16 [2048, 2048], P('seg'), may hold values from -0.125 to 0.125
- valve_projection: bfloat16 [2048, 2048], P('seg'), may hold values from -0.125 to 0.125
- timemix_result_projection: bfloat16 [2048, 2048], P('seg'), may hold values from -0.25 to 0.25
- subspace_cluster_gain: float32 [2048], replicated, may hold values from 0.5 to 1.5
- subspace_cluster_shift_term: float32 [2048], replicated, may hold values from -2 to 2
- second_layernorm_gain: float32 [2048], replicated, may hold values from 0.5 to 1.5
- second_layernorm_shift_term: float32 [2048], replicated, may hold values from -2 to 2
- feedforward_lag_blends: float32 [2048, 2], replicated, may hold values from 0 to 1
- feedforward_address_projection: bfloat16 [2048, 7168], P('seg', 'chan'), may hold values from -0.125 to 0.125
- feedforward_acceptor_projection: bfloat16 [2048, 2048], P('seg'), may hold values from -0.125 to 0.125
- feedforward_content_projection: bfloat16 [2048, 7168], P('seg', 'chan'), may hold values from -0.0625 to 0.0625
- result_adjoint: bfloat16 [4, 1024, 2048], P('seg', ('seq', 'chan')), may hold values from -6 to 6
- final_recurrence_adjoint: float32 [4, 8, 64, 2048], P('seg', ('seq', 'chan')), may hold values from -0.8 to 0.8
Outputs:
- output: bfloat16 [4, 1024, 2048], P('seg', ('seq', 'chan'))
- end_states: float32 [4, 8, 64, 2048], P('seg', ('seq', 'chan'))
- input_grad: float32 [4, 1024, 2048], P('seg', ('seq', 'chan'))
- grad_att_norm_gain: float32 [2048], P(('seg', 'seq', 'chan'))
- grad_att_norm_bias: float32 [2048], P(('seg', 'seq', 'chan'))
- grad_token_shift_mix: float32 [2048, 6], P(('seg', 'seq', 'chan'))
- shift_down_gradient: float32 [2048, 160], P(('seg', 'seq', 'chan'))
- shift_up_gradient: float32 [2048, 160], P(('seg', 'seq', 'chan'))
- grad_decay_base: float32 [2048], P(('seg', 'seq', 'chan'))
- grad_decay_down: float32 [2048, 64], P(('seg', 'seq', 'chan'))
- grad_decay_up: float32 [2048, 64], P(('seg', 'seq', 'chan'))
- reward_coefficient_sensitivity: float32 [2048], P(('seg', 'seq', 'chan'))
- grad_w_recept: float32 [2048, 2048], P(('seg', 'seq', 'chan'))
- grad_w_key: float32 [2048, 2048], P(('seg', 'seq', 'chan'))
- grad_w_value: float32 [2048, 2048], P(('seg', 'seq', 'chan'))
- grad_w_gate: float32 [2048, 2048], P(('seg', 'seq', 'chan'))
- grad_w_output: float32 [2048, 2048], P(('seg', 'seq', 'chan'))
- grad_group_gain: float32 [2048], P(('seg', 'seq', 'chan'))
- grad_group_bias: float32 [2048], P(('seg', 'seq', 'chan'))
- grad_ffn_norm_gain: float32 [2048], P(('seg', 'seq', 'chan'))
- grad_ffn_norm_bias: float32 [2048], P(('seg', 'seq', 'chan'))
- grad_ffn_shift_mix: float32 [2048, 2], P(('seg', 'seq', 'chan'))
- grad_ffn_key: float32 [2048, 7168], P(('seg', 'seq'), 'chan')
- grad_ffn_recept: float32 [2048, 2048], P(('seg', 'seq', 'chan'))
- grad_ffn_value: float32 [2048, 7168], P(('seg', 'seq'), 'chan')
The draws below stay inside these ranges and needn't reach their ends.
Inputs may be any that keep to these rules, and one draw needn't show every extreme that they name: `fading_exponent_baseline`: offsets of the decay's inner exponent lie between ln 0.1 - ln 1024 and ln 0.1.
All inputs are finite; a program needn't handle non-finite values.
Results may differ from the reference program's by a relative error of at most 0.03.
Values may be sent and summed in bfloat16 or wider, within the bound.
No kernel may reach another device: no remote copies, remote signals or barrier semaphores. Data moves between devices by JAX's collectives and lax.ppermute only.
A program may use at most 384 MiB of HBM per device.

```python
import math
import jax
import jax.numpy as jnp
from jax import lax

EMBEDDING_SIZE = 2048
SUBSPACE_SIZE = 64
FF = 7168
SHIFT_RANK = 32
DECAY_RANK = 64
TOK_DEV = 128
SEGMENTS = 4
SPANS = 8
SEG_LEN = 1024


def draw_fading_exponent_baseline(key, part):
    key = jax.random.fold_in(key, 7)
    head_key, slow_key, fast_key = jax.random.split(key, 3)
    slow_share = 0.5
    subspace_count = EMBEDDING_SIZE // SUBSPACE_SIZE
    slow_heads = jax.random.uniform(head_key, (subspace_count, 1)) < slow_share
    slow_log = jax.random.uniform(slow_key, (subspace_count, SUBSPACE_SIZE), minval=math.log(0.1), maxval=math.log(1.5)) - math.log(SEG_LEN)
    fast_log = jax.random.uniform(fast_key, (subspace_count, SUBSPACE_SIZE), minval=math.log(0.02), maxval=math.log(0.1))
    return jnp.where(slow_heads, slow_log, fast_log).reshape(EMBEDDING_SIZE).astype(jnp.float32)


def block_levels(key, dims, shards, low, largest):
    gain = 1.0
    for position, parts in shards:
        heights = jax.random.uniform(jax.random.fold_in(jax.random.fold_in(key, 6), position), (parts,), jnp.float32, low / len(shards), largest / len(shards))
        gain = gain * jnp.repeat(jnp.exp(heights), dims[position] // parts).reshape((-1,) + (1,) * (len(dims) - 1 - position))
    return gain


def scatter_about(own_key, dims, width, reach, pieces=(), dtype=jnp.bfloat16):
    factor_of = block_levels(own_key, dims, pieces, -0.22, 0.18) if pieces else 1.0
    values = jax.random.normal(own_key, dims, jnp.float32) * width * factor_of
    return jnp.minimum(jnp.maximum(values, -reach), reach).astype(dtype)


def setup_inputs(seed: int = 0) -> dict:
    keys = jax.random.split(jax.random.key(seed), 28)
    return {
        "sequence_elements": scatter_about(keys[0], (SEGMENTS, SEG_LEN, EMBEDDING_SIZE), 1.0, 6.0, ((0, 4), (1, 8))),
        "segment_predecessor_entries": scatter_about(keys[1], (SEGMENTS, 2, EMBEDDING_SIZE), 1.0, 6.0, ((0, 4),), jnp.float32),
        "opening_recurrences": scatter_about(keys[2], (SEGMENTS, SUBSPACE_SIZE, EMBEDDING_SIZE), 2.0, 12.0, ((0, 4),), jnp.float32),
        "first_layernorm_gain": jnp.clip(1.0 + 0.1 * jax.random.normal(keys[3], (EMBEDDING_SIZE,), jnp.float32), 0.5, 1.5),
        "first_layernorm_shift_term": scatter_about(keys[4], (EMBEDDING_SIZE,), 0.3, 2.0, (), jnp.float32),
        "lag_blend_coefficients": jnp.clip(jax.random.uniform(keys[5], (EMBEDDING_SIZE, 6), jnp.float32, 0.0, 1.0), 0.0, 1.0),
        "lag_narrowing_factor": scatter_about(keys[6], (EMBEDDING_SIZE, 5 * SHIFT_RANK), EMBEDDING_SIZE ** -0.5, 0.125),
        "lag_widening_factors": scatter_about(keys[7], (EMBEDDING_SIZE, 5 * SHIFT_RANK), SHIFT_RANK ** -0.5, 1.0),
        "fading_exponent_baseline": draw_fading_exponent_baseline(jax.random.fold_in(keys[27], 71), 0),
        "fading_narrowing_factor": scatter_about(keys[9], (EMBEDDING_SIZE, DECAY_RANK), EMBEDDING_SIZE ** -0.5, 0.125),
        "fading_widening_factor": scatter_about(keys[10], (EMBEDDING_SIZE, DECAY_RANK), DECAY_RANK ** -0.5, 0.75),
        "present_reward": scatter_about(keys[11], (EMBEDDING_SIZE,), 0.5, 3.0, (), jnp.float32),
        "acceptor_projection": scatter_about(keys[12], (EMBEDDING_SIZE, EMBEDDING_SIZE), EMBEDDING_SIZE ** -0.5, 0.125, ((0, 4),)),
        "address_projection": scatter_about(keys[13], (EMBEDDING_SIZE, EMBEDDING_SIZE), EMBEDDING_SIZE ** -0.5, 0.125, ((0, 4),)),
        "content_projection": scatter_about(keys[14], (EMBEDDING_SIZE, EMBEDDING_SIZE), EMBEDDING_SIZE ** -0.5, 0.125, ((0, 4),)),
        "valve_projection": scatter_about(keys[15], (EMBEDDING_SIZE, EMBEDDING_SIZE), EMBEDDING_SIZE ** -0.5, 0.125, ((0, 4),)),
        "timemix_result_projection": scatter_about(keys[16], (EMBEDDING_SIZE, EMBEDDING_SIZE), (EMBEDDING_SIZE // 4) ** -0.5, 0.25, ((0, 4),)),
        "subspace_cluster_gain": jnp.clip(1.0 + 0.1 * jax.random.normal(keys[17], (EMBEDDING_SIZE,), jnp.float32), 0.5, 1.5),
        "subspace_cluster_shift_term": scatter_about(keys[18], (EMBEDDING_SIZE,), 0.3, 2.0, (), jnp.float32),
        "second_layernorm_gain": jnp.clip(1.0 + 0.1 * jax.random.normal(keys[19], (EMBEDDING_SIZE,), jnp.float32), 0.5, 1.5),
        "second_layernorm_shift_term": scatter_about(keys[20], (EMBEDDING_SIZE,), 0.3, 2.0, (), jnp.float32),
        "feedforward_lag_blends": jnp.clip(jax.random.uniform(keys[21], (EMBEDDING_SIZE, 2), jnp.float32, 0.0, 1.0), 0.0, 1.0),
        "feedforward_address_projection": scatter_about(keys[22], (EMBEDDING_SIZE, FF), EMBEDDING_SIZE ** -0.5, 0.125, ((0, 4), (1, 4))),
        "feedforward_acceptor_projection": scatter_about(keys[23], (EMBEDDING_SIZE, EMBEDDING_SIZE), EMBEDDING_SIZE ** -0.5, 0.125, ((0, 4),)),
        "feedforward_content_projection": scatter_about(keys[24], (EMBEDDING_SIZE, FF), FF ** -0.5, 0.0625, ((0, 4), (1, 4))),
        "result_adjoint": scatter_about(keys[25], (SEGMENTS, SEG_LEN, EMBEDDING_SIZE), 1.0, 6.0, ((0, 4), (1, 8))),
        "final_recurrence_adjoint": scatter_about(keys[26], (SEGMENTS, SPANS, SUBSPACE_SIZE, EMBEDDING_SIZE), 0.1, 0.8, ((0, 4), (1, 8)), jnp.float32),
    }


@jax.custom_vjp
def lowrank_values(v):
    return lax.optimization_barrier(v.astype(jnp.bfloat16)).astype(jnp.float32)

@jax.custom_vjp
def low_back(v):
    return v

def low_keep(v):
    return (lowrank_values(v), None)

def low_pass(kept, grad):
    return (grad,)

def back_keep(v):
    return (v, None)

def back_low(kept, grad):
    return (lowrank_values(grad),)
lowrank_values.defvjp(low_keep, low_pass)
low_back.defvjp(back_keep, back_low)
EXACT_ARITHMETIC = lax.Precision.HIGHEST
LAYER_EPSILON = 1e-05
GROUP_EPSILON = 0.00064

def product_value(left_side, right_side):
    return jnp.dot(left_side, right_side, precision=EXACT_ARITHMETIC, preferred_element_type=jnp.float32)

def product_across(left_side, right_side):
    return lax.dot_general(left_side, right_side, (((1,), (1,)), ((), ())), precision=EXACT_ARITHMETIC, preferred_element_type=jnp.float32)

def layer_norm(values, scale_gain, shift_bias):
    center = values - lax.optimization_barrier(jnp.mean(values, -1, keepdims=True))
    spread = lax.optimization_barrier(jnp.mean(center * center, -1, keepdims=True))
    return center * lax.rsqrt(spread + LAYER_EPSILON) * scale_gain + shift_bias

def shifted_rows(values, first_row):
    return jnp.concatenate([first_row[None, :], values[:-1]], 0)

def wkv_token(handed_recurrence, token_items):
    recurrence_content, subspace_reward = handed_recurrence
    acceptor_entries, address_entries, content_entries, fading_exponent_entries = token_items
    address_content_tensor = address_entries[:, :, None] * content_entries[:, None, :]
    produced_recurrence = lax.optimization_barrier(jnp.sum(acceptor_entries[:, :, None] * (recurrence_content + subspace_reward[:, :, None] * address_content_tensor), 1))
    recurrence_content = jnp.exp(fading_exponent_entries)[:, :, None] * recurrence_content + address_content_tensor
    return ((recurrence_content, subspace_reward), produced_recurrence)

def blend_extent(handed_recurrence, span_items):
    handed_recurrence, produced_recurrence = lax.scan(wkv_token, handed_recurrence, span_items)
    return (handed_recurrence, (produced_recurrence, handed_recurrence[0]))

def segment_forward(learnable_settings, inputs, shift_pair, opening_recurrence):
    first_layernorm_gain, first_layernorm_shift_term, lag_blend_coefficients, lag_narrowing_factor, lag_widening_factors, fading_exponent_baseline, fading_narrowing_factor, fading_widening_factor, present_reward, acceptor_projection, address_projection, content_projection, valve_projection, timemix_result_projection, subspace_cluster_gain, subspace_cluster_shift_term, second_layernorm_gain, second_layernorm_shift_term, feedforward_lag_blends, feedforward_address_projection, feedforward_acceptor_projection, feedforward_content_projection = learnable_settings
    number_tokens, embedding_breadth = inputs.shape
    subspace_count = embedding_breadth // SUBSPACE_SIZE
    normed_input = layer_norm(inputs, first_layernorm_gain, first_layernorm_shift_term)
    shift_difference = shifted_rows(normed_input, shift_pair[0]) - normed_input
    shift_low_input = lowrank_values(normed_input + shift_difference * lag_blend_coefficients[:, 0])
    shift_low_middle = lowrank_values(jnp.tanh(product_value(shift_low_input, lag_narrowing_factor)))
    shift_modifiers = jnp.einsum('phy,shy->hps', shift_low_middle.reshape(number_tokens, 5, SHIFT_RANK), lag_widening_factors.reshape(embedding_breadth, 5, SHIFT_RANK), precision=EXACT_ARITHMETIC)
    mixed_rows = [lowrank_values(normed_input + shift_difference * (lag_blend_coefficients[:, column + 1] + shift_modifiers[column])) for column in range(5)]
    decay_mid = lowrank_values(jnp.tanh(product_value(mixed_rows[0], fading_narrowing_factor)))
    fading_exponent_level = -jnp.exp(fading_exponent_baseline + product_across(decay_mid, fading_widening_factor))
    acceptor_entries = lowrank_values(low_back(product_value(mixed_rows[3], acceptor_projection)))
    address_entries = lowrank_values(low_back(product_value(mixed_rows[1], address_projection)))
    content_entries = lowrank_values(low_back(product_value(mixed_rows[2], content_projection)))
    gate_raw = low_back(product_value(mixed_rows[4], valve_projection))

    def interval_contents(values):
        return values.reshape(number_tokens // TOK_DEV, TOK_DEV, subspace_count, SUBSPACE_SIZE)
    recurrence_opening = jnp.transpose(opening_recurrence.reshape(SUBSPACE_SIZE, subspace_count, SUBSPACE_SIZE), (1, 0, 2))
    handed_recurrence, (produced_recurrence, recurrence_sequence) = lax.scan(jax.checkpoint(blend_extent), (recurrence_opening, present_reward.reshape(subspace_count, SUBSPACE_SIZE)), (interval_contents(acceptor_entries), interval_contents(address_entries), interval_contents(content_entries), interval_contents(fading_exponent_level)))
    wkv_rows = produced_recurrence.reshape(number_tokens, subspace_count, SUBSPACE_SIZE)
    center = wkv_rows - lax.optimization_barrier(jnp.mean(wkv_rows, -1, keepdims=True))
    spread = lax.optimization_barrier(jnp.mean(center * center, -1, keepdims=True))
    grouped = (center * lax.rsqrt(spread + GROUP_EPSILON)).reshape(number_tokens, embedding_breadth) * subspace_cluster_gain + subspace_cluster_shift_term
    gated_rows = lowrank_values(grouped * jax.nn.silu(gate_raw))
    residual = inputs + low_back(product_value(gated_rows, timemix_result_projection))
    ffn_normed = layer_norm(residual, second_layernorm_gain, second_layernorm_shift_term)
    ffn_delta = shifted_rows(ffn_normed, shift_pair[1]) - ffn_normed
    ffn_key_in = lowrank_values(ffn_normed + ffn_delta * feedforward_lag_blends[:, 0])
    ffn_recept_in = lowrank_values(ffn_normed + ffn_delta * feedforward_lag_blends[:, 1])
    hidden = low_back(product_value(ffn_key_in, feedforward_address_projection))
    squared = lowrank_values(jnp.square(jax.nn.relu(hidden)))
    ffn_values = low_back(product_across(squared, feedforward_content_projection))
    ffn_gate = jax.nn.sigmoid(low_back(product_value(ffn_recept_in, feedforward_acceptor_projection)))
    result = residual + ffn_gate * ffn_values
    end_rows = jnp.transpose(recurrence_sequence, (0, 2, 1, 3)).reshape(number_tokens // TOK_DEV, SUBSPACE_SIZE, embedding_breadth)
    return (result, end_rows)

def reference(sequence_elements, segment_predecessor_entries, opening_recurrences, first_layernorm_gain, first_layernorm_shift_term, lag_blend_coefficients, lag_narrowing_factor, lag_widening_factors, fading_exponent_baseline, fading_narrowing_factor, fading_widening_factor, present_reward, acceptor_projection, address_projection, content_projection, valve_projection, timemix_result_projection, subspace_cluster_gain, subspace_cluster_shift_term, second_layernorm_gain, second_layernorm_shift_term, feedforward_lag_blends, feedforward_address_projection, feedforward_acceptor_projection, feedforward_content_projection, result_adjoint, final_recurrence_adjoint):
    learnable_settings = tuple((coefficient_array.astype(jnp.float32) for coefficient_array in (first_layernorm_gain, first_layernorm_shift_term, lag_blend_coefficients, lag_narrowing_factor, lag_widening_factors, fading_exponent_baseline, fading_narrowing_factor, fading_widening_factor, present_reward, acceptor_projection, address_projection, content_projection, valve_projection, timemix_result_projection, subspace_cluster_gain, subspace_cluster_shift_term, second_layernorm_gain, second_layernorm_shift_term, feedforward_lag_blends, feedforward_address_projection, feedforward_acceptor_projection, feedforward_content_projection)))

    def one_segment(totals, segment_items):
        inputs, shift_pair, opening_recurrence, cotangent, state_cotangent = segment_items

        def forward(weights, values):
            return segment_forward(weights, values, shift_pair, opening_recurrence)
        (result, end_rows), pullback = jax.vjp(forward, learnable_settings, inputs.astype(jnp.float32))
        grad_params, grad_inputs = pullback((cotangent.astype(jnp.float32), state_cotangent))
        totals = jax.tree.map(jnp.add, totals, grad_params)
        return (totals, (result.astype(jnp.bfloat16), end_rows, grad_inputs))
    zero_grads = jax.tree.map(jnp.zeros_like, learnable_settings)
    totals, (outputs, end_states, input_grads) = lax.scan(one_segment, zero_grads, (sequence_elements, segment_predecessor_entries, opening_recurrences, result_adjoint, final_recurrence_adjoint))
    return (outputs, end_states, input_grads, totals[0], totals[1], totals[2], totals[3], totals[4], totals[5], totals[6], totals[7], totals[8], totals[9], totals[10], totals[11], totals[12], totals[13], totals[14], totals[15], totals[16], totals[17], totals[18], totals[19], totals[20], totals[21])
```

```python
import jax
import jax.numpy as jnp
from jax import lax
from jax.experimental import pallas as pl
from jax.experimental.pallas import tpu as pltpu
from jax.sharding import PartitionSpec as P

HEAD = 64
TP = ("seq", "chan")
ALL = ("seg", "seq", "chan")
LAYER_EPSILON = 1e-05
GROUP_EPSILON = 0.00064
F32 = jnp.float32
BF16 = jnp.bfloat16
CHUNK = 256
VMEM = 56 * 2**20


def dot(a, b, dims):
    return lax.dot_general(
        a.astype(BF16), b.astype(BF16), (dims, ((), ())), preferred_element_type=F32
    )


def nn(a, b):
    return dot(a, b, ((1,), (0,)))


def nt(a, b):
    return dot(a, b, ((1,), (1,)))


def tn(a, b):
    return dot(a, b, ((0,), (0,)))


def iota(shape, axis):
    return lax.broadcasted_iota(jnp.int32, shape, axis)


def head_sum(values, ones):
    high = values.astype(BF16)
    low = (values - high.astype(F32)).astype(BF16)
    return nn(high, ones) + nn(low, ones)


def pyramid(w):
    length = w.shape[0]
    row = iota(w.shape, 0)
    before, after, total = jnp.zeros_like(w), jnp.zeros_like(w), w
    levels = []
    half = 1
    while half < length:
        upper = (row & half) != 0
        levels.append((half, upper, jnp.where(upper, before, after)))
        sibling = jnp.where(upper, pltpu.roll(total, half, 0), pltpu.roll(total, length - half, 0))
        before = jnp.where(upper, before + sibling, before)
        after = jnp.where(upper, after, after + sibling)
        total = total + sibling
        half *= 2
    return levels, before, after, total


def split_heads(values, heads):
    if heads == 1:
        return [values.astype(BF16)]
    lane = iota(values.shape, 1) // HEAD
    return [jnp.where(lane == head, values, 0.0).astype(BF16) for head in range(heads)]


def row_stats(x_ref):
    rows, width = x_ref.shape
    step = 128
    total = jnp.zeros((rows, step), F32)
    for at in range(0, width, step):
        total = total + x_ref[:, at : at + step].astype(F32)
    mean = jnp.sum(total, 1, keepdims=True) / width
    total = jnp.zeros((rows, step), F32)
    for at in range(0, width, step):
        center = x_ref[:, at : at + step].astype(F32) - mean
        total = total + center * center
    return mean, lax.rsqrt(jnp.sum(total, 1, keepdims=True) / width + LAYER_EPSILON)


def fold(values):
    rows, width = values.shape
    return jnp.sum(values.reshape(rows // 8, 8, width), 0)


def rank_blocks(values, rank):
    lane = iota(values.shape, 1) // rank
    return jnp.concatenate([jnp.where(lane == j, values, 0.0).astype(BF16) for j in range(5)], 0)


GAIN, BIAS, MIX, FIRST = 0, 1, 2, 8


def mix_forward(
    rank, x_ref, rows_ref, own_ref, wn_ref, wwt_ref, fn_ref, fwt_ref, wr_ref, wk_ref, wv_ref, wg_ref,
    ones_ref, start_ref,
    xk_ref, xv_ref, xr_ref, xg_ref, r_ref, k_ref, v_ref, w_ref, graw_ref, wkv_ref, gated_ref, lm_ref, dm_ref,
    ends_ref, normed_ref, delta_ref, carry_ref, state_ref,
):
    step = pl.program_id(0)
    length, width = x_ref.shape
    own = own_ref.shape[1]
    heads = own // HEAD

    @pl.when(step == 0)
    def _():
        carry_ref[...] = jnp.broadcast_to(rows_ref[FIRST : FIRST + 1, :], carry_ref.shape)
        state_ref[...] = start_ref[...]

    mean, scale = row_stats(x_ref)
    first = iota((length, CHUNK), 0) == 0
    narrow = jnp.zeros((length, wn_ref.shape[1]), F32)
    for at in range(0, width, CHUNK):
        c = slice(at, at + CHUNK)
        normed = (x_ref[:, c].astype(F32) - mean) * scale * rows_ref[GAIN : GAIN + 1, c] + rows_ref[BIAS : BIAS + 1, c]
        delta = jnp.where(first, carry_ref[0:1, c], pltpu.roll(normed, 1, 0)) - normed
        carry_ref[0:1, c] = normed[length - 1 : length, :]
        normed_ref[:, c] = normed
        delta_ref[:, c] = delta
        narrow = narrow + nn(normed + delta * rows_ref[MIX : MIX + 1, c], wn_ref[c, :])
    middle = jnp.tanh(narrow)
    lm_ref[...] = middle
    blocks = rank_blocks(middle, rank)
    decay_in = jnp.zeros((length, fn_ref.shape[1]), F32)
    for at in range(0, width, CHUNK):
        c = slice(at, at + CHUNK)
        normed, delta = normed_ref[:, c], delta_ref[:, c]
        modifiers = nn(blocks, wwt_ref[:, c])
        for j, ref in enumerate((None, xk_ref, xv_ref, xr_ref, xg_ref)):
            modifier = modifiers[j * length : (j + 1) * length, :]
            mixed = (normed + delta * (rows_ref[MIX + 1 + j : MIX + 2 + j, c] + modifier)).astype(BF16)
            if ref is None:
                decay_in = decay_in + nn(mixed, fn_ref[c, :])
            else:
                ref[:, c] = mixed
    decay_mid = jnp.tanh(decay_in)
    dm_ref[...] = decay_mid
    w = -jnp.exp(own_ref[0:1, :] + nn(decay_mid, fwt_ref[...]))
    w_ref[...] = w
    r = nn(xr_ref[...], wr_ref[...]).astype(BF16)
    k = nn(xk_ref[...], wk_ref[...]).astype(BF16)
    v = nn(xv_ref[...], wv_ref[...]).astype(BF16)
    graw = nn(xg_ref[...], wg_ref[...])
    r_ref[...], k_ref[...], v_ref[...], graw_ref[...] = r, k, v, graw

    rf, kf, vf = r.astype(F32), k.astype(F32), v.astype(F32)
    levels, before, after, total = pyramid(w)
    row, col = iota((length, length), 0), iota((length, length), 1)
    apart = jnp.where(row > col, row ^ col, 0)
    scores = [jnp.zeros((length, length), F32)] * heads
    for half, upper, exponent in levels:
        scaled = jnp.where(upper, rf, kf) * jnp.exp(exponent)
        flat = scaled.astype(BF16)
        here = (apart >= half) & (apart < 2 * half)
        for head, one in enumerate(split_heads(scaled, heads)):
            scores[head] = jnp.where(here, nt(one, flat), scores[head])
    ones = ones_ref[...]
    wkv = nn(jnp.concatenate([s.astype(BF16) for s in scores], 1), jnp.concatenate(split_heads(vf, heads), 0))
    state = state_ref[...]
    wkv = wkv + nt(rf * jnp.exp(before), state) + head_sum(rf * own_ref[1:2, :] * kf, ones) * vf
    wkv_ref[...] = wkv
    state = state * jnp.exp(total[0:1, :]) + tn(v, kf * jnp.exp(after)) * ones.astype(F32)
    state_ref[...] = state
    ends_ref[0] = state

    center = wkv - head_sum(wkv, ones) / HEAD
    spread = head_sum(center * center, ones) / HEAD
    grouped = center * lax.rsqrt(spread + GROUP_EPSILON) * own_ref[2:3, :] + own_ref[3:4, :]
    gated_ref[...] = (grouped * graw * jax.nn.sigmoid(graw)).astype(BF16)


def wkv_backward(
    count, d_ref, r_ref, k_ref, v_ref, w_ref, graw_ref, wkv_ref, own_ref, ones_ref, sums_ref, start_ref, ends_ref,
    adj_ref,
    dr_ref, dk_ref, dv_ref, dg_ref, dpre_ref, own_sums_ref, state_ref,
):
    step = pl.program_id(0)
    length, own = d_ref.shape
    heads = own // HEAD
    ones = ones_ref[...]

    @pl.when(step == 0)
    def _():
        state_ref[...] = jnp.zeros_like(state_ref)
        own_sums_ref[...] = jnp.zeros_like(own_sums_ref)

    reward, gain, bias = own_ref[1:2, :], own_ref[2:3, :], own_ref[3:4, :]
    wkv, graw, d_gated = wkv_ref[...], graw_ref[...], d_ref[...]
    center = wkv - head_sum(wkv, ones) / HEAD
    scale = lax.rsqrt(head_sum(center * center, ones) / HEAD + GROUP_EPSILON)
    normed = center * scale
    sigma = jax.nn.sigmoid(graw)
    d_grouped = d_gated * graw * sigma
    dg_ref[...] = (d_gated * (normed * gain + bias) * sigma * (1.0 + graw * (1.0 - sigma))).astype(BF16)
    d_normed = d_grouped * gain
    do = scale * (d_normed - head_sum(d_normed, ones) / HEAD - normed * (head_sum(d_normed * normed, ones) / HEAD))

    rb, kb, vb, dob = r_ref[...], k_ref[...], v_ref[...], do.astype(BF16)
    r, k, v, w = rb.astype(F32), kb.astype(F32), vb.astype(F32), w_ref[...]
    levels, before, after, total = pyramid(w)
    d_state = state_ref[...] + adj_ref[0]
    state = jnp.where(step == count - 1, start_ref[...], ends_ref[0])
    d_flat, flat = d_state.astype(BF16), state.astype(BF16)
    from_start, to_end, decay = jnp.exp(before), jnp.exp(after), jnp.exp(total[0:1, :])
    dr = from_start * nn(dob, flat)
    dk = to_end * nn(vb, d_flat)
    dv = nt(k * to_end, d_flat)
    through = [r * dr, k * dk]
    state_ref[...] = d_state * decay + tn(dob, r * from_start) * ones.astype(F32)
    whole = decay * jnp.sum(state * d_state, 0, keepdims=True)

    row, col = iota((length, length), 0), iota((length, length), 1)
    apart = row ^ col
    do_heads, v_heads = split_heads(do, heads), split_heads(v, heads)
    d_scores = [
        jnp.where(row > col, nt(do_heads[h], vb), jnp.where(row < col, nt(v_heads[h], dob), 0.0)).astype(BF16)
        for h in range(heads)
    ]
    scores = [jnp.zeros((length, length), F32)] * heads
    for half, upper, exponent in levels:
        factor = jnp.exp(exponent)
        scaled = jnp.where(upper, r, k) * factor
        mine = split_heads(scaled, heads)
        here = (apart >= half) & (apart < 2 * half)
        late = here & (row < col)
        for h in range(heads):
            scores[h] = jnp.where(late, nt(mine[h], scaled), scores[h])
        pulled = nn(
            jnp.concatenate([jnp.where(here, d, 0.0).astype(BF16) for d in d_scores], 1), jnp.concatenate(mine, 0)
        )
        if half > 1:
            through.append(scaled * pulled)
        pulled = pulled * factor
        dr = dr + jnp.where(upper, pulled, 0.0)
        dk = dk + jnp.where(upper, 0.0, pulled)
    dv = dv + nn(jnp.concatenate([s.astype(BF16) for s in scores], 1), jnp.concatenate(do_heads, 0))
    met = head_sum(v * do, ones)
    dr = dr + reward * k * met
    dk = dk + reward * r * met
    dv = dv + head_sum(r * reward * k, ones) * do
    d_log = whole + nn(sums_ref[...], jnp.concatenate([q.astype(BF16) for q in through], 0))
    d_pre = d_log * w
    dr_ref[...], dk_ref[...], dv_ref[...] = dr.astype(BF16), dk.astype(BF16), dv.astype(BF16)
    dpre_ref[...] = d_pre
    for i, part in enumerate((d_pre, r * k * met, d_grouped * normed, d_grouped)):
        own_sums_ref[8 * i : 8 * i + 8, :] += fold(part)


def sum_table(length):
    row, col = iota((length, length), 0), iota((length, length), 1)
    tables = [col > row, col < row]
    half = 2
    while half < length:
        inside = (row // half) == (col // half)
        upper = (row // half) % 2 == 1
        tables.append(inside & jnp.where(upper, col > row, col < row))
        half *= 2
    return jnp.concatenate(tables, 1).astype(BF16)


def mix_backward(
    rank, count, x_ref, edge_ref, rows_ref, lm_ref, dm_ref, dr_ref, dk_ref, dv_ref, dg_ref, dpre_ref,
    wn_ref, ww_ref, wwt_ref, fn_ref, fwt_ref, wr_ref, wk_ref, wv_ref, wg_ref,
    dx_ref, row_sums_ref, up_ref, down_ref, decay_down_ref, decay_up_ref,
    sum_ref, coef_ref, normed_ref, delta_ref, carry_ref,
):
    step = pl.program_id(0)
    length, width = x_ref.shape

    @pl.when(step == 0)
    def _():
        carry_ref[...] = jnp.zeros_like(carry_ref)
        for ref in (row_sums_ref, up_ref, down_ref, decay_down_ref, decay_up_ref):
            ref[...] = jnp.zeros_like(ref)

    mean, scale = row_stats(x_ref)
    edge = edge_ref.shape[0]
    edge_mean, edge_scale = row_stats(edge_ref)
    middle, decay_mid = lm_ref[...], dm_ref[...]
    blocks = rank_blocks(middle, rank)
    d_pre = dpre_ref[...]
    decay_up_ref[...] += tn(decay_mid, d_pre)
    d_decay = (nt(d_pre, fwt_ref[...]) * (1.0 - decay_mid * decay_mid)).astype(BF16)
    sources = (
        (d_decay, fn_ref), (dk_ref[...], wk_ref), (dv_ref[...], wv_ref), (dr_ref[...], wr_ref), (dg_ref[...], wg_ref),
    )
    first = iota((length, CHUNK), 0) == 0
    last = iota((length, CHUNK), 0) == length - 1
    d_mid = jnp.zeros((5 * length, wn_ref.shape[1]), F32)
    for at in range(0, width, CHUNK):
        c = slice(at, at + CHUNK)
        gain, bias = rows_ref[GAIN : GAIN + 1, c], rows_ref[BIAS : BIAS + 1, c]
        normed = (x_ref[:, c].astype(F32) - mean) * scale * gain + bias
        edge_normed = (edge_ref[:, c].astype(F32) - edge_mean) * edge_scale * gain + bias
        before = jnp.where(step == count - 1, rows_ref[FIRST : FIRST + 1, c], edge_normed[edge - 1 : edge, :])
        delta = jnp.where(first, before, pltpu.roll(normed, 1, 0)) - normed
        normed_ref[:, c] = normed
        delta_ref[:, c] = delta
        modifiers = nn(blocks, wwt_ref[:, c])
        total = jnp.zeros_like(normed)
        by_coef = jnp.zeros_like(normed)
        d_mods = []
        for j, (d, w_ref) in enumerate(sources):
            d_mixed = nt(d, w_ref[c, :])
            coef = rows_ref[MIX + 1 + j : MIX + 2 + j, c] + modifiers[j * length : (j + 1) * length, :]
            if j == 0:
                decay_down_ref[:, c] += tn(d_decay, normed + delta * coef)
            d_mod = delta * d_mixed
            row_sums_ref[8 * (MIX + 1 + j) : 8 * (MIX + 2 + j), c] += fold(d_mod)
            d_mods.append(d_mod.astype(BF16))
            total = total + d_mixed
            by_coef = by_coef + d_mixed * coef
        d_mods = jnp.concatenate(d_mods, 0)
        up_ref[:, c] += tn(blocks, d_mods)
        d_mid = d_mid + nn(d_mods, ww_ref[c, :])
        sum_ref[:, c] = total
        coef_ref[:, c] = by_coef
    lane = iota(middle.shape, 1) // rank
    d_low = jnp.zeros_like(middle)
    for j in range(5):
        d_low = jnp.where(lane == j, d_mid[j * length : (j + 1) * length, :], d_low)
    d_low = (d_low * (1.0 - middle * middle)).astype(BF16)
    sum_g = jnp.zeros((length, CHUNK), F32)
    sum_gn = jnp.zeros((length, CHUNK), F32)
    for at in range(0, width, CHUNK):
        c = slice(at, at + CHUNK)
        normed, delta = normed_ref[:, c], delta_ref[:, c]
        mix = rows_ref[MIX : MIX + 1, c]
        d_in = nt(d_low, wn_ref[c, :])
        down_ref[:, c] += tn(d_low, normed + delta * mix)
        row_sums_ref[8 * MIX : 8 * MIX + 8, c] += fold(delta * d_in)
        d_delta = coef_ref[:, c] + d_in * mix
        above = jnp.where(last, carry_ref[0:1, c], pltpu.roll(d_delta, length - 1, 0))
        carry_ref[0:1, c] = d_delta[0:1, :]
        d_normed = sum_ref[:, c] + d_in - d_delta + above
        unit = (x_ref[:, c].astype(F32) - mean) * scale
        row_sums_ref[8 * GAIN : 8 * GAIN + 8, c] += fold(d_normed * unit)
        row_sums_ref[8 * BIAS : 8 * BIAS + 8, c] += fold(d_normed)
        g = d_normed * rows_ref[GAIN : GAIN + 1, c]
        sum_g = sum_g + g
        sum_gn = sum_gn + g * unit
        sum_ref[:, c] = g
    mean_g = jnp.sum(sum_g, 1, keepdims=True) / width
    mean_gn = jnp.sum(sum_gn, 1, keepdims=True) / width
    for at in range(0, width, CHUNK):
        c = slice(at, at + CHUNK)
        unit = (x_ref[:, c].astype(F32) - mean) * scale
        dx_ref[:, c] = (scale * (sum_ref[:, c] - mean_g - unit * mean_gn)).astype(BF16)


def whole(a):
    return pl.BlockSpec(a.shape, lambda t: (0,) * a.ndim)


def params(**more):
    return pltpu.CompilerParams(
        dimension_semantics=("arbitrary",), vmem_limit_bytes=VMEM, **more
    )


def call_forward(rank, length, x, rows, own, wn, wwt, fn, fwt, wr, wk, wv, wg, ones, start):
    tokens, width = x.shape
    cw = own.shape[1]
    count = tokens // length
    tile = lambda n: pl.BlockSpec((length, n), lambda t: (t, 0))
    shape = lambda n, dtype: jax.ShapeDtypeStruct((tokens, n), dtype)
    fixed = (rows, own, wn, wwt, fn, fwt, wr, wk, wv, wg, ones, start)
    return pl.pallas_call(
        lambda *refs: mix_forward(rank, *refs),
        grid=(count,),
        in_specs=[tile(width)] + [whole(a) for a in fixed],
        out_specs=[tile(width)] * 4 + [tile(cw)] * 7 + [tile(wn.shape[1]), tile(fn.shape[1])]
        + [pl.BlockSpec((1, cw, cw), lambda t: (t, 0, 0))],
        out_shape=[shape(width, BF16)] * 4 + [shape(cw, BF16)] * 3 + [shape(cw, F32)] * 3 + [shape(cw, BF16)]
        + [shape(wn.shape[1], F32), shape(fn.shape[1], F32), jax.ShapeDtypeStruct((count, cw, cw), F32)],
        scratch_shapes=[
            pltpu.VMEM((length, width), F32), pltpu.VMEM((length, width), F32), pltpu.VMEM((8, width), F32),
            pltpu.VMEM((cw, cw), F32),
        ],
        compiler_params=params(),
        cost_estimate=pl.CostEstimate(
            flops=2 * tokens * width * (4 * cw + 5 * 256 + 384), bytes_accessed=tokens * width * 10 + width * cw * 8,
            transcendentals=0,
        ),
        name="mix_forward",
    )(x, *fixed)


def call_wkv_backward(length, d, r, k, v, w, graw, wkv, own, ones, sums, start, ends, adj):
    tokens, cw = d.shape
    count = tokens // length
    tile = pl.BlockSpec((length, cw), lambda t: (count - 1 - t, 0))
    shape = lambda dtype: jax.ShapeDtypeStruct((tokens, cw), dtype)
    return pl.pallas_call(
        lambda *refs: wkv_backward(count, *refs),
        grid=(count,),
        in_specs=[tile] * 7 + [whole(a) for a in (own, ones, sums, start)]
        + [
            pl.BlockSpec((1, cw, cw), lambda t: (jnp.maximum(count - 2 - t, 0), 0, 0)),
            pl.BlockSpec((1, cw, cw), lambda t: (count - 1 - t, 0, 0)),
        ],
        out_specs=[tile] * 5 + [pl.BlockSpec((32, cw), lambda t: (0, 0))],
        out_shape=[shape(BF16)] * 4 + [shape(F32), jax.ShapeDtypeStruct((32, cw), F32)],
        scratch_shapes=[pltpu.VMEM((cw, cw), F32)],
        compiler_params=params(),
        cost_estimate=pl.CostEstimate(
            flops=2 * tokens * cw * 128 * 50, bytes_accessed=tokens * cw * 40, transcendentals=0
        ),
        name="wkv_backward",
    )(d, r, k, v, w, graw, wkv, own, ones, sums, start, ends, adj)


def call_mix_backward(rank, length, x, rows, lm, dm, dr, dk, dv, dg, dpre, wn, ww, wwt, fn, fwt, wr, wk, wv, wg):
    tokens, width = x.shape
    cw = dr.shape[1]
    count = tokens // length
    edge = 16
    tile = lambda n: pl.BlockSpec((length, n), lambda t: (count - 1 - t, 0))
    before = pl.BlockSpec((edge, width), lambda t: (jnp.maximum((count - 1 - t) * (length // edge) - 1, 0), 0))
    fixed = (wn, ww, wwt, fn, fwt, wr, wk, wv, wg)
    sums = [(8 * 8, width), (wn.shape[1], width), (wn.shape[1], width), (fn.shape[1], width), (fn.shape[1], cw)]
    return pl.pallas_call(
        lambda *refs: mix_backward(rank, count, *refs),
        grid=(count,),
        in_specs=[tile(width), before, whole(rows), tile(lm.shape[1]), tile(dm.shape[1])] + [tile(cw)] * 5
        + [whole(a) for a in fixed],
        out_specs=[tile(width)] + [pl.BlockSpec(s, lambda t: (0, 0)) for s in sums],
        out_shape=[jax.ShapeDtypeStruct((tokens, width), BF16)] + [jax.ShapeDtypeStruct(s, F32) for s in sums],
        scratch_shapes=[pltpu.VMEM((length, width), F32)] * 4 + [pltpu.VMEM((8, width), F32)],
        compiler_params=params(),
        cost_estimate=pl.CostEstimate(
            flops=2 * tokens * width * (4 * cw + 15 * 256 + 768), bytes_accessed=tokens * width * 6 + width * cw * 8,
            transcendentals=0,
        ),
        name="mix_backward",
    )(x, x, rows, lm, dm, dr, dk, dv, dg, dpre, *fixed)


def gather_group(block):
    return lax.all_gather(block, TP, axis=0, tiled=True)


def reduce_group(parts):
    seqs, chans = lax.axis_size("seq"), lax.axis_size("chan")
    parts = parts.reshape((seqs, chans) + parts.shape[1:])
    me, at = lax.axis_index("seq"), lax.axis_index("chan")
    if seqs == 2:
        other = lax.ppermute(lax.dynamic_index_in_dim(parts, 1 - me, 0, False), "seq", [(0, 1), (1, 0)])
        mine = lax.dynamic_index_in_dim(parts, me, 0, False).astype(F32) + other.astype(F32)
    else:
        mine = lax.psum_scatter(parts, "seq", scatter_dimension=0, tiled=True)[0].astype(F32)
    sent = mine.astype(BF16)
    total = lax.dynamic_index_in_dim(mine, at, 0, False)
    for k in range(1, chans):
        block = lax.dynamic_index_in_dim(sent, (at + k) % chans, 0, False)
        total = total + lax.ppermute(block, "chan", [(i, (i + k) % chans) for i in range(chans)]).astype(F32)
    return total


def next_row(row, by):
    count = lax.axis_size(TP)
    return lax.ppermute(row, TP, [(i, i + by) for i in range(count) if 0 <= i + by < count])


def shift_down(values, first_row):
    return jnp.concatenate([first_row, values[:-1]], 0)


def unit_rows(values):
    center = values - jnp.mean(values, -1, keepdims=True)
    scale = lax.rsqrt(jnp.mean(center * center, -1, keepdims=True) + LAYER_EPSILON)
    return center * scale, scale


def on_device(
    sequence_elements,
    segment_predecessor_entries,
    opening_recurrences,
    first_layernorm_gain,
    first_layernorm_shift_term,
    lag_blend_coefficients,
    lag_narrowing_factor,
    lag_widening_factors,
    fading_exponent_baseline,
    fading_narrowing_factor,
    fading_widening_factor,
    present_reward,
    acceptor_projection,
    address_projection,
    content_projection,
    valve_projection,
    timemix_result_projection,
    subspace_cluster_gain,
    subspace_cluster_shift_term,
    second_layernorm_gain,
    second_layernorm_shift_term,
    feedforward_lag_blends,
    feedforward_address_projection,
    feedforward_acceptor_projection,
    feedforward_content_projection,
    result_adjoint,
    final_recurrence_adjoint,
):
    segs, seqs, chans = lax.axis_size("seg"), lax.axis_size("seq"), lax.axis_size("chan")
    group = seqs * chans
    p = lax.axis_index(TP)
    x = sequence_elements[0]
    length, width = x.shape
    tokens = group * length
    cw = width // group
    heads = cw // HEAD
    rank = lag_widening_factors.shape[1] // 5
    ranks, decays = 5 * rank, fading_widening_factor.shape[1]
    wide_rank, wide_decay = -(-ranks // 128) * 128, -(-decays // 128) * 128

    def columns(a, axis=-1):
        return lax.dynamic_slice_in_dim(a, p * cw, cw, axis if axis >= 0 else a.ndim + axis)

    def gather_rows(a):
        return lax.all_gather(a, "seg", axis=0, tiled=True)

    x_all = gather_group(x)
    four = gather_rows(
        jnp.concatenate(
            [columns(a) for a in (acceptor_projection, address_projection, content_projection, valve_projection)], 1
        )
    )
    wr, wk, wv, wg = (four[:, i * cw : (i + 1) * cw] for i in range(4))
    share = group // segs
    out_rows = lax.dynamic_slice_in_dim(timemix_result_projection, (p % share) * cw, cw, 0)
    w_out = lax.ppermute(
        out_rows, ALL,
        [(s * group + j, (j // share) * group + s * share + j % share) for s in range(segs) for j in range(group)],
    )
    hidden_units = feedforward_address_projection.shape[1] // seqs
    me = lax.axis_index("seq")

    def hidden_part(a):
        return lax.dynamic_slice_in_dim(a, me * hidden_units, hidden_units, 1)

    fr_columns = width // seqs
    w_recept = lax.all_gather(
        gather_rows(lax.dynamic_slice_in_dim(feedforward_acceptor_projection, me * fr_columns, fr_columns, 1)),
        "seq", axis=1, tiled=True,
    )
    w_key = gather_rows(hidden_part(feedforward_address_projection))
    w_value = gather_rows(hidden_part(feedforward_content_projection))

    zeros_row = jnp.zeros((7, width), F32)
    rows = jnp.concatenate(
        [
            first_layernorm_gain[None], first_layernorm_shift_term[None], lag_blend_coefficients.T,
            segment_predecessor_entries[0, 0][None], zeros_row,
        ]
    )
    own = jnp.stack(
        [columns(a) for a in (fading_exponent_baseline, present_reward, subspace_cluster_gain, subspace_cluster_shift_term)]
        + [jnp.zeros((cw,), F32)] * 4
    )
    wn = jnp.pad(lag_narrowing_factor, ((0, 0), (0, wide_rank - ranks)))
    ww = jnp.pad(lag_widening_factors, ((0, 0), (0, wide_rank - ranks)))
    wwt = ww.T
    fn = jnp.pad(fading_narrowing_factor, ((0, 0), (0, wide_decay - decays)))
    fwt = columns(jnp.pad(fading_widening_factor, ((0, 0), (0, wide_decay - decays))).T)
    same_head = (iota((cw, cw), 0) // HEAD) == (iota((cw, cw), 1) // HEAD)

    def spread(states):
        flat = jnp.swapaxes(states, -1, -2)
        return jnp.where(same_head, jnp.concatenate([flat] * heads, -1), 0.0)

    start = spread(columns(opening_recurrences[0]))
    adjoints = lax.all_to_all(
        final_recurrence_adjoint[0, 0].reshape(HEAD, group, cw).transpose(1, 0, 2), TP, 0, 0, tiled=True
    )
    adjoints = spread(adjoints)

    (xk, xv, xr, xg, r, k, v, w, graw, wkv, gated, lm, dm, ends) = call_forward(
        rank, length, x_all, rows, own, wn, wwt, fn, fwt, wr, wk, wv, wg, same_head.astype(BF16), start
    )
    mixed_out = nn(gated, w_out).astype(BF16).reshape(group, length, width)
    residual = x.astype(F32) + reduce_group(mixed_out)

    cot = result_adjoint[0].astype(F32)
    ffn_unit, ffn_scale = unit_rows(residual)
    ffn_normed = ffn_unit * second_layernorm_gain + second_layernorm_shift_term
    first_row = segment_predecessor_entries[0, 1][None]
    previous = jnp.where(p == 0, first_row, next_row(ffn_normed[-1:], 1))
    ffn_delta = shift_down(ffn_normed, previous) - ffn_normed
    mix_key, mix_recept = feedforward_lag_blends[:, 0], feedforward_lag_blends[:, 1]
    recept_in = (ffn_normed + ffn_delta * mix_recept).astype(BF16)
    ffn_gate = jax.nn.sigmoid(nn(recept_in, w_recept))
    d_values = (cot * ffn_gate).astype(BF16)

    normed_all = gather_group(ffn_normed.astype(BF16))
    d_values_all = gather_group(d_values)
    normed_f32 = normed_all.astype(F32)
    delta_all = shift_down(normed_f32, first_row) - normed_f32
    key_in_all = (normed_f32 + delta_all * mix_key).astype(BF16)
    recept_in_all = (normed_f32 + delta_all * mix_recept).astype(BF16)
    hidden = jax.nn.relu(nn(key_in_all, w_key))
    squared = jnp.square(hidden).astype(BF16)
    ffn_values = reduce_group(nt(squared, w_value).astype(BF16).reshape(group, length, width))
    d_hidden = (nn(d_values_all, w_value) * 2.0 * hidden).astype(BF16)
    d_fk = reduce_group(nt(d_hidden, w_key).astype(BF16).reshape(group, length, width))

    def reduce_rows(a):
        return lax.psum_scatter(a.astype(BF16), "seg", scatter_dimension=0, tiled=True)

    def join_hidden(a):
        return lax.all_to_all(a, "seq", 0, 1, tiled=True).astype(F32)

    grad_ffn_value = join_hidden(reduce_rows(tn(d_values_all, squared)))
    grad_ffn_key = join_hidden(reduce_rows(tn(key_in_all, d_hidden)))

    output = residual + ffn_gate * ffn_values
    d_ffn_gate = (cot * ffn_values * ffn_gate * (1.0 - ffn_gate)).astype(BF16)
    d_fr = nt(d_ffn_gate, w_recept)
    d_fdelta = d_fk * mix_key + d_fr * mix_recept
    d_ffn_normed = d_fk + d_fr - d_fdelta + jnp.concatenate([d_fdelta[1:], next_row(d_fdelta[:1], -1)], 0)
    g = d_ffn_normed * second_layernorm_gain
    d_residual = cot + ffn_scale * (
        g - jnp.mean(g, -1, keepdims=True) - ffn_unit * jnp.mean(g * ffn_unit, -1, keepdims=True)
    )
    ffn_sums = jnp.stack(
        [
            jnp.sum(d_ffn_normed * ffn_unit, 0), jnp.sum(d_ffn_normed, 0),
            jnp.sum(ffn_delta * d_fk, 0), jnp.sum(ffn_delta * d_fr, 0),
        ]
    )
    d_att = gather_group(d_residual.astype(BF16))
    d_gate_own = lax.all_to_all(d_ffn_gate.reshape(length, group, cw).transpose(1, 0, 2), TP, 0, 0, tiled=True)
    grad_recept_part = tn(recept_in_all, d_gate_own.reshape(tokens, cw))

    d_gated = nt(d_att, w_out)
    dr, dk, dv, dg, d_pre, own_sums = call_wkv_backward(
        length, d_gated, r, k, v, w, graw, wkv, own, same_head.astype(BF16), sum_table(length), start, ends, adjoints
    )
    grad_four = jnp.concatenate([tn(xr, dr), tn(xk, dk), tn(xv, dv), tn(xg, dg), grad_recept_part], 1)
    dx, row_sums, up, down, decay_down, decay_up = call_mix_backward(
        rank, length, x_all, rows, lm, dm, dr, dk, dv, dg, d_pre, wn, ww, wwt, fn, fwt, wr, wk, wv, wg
    )
    input_grad = d_residual + reduce_group(dx.reshape(group, length, width))

    five = reduce_rows(grad_four).reshape(group, width // (segs * group), 5 * cw)
    five = lax.all_to_all(five, TP, 0, 0, tiled=True).astype(F32)
    block = width // (segs * group)
    five = five.reshape(group, block, 5, cw).transpose(2, 1, 0, 3).reshape(5, block, width)
    grad_out = lax.psum_scatter(tn(gated, d_att).astype(BF16), "seg", scatter_dimension=0, tiled=True)
    grad_out = lax.ppermute(
        grad_out, ALL, [(i * group + j, segs * j + i) for i in range(segs) for j in range(group)]
    ).astype(F32)

    own_rows = jnp.concatenate([jnp.sum(own_sums.reshape(4, 8, cw), 1), decay_up[:decays]], 0)
    own_rows = lax.dynamic_update_slice_in_dim(jnp.zeros((4 + decays, width), F32), own_rows, p * cw, 1)
    small = jnp.concatenate(
        [jnp.sum(row_sums.reshape(8, 8, width), 1), ffn_sums, own_rows, down[:ranks], up[:ranks], decay_down[:decays]], 0
    )
    count = small.shape[0]
    small = small.astype(BF16).reshape(count, segs, group, block).transpose(2, 1, 0, 3).reshape(group, segs * count, block)
    small = reduce_group(small).astype(BF16).reshape(segs, count, block)
    small = jnp.sum(lax.all_to_all(small, "seg", 0, 0, tiled=True).astype(F32), 0)
    norm_gain, norm_bias, shift_mix = small[0], small[1], small[2:8].T
    ffn_gain, ffn_bias, ffn_shift_mix = small[8], small[9], small[10:12].T
    decay_base, reward, group_gain, group_bias = small[12], small[13], small[14], small[15]
    at = 16
    d_up, at = small[at : at + decays].T, at + decays
    shift_down_grad, at = small[at : at + ranks].T, at + ranks
    shift_up_grad, at = small[at : at + ranks].T, at + ranks
    d_down = small[at : at + decays].T

    end_states = jnp.swapaxes(jnp.sum(ends.reshape(group, cw, heads, HEAD), 2), 1, 2)
    end_states = lax.all_to_all(end_states, TP, 0, 0, tiled=True).transpose(1, 0, 2).reshape(HEAD, width)
    return (
        output.astype(BF16)[None],
        end_states[None, None],
        input_grad[None],
        norm_gain,
        norm_bias,
        shift_mix,
        shift_down_grad,
        shift_up_grad,
        decay_base,
        d_down,
        d_up,
        reward,
        five[0],
        five[1],
        five[2],
        five[3],
        grad_out,
        group_gain,
        group_bias,
        ffn_gain,
        ffn_bias,
        ffn_shift_mix,
        grad_ffn_key,
        five[4],
        grad_ffn_value,
    )


def solution(mesh):
    rows, tokens = P("seg", None), P("seg", TP, None)
    matrix = P("seg", "chan")
    vector_out, matrix_out = P(ALL), P(ALL, None)
    ffn_out = P(("seg", "seq"), "chan")
    return jax.shard_map(
        on_device,
        mesh=mesh,
        in_specs=(tokens, P("seg", None, None), P("seg", None, None)) + (P(),) * 9 + (rows,) * 5 + (P(),) * 5
        + (matrix, rows, matrix, tokens, P("seg", TP, None, None)),
        out_specs=(tokens, P("seg", TP, None, None), tokens) + (vector_out,) * 2 + (matrix_out,) * 3 + (vector_out,)
        + (matrix_out,) * 2 + (vector_out,) + (matrix_out,) * 5 + (vector_out,) * 4
        + (matrix_out, ffn_out, matrix_out, ffn_out),
        check_vma=False,
    )
```

```python
import jax
import jax.numpy as jnp
import numpy as np
from jax import lax
from jax.experimental import pallas as pl
from jax.experimental.pallas import tpu as pltpu
from jax.sharding import PartitionSpec as P

HEAD = 64
TP = ("seq", "chan")
ALL = ("seg", "seq", "chan")
LAYER_EPSILON = 1e-05
GROUP_EPSILON = 0.00064
F32 = jnp.float32
BF16 = jnp.bfloat16
CHUNK = 256
VMEM = 56 * 2**20


def dot(a, b, dims):
    return lax.dot_general(
        a.astype(BF16), b.astype(BF16), (dims, ((), ())), preferred_element_type=F32
    )


def nn(a, b):
    return dot(a, b, ((1,), (0,)))


def nt(a, b):
    return dot(a, b, ((1,), (1,)))


def tn(a, b):
    return dot(a, b, ((0,), (0,)))


def iota(shape, axis):
    return lax.broadcasted_iota(jnp.int32, shape, axis)


def head_sum(values, ones):
    high = values.astype(BF16)
    low = (values - high.astype(F32)).astype(BF16)
    return nn(high, ones) + nn(low, ones)


def pyramid(w):
    length = w.shape[0]
    row = iota(w.shape, 0)
    before, after, total = jnp.zeros_like(w), jnp.zeros_like(w), w
    levels = []
    half = 1
    while half < length:
        upper = (row & half) != 0
        levels.append((half, upper, jnp.where(upper, before, after)))
        sibling = jnp.where(upper, pltpu.roll(total, half, 0), pltpu.roll(total, length - half, 0))
        before = jnp.where(upper, before + sibling, before)
        after = jnp.where(upper, after, after + sibling)
        total = total + sibling
        half *= 2
    return levels, before, after, total


def split_heads(values, heads):
    if heads == 1:
        return [values.astype(BF16)]
    lane = iota(values.shape, 1) // HEAD
    return [jnp.where(lane == head, values, 0.0).astype(BF16) for head in range(heads)]


def row_stats(x_ref):
    rows, width = x_ref.shape
    step = 128
    total = jnp.zeros((rows, step), F32)
    for at in range(0, width, step):
        total = total + x_ref[:, at : at + step].astype(F32)
    mean = jnp.sum(total, 1, keepdims=True) / width
    total = jnp.zeros((rows, step), F32)
    for at in range(0, width, step):
        center = x_ref[:, at : at + step].astype(F32) - mean
        total = total + center * center
    return mean, lax.rsqrt(jnp.sum(total, 1, keepdims=True) / width + LAYER_EPSILON)


def fold(values):
    rows, width = values.shape
    return jnp.sum(values.reshape(rows // 8, 8, width), 0)


def rank_blocks(values, rank):
    lane = iota(values.shape, 1) // rank
    return jnp.concatenate([jnp.where(lane == j, values, 0.0).astype(BF16) for j in range(5)], 0)


def spread(states, same):
    flat = states.T
    return jnp.concatenate([flat] * (flat.shape[0] // HEAD), 1) * same


def compact(state):
    return sum(state[:, at : at + HEAD] for at in range(0, state.shape[1], HEAD)).T


def part_copies(place_ref, parts, full_ref, sem):
    rows = parts[0].shape[0]
    copies = []
    for m, part in enumerate(parts):
        at = pl.multiple_of((place_ref[0] ^ m) * rows, rows)
        copies.append(pltpu.make_async_copy(part, full_ref.at[pl.ds(at, rows), :], sem.at[m]))
    return copies


def load_parts(place_ref, parts, full_ref, sem):
    for copy in part_copies(place_ref, parts, full_ref, sem):
        copy.start()


def wait_parts(place_ref, parts, full_ref, sem):
    @pl.when(pl.program_id(0) == 0)
    def _():
        for copy in part_copies(place_ref, parts, full_ref, sem):
            copy.wait()


GAIN, BIAS, MIX, FIRST = 0, 1, 2, 8


def mix_forward(
    rank, x_ref, rows_ref, own_ref, wn_ref, ww_ref, fn_ref, fw_ref,
    ones_ref, start_ref, place_ref, part0, part1, part2, part3, *refs,
):
    (
        gated_ref, xk_ref, xv_ref, xr_ref, xg_ref, r_ref, k_ref, v_ref, w_ref, graw_ref, wkv_ref, lm_ref, dm_ref,
        ends_ref, normed_ref, delta_ref, carry_ref, state_ref, four_ref, sem,
    ) = refs[-20:]
    step = pl.program_id(0)
    length, width = x_ref.shape
    own = own_ref.shape[1]
    heads = own // HEAD

    @pl.when(step == 0)
    def _():
        carry_ref[...] = jnp.broadcast_to(rows_ref[FIRST : FIRST + 1, :], carry_ref.shape)
        state_ref[...] = spread(start_ref[...], ones_ref[...].astype(F32))
        load_parts(place_ref, (part0, part1, part2, part3), four_ref, sem)

    mean, scale = row_stats(x_ref)
    first = iota((length, CHUNK), 0) == 0
    narrow = jnp.zeros((length, wn_ref.shape[0]), F32)
    for at in range(0, width, CHUNK):
        c = slice(at, at + CHUNK)
        normed = (x_ref[:, c].astype(F32) - mean) * scale * rows_ref[GAIN : GAIN + 1, c] + rows_ref[BIAS : BIAS + 1, c]
        delta = jnp.where(first, carry_ref[0:1, c], pltpu.roll(normed, 1, 0)) - normed
        carry_ref[0:1, c] = normed[length - 1 : length, :]
        normed_ref[:, c] = normed
        delta_ref[:, c] = delta
        narrow = narrow + nt(normed + delta * rows_ref[MIX : MIX + 1, c], wn_ref[:, c])
    middle = jnp.tanh(narrow)
    lm_ref[...] = middle
    blocks = rank_blocks(middle, rank)
    decay_in = jnp.zeros((length, fn_ref.shape[0]), F32)
    for at in range(0, width, CHUNK):
        c = slice(at, at + CHUNK)
        normed, delta = normed_ref[:, c], delta_ref[:, c]
        modifiers = nn(blocks, ww_ref[:, c])
        for j, ref in enumerate((None, xk_ref, xv_ref, xr_ref, xg_ref)):
            modifier = modifiers[j * length : (j + 1) * length, :]
            mixed = (normed + delta * (rows_ref[MIX + 1 + j : MIX + 2 + j, c] + modifier)).astype(BF16)
            if ref is None:
                decay_in = decay_in + nt(mixed, fn_ref[:, c])
            else:
                ref[:, c] = mixed
    decay_mid = jnp.tanh(decay_in)
    dm_ref[...] = decay_mid
    w = -jnp.exp(own_ref[0:1, :] + nn(decay_mid, fw_ref[...]))
    w_ref[...] = w
    wait_parts(place_ref, (part0, part1, part2, part3), four_ref, sem)
    r = nn(xr_ref[...], four_ref[:, :own]).astype(BF16)
    k = nn(xk_ref[...], four_ref[:, own : 2 * own]).astype(BF16)
    v = nn(xv_ref[...], four_ref[:, 2 * own : 3 * own]).astype(BF16)
    graw = nn(xg_ref[...], four_ref[:, 3 * own :])
    r_ref[...], k_ref[...], v_ref[...], graw_ref[...] = r, k, v, graw

    rf, kf, vf = r.astype(F32), k.astype(F32), v.astype(F32)
    levels, before, after, total = pyramid(w)
    row, col = iota((length, length), 0), iota((length, length), 1)
    apart = jnp.where(row > col, row ^ col, 0)
    scores = [jnp.zeros((length, length), F32)] * heads
    for half, upper, exponent in levels:
        scaled = jnp.where(upper, rf, kf) * jnp.exp(exponent)
        flat = scaled.astype(BF16)
        here = (apart >= half) & (apart < 2 * half)
        for head, one in enumerate(split_heads(scaled, heads)):
            scores[head] = jnp.where(here, nt(one, flat), scores[head])
    ones = ones_ref[...]
    wkv = nn(jnp.concatenate([s.astype(BF16) for s in scores], 1), jnp.concatenate(split_heads(vf, heads), 0))
    state = state_ref[...]
    wkv = wkv + nt(rf * jnp.exp(before), state) + head_sum(rf * own_ref[1:2, :] * kf, ones) * vf
    wkv_ref[...] = wkv
    state = state * jnp.exp(total[0:1, :]) + tn(v, kf * jnp.exp(after)) * ones.astype(F32)
    state_ref[...] = state
    ends_ref[0] = compact(state)

    center = wkv - head_sum(wkv, ones) / HEAD
    variance = head_sum(center * center, ones) / HEAD
    grouped = center * lax.rsqrt(variance + GROUP_EPSILON) * own_ref[2:3, :] + own_ref[3:4, :]
    gated_ref[...] = (grouped * graw * jax.nn.sigmoid(graw)).astype(BF16)


def wkv_backward(
    d_ref, r_ref, k_ref, v_ref, w_ref, graw_ref, wkv_ref, dm_ref, w_out_ref, own_ref, ones_ref, sums_ref, start_ref,
    ends_ref, adj_ref, *refs,
):
    own_sums_ref, decay_up_ref, dr_ref, dk_ref, dv_ref, dg_ref, dpre_ref, state_ref = refs[-8:]
    step = pl.program_id(0)
    length, own = r_ref.shape
    heads = own // HEAD
    ones = ones_ref[...]

    @pl.when(step == 0)
    def _():
        for ref in (state_ref, own_sums_ref, decay_up_ref):
            ref[...] = jnp.zeros_like(ref)

    reward, gain, bias = own_ref[1:2, :], own_ref[2:3, :], own_ref[3:4, :]
    wkv, graw, d_gated = wkv_ref[...], graw_ref[...], nt(d_ref[...], w_out_ref[...])
    center = wkv - head_sum(wkv, ones) / HEAD
    scale = lax.rsqrt(head_sum(center * center, ones) / HEAD + GROUP_EPSILON)
    normed = center * scale
    sigma = jax.nn.sigmoid(graw)
    d_grouped = d_gated * graw * sigma
    dg_ref[...] = (d_gated * (normed * gain + bias) * sigma * (1.0 + graw * (1.0 - sigma))).astype(BF16)
    d_normed = d_grouped * gain
    do = scale * (d_normed - head_sum(d_normed, ones) / HEAD - normed * (head_sum(d_normed * normed, ones) / HEAD))

    rb, kb, vb, dob = r_ref[...], k_ref[...], v_ref[...], do.astype(BF16)
    r, k, v, w = rb.astype(F32), kb.astype(F32), vb.astype(F32), w_ref[...]
    levels, before, after, total = pyramid(w)
    same = ones.astype(F32)
    d_state = state_ref[...] + spread(adj_ref[0], same)
    state = spread(jnp.where(step == pl.num_programs(0) - 1, start_ref[...], ends_ref[0]), same)
    d_flat, flat = d_state.astype(BF16), state.astype(BF16)
    from_start, to_end, decay = jnp.exp(before), jnp.exp(after), jnp.exp(total[0:1, :])
    dr = from_start * nn(dob, flat)
    dk = to_end * nn(vb, d_flat)
    dv = nt(k * to_end, d_flat)
    through = [r * dr, k * dk]
    state_ref[...] = d_state * decay + tn(dob, r * from_start) * same
    whole = decay * jnp.sum(state * d_state, 0, keepdims=True)

    row, col = iota((length, length), 0), iota((length, length), 1)
    apart = row ^ col
    do_heads, v_heads = split_heads(do, heads), split_heads(v, heads)
    d_scores = [
        jnp.where(row > col, nt(do_heads[h], vb), jnp.where(row < col, nt(v_heads[h], dob), 0.0)).astype(BF16)
        for h in range(heads)
    ]
    scores = [jnp.zeros((length, length), F32)] * heads
    for half, upper, exponent in levels:
        factor = jnp.exp(exponent)
        scaled = jnp.where(upper, r, k) * factor
        mine = split_heads(scaled, heads)
        here = (apart >= half) & (apart < 2 * half)
        late = here & (row < col)
        for h in range(heads):
            scores[h] = jnp.where(late, nt(mine[h], scaled), scores[h])
        pulled = nn(
            jnp.concatenate([jnp.where(here, d, 0.0).astype(BF16) for d in d_scores], 1), jnp.concatenate(mine, 0)
        )
        if half > 1:
            through.append(scaled * pulled)
        pulled = pulled * factor
        dr = dr + jnp.where(upper, pulled, 0.0)
        dk = dk + jnp.where(upper, 0.0, pulled)
    dv = dv + nn(jnp.concatenate([s.astype(BF16) for s in scores], 1), jnp.concatenate(do_heads, 0))
    met = head_sum(v * do, ones)
    dr = dr + reward * k * met
    dk = dk + reward * r * met
    dv = dv + head_sum(r * reward * k, ones) * do
    d_log = whole + nn(sums_ref[...], jnp.concatenate([q.astype(BF16) for q in through], 0))
    d_pre = d_log * w
    dr_ref[...], dk_ref[...], dv_ref[...] = dr.astype(BF16), dk.astype(BF16), dv.astype(BF16)
    dpre_ref[...] = d_pre
    decay_up_ref[...] += tn(dm_ref[...], d_pre)
    for i, part in enumerate((d_pre, r * k * met, d_grouped * normed, d_grouped)):
        own_sums_ref[8 * i : 8 * i + 8, :] += fold(part)


def sum_table(length):
    row, col = np.arange(length)[:, None], np.arange(length)[None, :]
    tables = [col > row, col < row]
    half = 2
    while half < length:
        inside = (row // half) == (col // half)
        upper = (row // half) % 2 == 1
        tables.append(inside & np.where(upper, col > row, col < row))
        half *= 2
    return jnp.asarray(np.concatenate(tables, 1), BF16)


def mix_backward(rank, halves, *refs):
    (
        place_ref, x_ref, edge_ref, rows_ref, lm_ref, dm_ref, dr_ref, dk_ref, dv_ref, dg_ref, dpre_ref,
        wn_ref, ww_ref, fn_ref, fw_ref, more_ref, part0, part1, part2, part3,
    ) = refs[:20]
    packed_ref = refs[-13 - halves]
    outs = refs[-12 - halves : -12]
    (
        row_sums_ref, up_ref, down_ref, decay_down_ref, dx_ref, carry_ref, sum_ref, coef_ref, normed_ref, delta_ref,
        four_ref, sem,
    ) = refs[-12:]
    step = pl.program_id(0)
    from_first = pl.num_programs(0) - 1 - step
    length, width = x_ref.shape

    @pl.when(step == 0)
    def _():
        load_parts(place_ref, (part0, part1, part2, part3), four_ref, sem)
        for ref in (carry_ref, row_sums_ref, up_ref, down_ref, decay_down_ref):
            ref[...] = jnp.zeros_like(ref)

    own = dr_ref.shape[1]
    mean, scale = row_stats(x_ref)
    edge = edge_ref.shape[0]
    edge_mean, edge_scale = row_stats(edge_ref)
    middle, decay_mid = lm_ref[...], dm_ref[...]
    blocks = rank_blocks(middle, rank)
    d_pre = dpre_ref[...]
    d_decay = (nt(d_pre, fw_ref[...]) * (1.0 - decay_mid * decay_mid)).astype(BF16)
    sources = ((d_decay, None), (dk_ref[...], own), (dv_ref[...], 2 * own), (dr_ref[...], 0), (dg_ref[...], 3 * own))
    first = iota((length, CHUNK), 0) == 0
    last = iota((length, CHUNK), 0) == length - 1
    d_mid = jnp.zeros((5 * length, wn_ref.shape[0]), F32)
    wait_parts(place_ref, (part0, part1, part2, part3), four_ref, sem)
    for at in range(0, width, CHUNK):
        c = slice(at, at + CHUNK)
        gain, bias = rows_ref[GAIN : GAIN + 1, c], rows_ref[BIAS : BIAS + 1, c]
        normed = (x_ref[:, c].astype(F32) - mean) * scale * gain + bias
        edge_normed = (edge_ref[:, c].astype(F32) - edge_mean) * edge_scale * gain + bias
        before = jnp.where(from_first == 0, rows_ref[FIRST : FIRST + 1, c], edge_normed[edge - 1 : edge, :])
        delta = jnp.where(first, before, pltpu.roll(normed, 1, 0)) - normed
        normed_ref[:, c] = normed
        delta_ref[:, c] = delta
        modifiers = nn(blocks, ww_ref[:, c])
        total = jnp.zeros_like(normed)
        by_coef = jnp.zeros_like(normed)
        d_mods = []
        for j, (d, begin) in enumerate(sources):
            d_mixed = nt(d, four_ref[c, begin : begin + own]) if j else nn(d, fn_ref[:, c])
            coef = rows_ref[MIX + 1 + j : MIX + 2 + j, c] + modifiers[j * length : (j + 1) * length, :]
            if j == 0:
                decay_down_ref[:, c] += tn(d_decay, normed + delta * coef)
            d_mod = delta * d_mixed
            row_sums_ref[8 * (MIX + 1 + j) : 8 * (MIX + 2 + j), c] += fold(d_mod)
            d_mods.append(d_mod.astype(BF16))
            total = total + d_mixed
            by_coef = by_coef + d_mixed * coef
        d_mods = jnp.concatenate(d_mods, 0)
        up_ref[:, c] += tn(blocks, d_mods)
        d_mid = d_mid + nt(d_mods, ww_ref[:, c])
        sum_ref[:, c] = total
        coef_ref[:, c] = by_coef
    lane = iota(middle.shape, 1) // rank
    d_low = jnp.zeros_like(middle)
    for j in range(5):
        d_low = jnp.where(lane == j, d_mid[j * length : (j + 1) * length, :], d_low)
    d_low = (d_low * (1.0 - middle * middle)).astype(BF16)
    sum_g = jnp.zeros((length, CHUNK), F32)
    sum_gn = jnp.zeros((length, CHUNK), F32)
    for at in range(0, width, CHUNK):
        c = slice(at, at + CHUNK)
        normed, delta = normed_ref[:, c], delta_ref[:, c]
        mix = rows_ref[MIX : MIX + 1, c]
        d_in = nn(d_low, wn_ref[:, c])
        down_ref[:, c] += tn(d_low, normed + delta * mix)
        row_sums_ref[8 * MIX : 8 * MIX + 8, c] += fold(delta * d_in)
        d_delta = coef_ref[:, c] + d_in * mix
        above = jnp.where(last, carry_ref[0:1, c], pltpu.roll(d_delta, length - 1, 0))
        carry_ref[0:1, c] = d_delta[0:1, :]
        d_normed = sum_ref[:, c] + d_in - d_delta + above
        unit = (x_ref[:, c].astype(F32) - mean) * scale
        row_sums_ref[8 * GAIN : 8 * GAIN + 8, c] += fold(d_normed * unit)
        row_sums_ref[8 * BIAS : 8 * BIAS + 8, c] += fold(d_normed)
        g = d_normed * rows_ref[GAIN : GAIN + 1, c]
        sum_g = sum_g + g
        sum_gn = sum_gn + g * unit
        sum_ref[:, c] = g
    mean_g = jnp.sum(sum_g, 1, keepdims=True) / width
    mean_gn = jnp.sum(sum_gn, 1, keepdims=True) / width
    for at in range(0, width, CHUNK):
        c = slice(at, at + CHUNK)
        unit = (x_ref[:, c].astype(F32) - mean) * scale
        dx_ref[:, c] = (scale * (sum_ref[:, c] - mean_g - unit * mean_gn)).astype(BF16)
    store_half(place_ref, dx_ref, outs, from_first)

    @pl.when(step == pl.num_programs(0) - 1)
    def _():
        at = 16
        packed_ref[0:at, :] = jnp.zeros((at, width), BF16)
        for i in range(8):
            packed_ref[i : i + 1, :] = jnp.sum(row_sums_ref[8 * i : 8 * i + 8, :], 0, keepdims=True).astype(BF16)
        more = more_ref.shape[0]
        decays = packed_ref.shape[0] - at - 10 * rank - more
        for ref, size in ((down_ref, 5 * rank), (up_ref, 5 * rank), (decay_down_ref, decays), (more_ref, more)):
            packed_ref[at : at + size, :] = ref[0:size, :].astype(BF16)
            at += size


def whole(a):
    return pl.BlockSpec(a.shape, lambda t: (0,) * a.ndim)


def params(**more):
    return pltpu.CompilerParams(
        dimension_semantics=("arbitrary",), vmem_limit_bytes=VMEM, **more
    )


def light():
    return pl.CostEstimate(flops=0, bytes_accessed=0, transcendentals=0)


def pinned(pins):
    return [pl.BlockSpec(memory_space=pl.ANY)] * len(pins)


def part_specs(parts):
    return [pl.BlockSpec(memory_space=pltpu.SMEM)] + [pl.BlockSpec(memory_space=pl.ANY)] * len(parts)


def part_scratch(parts):
    rows, columns = parts[0].shape
    return [pltpu.VMEM((len(parts) * rows, columns), BF16), pltpu.SemaphoreType.DMA((len(parts),))]


def call_forward(rank, length, x, rows, own, wn, ww, fn, fw, ones, start, place, parts, pins):
    tokens, width = x.shape
    cw = own.shape[1]
    count = tokens // length
    tile = lambda n: pl.BlockSpec((length, n), lambda t: (t, 0))
    shape = lambda n, dtype: jax.ShapeDtypeStruct((tokens, n), dtype)
    fixed = (rows, own, wn, ww, fn, fw, ones, start)
    return pl.pallas_call(
        lambda *refs: mix_forward(rank, *refs),
        grid=(count,),
        in_specs=[tile(width)] + [whole(a) for a in fixed] + part_specs(parts) + pinned(pins),
        out_specs=[tile(cw)] + [tile(width)] * 4 + [tile(cw)] * 6 + [tile(wn.shape[0]), tile(fn.shape[0])]
        + [pl.BlockSpec((1, HEAD, cw), lambda t: (t, 0, 0))],
        out_shape=[shape(cw, BF16)] + [shape(width, BF16)] * 4 + [shape(cw, BF16)] * 3 + [shape(cw, F32)] * 3
        + [shape(wn.shape[0], F32), shape(fn.shape[0], F32), jax.ShapeDtypeStruct((count, HEAD, cw), F32)],
        scratch_shapes=[
            pltpu.VMEM((length, width), F32), pltpu.VMEM((length, width), F32), pltpu.VMEM((8, width), F32),
            pltpu.VMEM((cw, cw), F32),
        ]
        + part_scratch(parts),
        compiler_params=params(),
        cost_estimate=light(),
        name="mix_forward",
    )(x, *fixed, place, *parts, *pins)


def two_halves(tokens, width, length, seqs, backward=False):
    half = tokens // length // 2
    order = (lambda t: tokens // length - 1 - t) if backward else (lambda t: t)
    if seqs != 2:
        return [pl.BlockSpec((length, width), lambda t, place: (order(t), 0))], [jax.ShapeDtypeStruct((tokens, width), BF16)]
    mine = lambda t, place: (jnp.clip(order(t) - place[1] * half, 0, half - 1), 0)
    other = lambda t, place: (jnp.clip(order(t) - (1 - place[1]) * half, 0, half - 1), 0)
    return (
        [pl.BlockSpec((length, width), mine), pl.BlockSpec((length, width), other)],
        [jax.ShapeDtypeStruct((tokens // 2, width), BF16)] * 2,
    )


def store_half(place_ref, value_ref, outs, tile=None):
    if len(outs) == 1:
        outs[0][...] = value_ref[...]
        return
    tile = pl.program_id(0) if tile is None else tile
    is_mine = tile // (pl.num_programs(0) // 2) == place_ref[1]

    @pl.when(is_mine)
    def _():
        outs[0][...] = value_ref[...]

    @pl.when(jnp.logical_not(is_mine))
    def _():
        outs[1][...] = value_ref[...]


def ffn_forward(halves, place_ref, x_ref, edge_ref, rows_ref, w_all, *refs):
    key_ref, recept_ref, hidden_ref, squared_ref = refs[-7 - halves : -3 - halves]
    outs = refs[-3 - halves : -3]
    w_ref, value_ref, sem = refs[-3:]
    length, width = x_ref.shape
    units = hidden_ref.shape[1]
    edge = edge_ref.shape[0]
    load = pltpu.make_async_copy(w_all, w_ref, sem)

    @pl.when(pl.program_id(0) == 0)
    def _():
        load.start()

    first = iota((length, CHUNK), 0) == 0
    for at in range(0, width, CHUNK):
        c = slice(at, at + CHUNK)
        normed = x_ref[:, c].astype(F32)
        before = jnp.where(pl.program_id(0) == 0, rows_ref[2:3, c], edge_ref[edge - 1 : edge, c].astype(F32))
        delta = jnp.where(first, before, pltpu.roll(normed, 1, 0)) - normed
        key_ref[:, c] = (normed + delta * rows_ref[3:4, c]).astype(BF16)
        recept_ref[:, c] = (normed + delta * rows_ref[4:5, c]).astype(BF16)

    @pl.when(pl.program_id(0) == 0)
    def _():
        load.wait()

    hidden = jnp.maximum(nn(key_ref[...], w_ref[:, :units]), 0.0)
    hidden_ref[...] = hidden
    squared = (hidden * hidden).astype(BF16)
    squared_ref[...] = squared
    for at in range(0, width, 2 * CHUNK):
        c = slice(at, at + 2 * CHUNK)
        value_ref[:, c] = nt(squared, w_ref[c, units:]).astype(BF16)
    store_half(place_ref, value_ref, outs)


def call_ffn_forward(x, rows, w, place, seqs, pins):
    tokens, width = x.shape
    length, edge = 256, 16
    units = w.shape[1] // 2
    tile = lambda n: pl.BlockSpec((length, n), lambda t, place: (t, 0))
    shape = lambda n, dtype: jax.ShapeDtypeStruct((tokens, n), dtype)
    specs, shapes = two_halves(tokens, width, length, seqs)
    return pl.pallas_call(
        lambda *refs: ffn_forward(len(specs), *refs),
        grid_spec=pltpu.PrefetchScalarGridSpec(
            num_scalar_prefetch=1,
            grid=(tokens // length,),
            in_specs=[
                tile(width),
                pl.BlockSpec((edge, width), lambda t, place: (jnp.maximum(t * (length // edge) - 1, 0), 0)),
                pl.BlockSpec(rows.shape, lambda t, place: (0, 0)),
            ]
            + pinned([w]) + pinned(pins),
            out_specs=[tile(width)] * 2 + [tile(units)] * 2 + specs,
            scratch_shapes=[
                pltpu.VMEM(w.shape, BF16), pltpu.VMEM((length, width), BF16), pltpu.SemaphoreType.DMA,
            ],
        ),
        out_shape=[shape(width, BF16)] * 2 + [shape(units, F32), shape(units, BF16)] + shapes,
        compiler_params=params(),
        cost_estimate=light(),
        name="ffn_forward",
    )(place, x, x, rows, w, *pins)


def call_ffn_gate(recept, cot_mine, cot_other, gate, place, pins):
    tokens, width = recept.shape
    length = 256
    half = gate.shape[1]
    step = min(2 * CHUNK, half)
    rows = 128
    tiles, per = tokens // length, length // rows
    split = cot_mine.shape[0] < tiles * per

    def kernel(place_ref, recept_ref, mine_ref, other_ref, gate_ref, *refs):
        recept = recept_ref[...]
        is_mine = pl.program_id(0) // (tiles // 2) == place_ref[1]
        for at in range(0, half, step):
            c = slice(at, at + step)
            gate = jax.nn.sigmoid(nn(recept, gate_ref[:, c]))
            for i in range(per):
                r = slice(i * rows, (i + 1) * rows)
                cot = jnp.where(is_mine, mine_ref[i, :, c].astype(F32), other_ref[i, :, c].astype(F32))
                refs[-1][r, c] = (cot * gate[r, :]).astype(BF16)

    column = (lambda place: place[1]) if half < width else (lambda place: 0)

    def cot_spec(core):
        if not split:
            return pl.BlockSpec((per, rows, half), lambda t, place: (t, 0, column(place)))
        at = lambda t, place: jnp.clip(t - core(place) * (tiles // 2), 0, tiles // 2 - 1)
        return pl.BlockSpec((per, rows, half), lambda t, place: (at(t, place), 0, column(place)))

    return pl.pallas_call(
        kernel,
        grid_spec=pltpu.PrefetchScalarGridSpec(
            num_scalar_prefetch=1,
            grid=(tiles,),
            in_specs=[
                pl.BlockSpec((length, width), lambda t, place: (t, 0)),
                cot_spec(lambda place: place[1]), cot_spec(lambda place: 1 - place[1]),
                pl.BlockSpec(gate.shape, lambda t, place: (0, 0), pipeline_mode=pl.Buffered(1)),
            ]
            + pinned(pins),
            out_specs=pl.BlockSpec((length, half), lambda t, place: (t, 0)),
        ),
        out_shape=jax.ShapeDtypeStruct((tokens, half), BF16),
        compiler_params=params(),
        cost_estimate=light(),
        name="ffn_gate",
    )(place, recept, cot_mine, cot_other, gate, *pins)


def ffn_backward(halves, place_ref, mine_ref, other_ref, hidden_ref, w_all, *refs):
    d_values_ref, d_hidden_ref = refs[-5 - halves : -3 - halves]
    outs = refs[-3 - halves : -3]
    w_ref, value_ref, sem = refs[-3:]
    width = d_values_ref.shape[1]
    half = mine_ref.shape[1]
    units = hidden_ref.shape[1]
    load = pltpu.make_async_copy(w_all, w_ref, sem)

    @pl.when(pl.program_id(0) == 0)
    def _():
        load.start()

    cores = ((mine_ref, place_ref[1]), (other_ref, 1 - place_ref[1])) if half < width else ((mine_ref, 0),)
    for ref, core in cores:
        d_values_ref[:, pl.ds(pl.multiple_of(core * half, half), half)] = ref[...]

    @pl.when(pl.program_id(0) == 0)
    def _():
        load.wait()

    d_hidden = (nn(d_values_ref[...], w_ref[:, units:]) * 2.0 * hidden_ref[...]).astype(BF16)
    d_hidden_ref[...] = d_hidden
    for at in range(0, width, 2 * CHUNK):
        c = slice(at, at + 2 * CHUNK)
        value_ref[:, c] = nt(d_hidden, w_ref[c, :units]).astype(BF16)
    store_half(place_ref, value_ref, outs)


def call_ffn_backward(mine, other, hidden, w, place, seqs, pins):
    tokens, half = mine.shape
    width = w.shape[0]
    length = 256
    units = hidden.shape[1]
    tile = lambda n: pl.BlockSpec((length, n), lambda t, place: (t, 0))
    shape = lambda n: jax.ShapeDtypeStruct((tokens, n), BF16)
    specs, shapes = two_halves(tokens, width, length, seqs)
    return pl.pallas_call(
        lambda *refs: ffn_backward(len(specs), *refs),
        grid_spec=pltpu.PrefetchScalarGridSpec(
            num_scalar_prefetch=1,
            grid=(tokens // length,),
            in_specs=[tile(half), tile(half), tile(units)] + pinned([w]) + pinned(pins),
            out_specs=[tile(width), tile(units)] + specs,
            scratch_shapes=[
                pltpu.VMEM(w.shape, BF16), pltpu.VMEM((length, width), BF16), pltpu.SemaphoreType.DMA,
            ],
        ),
        out_shape=[shape(width), shape(units)] + shapes,
        compiler_params=params(),
        cost_estimate=light(),
        name="ffn_backward",
    )(place, mine, other, hidden, w, *pins)


def call_grad(x, d, pins):
    tokens, width = x.shape
    units = d.shape[1]
    columns = 512 if tokens <= 1024 else 256

    def kernel(x_ref, d_ref, *refs):
        refs[-1][...] = tn(x_ref[...], d_ref[...]).astype(BF16)

    return pl.pallas_call(
        kernel,
        grid=(width // columns,),
        in_specs=[
            pl.BlockSpec((tokens, columns), lambda t: (0, t)),
            pl.BlockSpec(d.shape, lambda t: (0, 0), pipeline_mode=pl.Buffered(1)),
        ]
        + pinned(pins),
        out_specs=pl.BlockSpec((columns, units), lambda t: (t, 0)),
        out_shape=jax.ShapeDtypeStruct((width, units), BF16),
        compiler_params=params(),
        cost_estimate=light(),
        name="grad",
    )(x, d, *pins)


def call_grads(xs, ds, gated, d_att, segs, pins):
    tokens, width = d_att.shape
    cw = gated.shape[1]
    rows, count = width // segs, len(xs)
    columns = 512 if tokens <= 1024 else 128
    per, cut = rows // columns, cw // segs

    def kernel(*refs):
        x_refs, d_refs, gated_ref, att_ref, out_ref = refs[:count], refs[count : 2 * count], refs[-3 - len(pins)], refs[-2 - len(pins)], refs[-1]
        s, at = pl.program_id(0) // per, pl.program_id(0) % per
        for j in range(count):
            out_ref[s, j, pl.ds(pl.multiple_of(at * columns, columns), columns), :] = tn(
                x_refs[j][...], d_refs[j][...]
            ).astype(BF16)
        result = tn(gated_ref[...], att_ref[...]).astype(BF16)
        each = columns // cw
        for i in range(each):
            to = pl.multiple_of((pl.program_id(0) * each + i) * cut, cut)
            for m in range(segs):
                out_ref[m, count, pl.ds(to, cut), :] = result[m * cut : (m + 1) * cut, i * cw : (i + 1) * cw]

    block = pl.BlockSpec((tokens, columns), lambda t: (0, t))
    fixed = pl.BlockSpec((tokens, cw), lambda t: (0, 0), pipeline_mode=pl.Buffered(1))
    shape = (segs, count + 1, rows, cw)
    return pl.pallas_call(
        kernel,
        grid=(width // columns,),
        in_specs=[block] * count + [fixed] * count + [fixed, block] + pinned(pins),
        out_specs=pl.BlockSpec(shape, lambda t: (0, 0, 0, 0)),
        out_shape=jax.ShapeDtypeStruct(shape, BF16),
        compiler_params=params(),
        cost_estimate=light(),
        name="grads",
    )(*xs, *ds, gated, d_att, *pins)


def call_ffn_norm(x, blocks, rows, pins):
    length, width = x.shape
    count = blocks.shape[0]

    def kernel(x_ref, blocks_ref, rows_ref, *refs):
        sum_ref, unit_ref, scale_ref, normed_ref, low_ref = refs[-5:]
        lanes = 128
        total = jnp.zeros((length, lanes), F32)
        for at in range(0, width, lanes):
            c = slice(at, at + lanes)
            value = x_ref[:, c].astype(F32)
            for i in range(count):
                value = value + blocks_ref[i, :, c].astype(F32)
            sum_ref[:, c] = value
            total = total + value
        mean = jnp.sum(total, 1, keepdims=True) / width
        total = jnp.zeros((length, lanes), F32)
        for at in range(0, width, lanes):
            center = sum_ref[:, at : at + lanes] - mean
            total = total + center * center
        scale = lax.rsqrt(jnp.sum(total, 1, keepdims=True) / width + LAYER_EPSILON)
        scale_ref[...] = jnp.broadcast_to(scale, scale_ref.shape)
        for at in range(0, width, lanes):
            c = slice(at, at + lanes)
            unit = (sum_ref[:, c] - mean) * scale
            unit_ref[:, c] = unit
            normed = unit * rows_ref[0:1, c] + rows_ref[1:2, c]
            normed_ref[:, c] = normed
            low_ref[:, c] = normed.astype(BF16)

    shape = lambda n, dtype: jax.ShapeDtypeStruct((length, n), dtype)
    return pl.pallas_call(
        kernel,
        grid=(1,),
        in_specs=[whole(x), whole(blocks), whole(rows)] + pinned(pins),
        out_specs=[pl.BlockSpec((length, n), lambda t: (0, 0)) for n in (width, width, 128, width, width)],
        out_shape=[shape(width, F32), shape(width, F32), shape(128, F32), shape(width, F32), shape(width, BF16)],
        compiler_params=params(),
        cost_estimate=light(),
        name="ffn_norm",
    )(x, blocks, rows, *pins)


def call_ffn_local(place, recept_in, blocks, cot, residual, gate_mine, gate_other, group, pins):
    length, width = recept_in.shape
    count, half = blocks.shape[0], gate_mine.shape[1]
    cw = width // group
    step = min(2 * CHUNK, half)

    def kernel(place_ref, recept_ref, blocks_ref, cot_ref, residual_ref, mine_ref, other_ref, *refs):
        out_ref, cut_ref, d_ref, gate_ref = refs[-4:]
        recept = recept_ref[...]
        cores = ((mine_ref, place_ref[1]), (other_ref, 1 - place_ref[1])) if half < width else ((mine_ref, 0),)
        for ref, core in cores:
            for at in range(0, half, step):
                c = pl.ds(pl.multiple_of(core * half + at, step), step)
                gate = jax.nn.sigmoid(nn(recept, ref[:, at : at + step]))
                values = sum(blocks_ref[i, :, c].astype(F32) for i in range(count))
                out_ref[:, c] = (residual_ref[:, c] + gate * values).astype(BF16)
                gate_ref[:, c] = (cot_ref[:, c].astype(F32) * values * gate * (1.0 - gate)).astype(BF16)
        for i in range(group):
            cut_ref[i] = gate_ref[:, i * cw : (i + 1) * cw]
        for at in range(0, width, 2 * CHUNK):
            c = slice(at, at + 2 * CHUNK)
            d = jnp.zeros((length, 2 * CHUNK), F32)
            for ref, core in cores:
                d = d + nt(gate_ref[:, pl.ds(pl.multiple_of(core * half, half), half)], ref[c, :])
            d_ref[:, c] = d

    fixed = lambda a: pl.BlockSpec(a.shape, lambda t, place: (0,) * a.ndim)
    shapes = [(length, width), (group, length, cw), (length, width)]
    return pl.pallas_call(
        kernel,
        grid_spec=pltpu.PrefetchScalarGridSpec(
            num_scalar_prefetch=1,
            grid=(1,),
            in_specs=[fixed(a) for a in (recept_in, blocks, cot, residual, gate_mine, gate_other)] + pinned(pins),
            out_specs=[pl.BlockSpec(s, lambda t, place, n=len(s): (0,) * n) for s in shapes],
            scratch_shapes=[pltpu.VMEM((length, width), BF16)],
        ),
        out_shape=[jax.ShapeDtypeStruct(s, dtype) for s, dtype in zip(shapes, (BF16, BF16, F32))],
        compiler_params=params(),
        cost_estimate=light(),
        name="ffn_local",
    )(place, recept_in, blocks, cot, residual, gate_mine, gate_other, *pins)


def call_out(place, gated, own, parts, sender, seqs, pins):
    tokens, cw = gated.shape
    width = own.shape[1]
    length = 256
    specs, shapes = two_halves(tokens, width, length, seqs)

    def kernel(place_ref, gated_ref, own_ref, *refs):
        w_ref, value_ref = refs[-2:]

        @pl.when(pl.program_id(0) == 0)
        def _():
            received = refs[0][...]
            for ref in refs[1 : len(parts)]:
                received = received + ref[...]
            w_ref[...] = jnp.where(place_ref[2] == 1, own_ref[...], received)

        for at in range(0, width, 2 * CHUNK):
            c = slice(at, at + 2 * CHUNK)
            value_ref[:, c] = nn(gated_ref[...], w_ref[:, c]).astype(BF16)
        store_half(place_ref, value_ref, refs[-2 - len(specs) : -2])

    fixed = lambda a: pl.BlockSpec(a.shape, lambda t, place: (0, 0))

    return pl.pallas_call(
        kernel,
        grid_spec=pltpu.PrefetchScalarGridSpec(
            num_scalar_prefetch=1,
            grid=(tokens // length,),
            in_specs=[pl.BlockSpec((length, cw), lambda t, place: (t, 0))] + [fixed(a) for a in (own, *parts)]
            + pinned(pins),
            out_specs=specs + [pl.BlockSpec((cw, width), lambda t, place: (0, 0))],
            scratch_shapes=[pltpu.VMEM((length, width), BF16)],
        ),
        out_shape=shapes + [jax.ShapeDtypeStruct((cw, width), BF16)],
        compiler_params=params(),
        cost_estimate=light(),
        name="out_projection",
    )(jnp.concatenate([place, sender.reshape(1)]), gated, own, *parts, *pins)


def call_add(mine, other, pins):
    rows, width = mine.shape
    length = 128

    def kernel(a_ref, b_ref, *refs):
        refs[-1][...] = (a_ref[...].astype(F32) + b_ref[...].astype(F32)).astype(BF16)

    tile = pl.BlockSpec((length, width), lambda t: (t, 0))
    return pl.pallas_call(
        kernel,
        grid=(rows // length,),
        in_specs=[tile, tile] + pinned(pins),
        out_specs=tile,
        out_shape=jax.ShapeDtypeStruct((rows, width), BF16),
        compiler_params=params(),
        cost_estimate=light(),
        name="add",
    )(mine, other, *pins)


def call_wkv_backward(length, d, r, k, v, w, graw, wkv, dm, w_out, own, ones, sums, start, ends, adj, pins):
    tokens, cw = r.shape
    count = tokens // length
    tile = lambda n: pl.BlockSpec((length, n), lambda t: (count - 1 - t, 0))
    shape = lambda dtype: jax.ShapeDtypeStruct((tokens, cw), dtype)
    wide = dm.shape[1]
    return pl.pallas_call(
        wkv_backward,
        grid=(count,),
        in_specs=[tile(d.shape[1])] + [tile(cw)] * 6 + [tile(wide)]
        + [whole(a) for a in (w_out, own, ones, sums, start)]
        + [
            pl.BlockSpec((1, HEAD, cw), lambda t: (jnp.maximum(count - 2 - t, 0), 0, 0)),
            pl.BlockSpec((1, HEAD, cw), lambda t: (count - 1 - t, 0, 0)),
        ]
        + pinned(pins),
        out_specs=[pl.BlockSpec((32, cw), lambda t: (0, 0)), pl.BlockSpec((wide, cw), lambda t: (0, 0))] + [tile(cw)] * 5,
        out_shape=[jax.ShapeDtypeStruct((32, cw), F32), jax.ShapeDtypeStruct((wide, cw), F32)]
        + [shape(BF16)] * 4 + [shape(F32)],
        scratch_shapes=[pltpu.VMEM((cw, cw), F32)],
        compiler_params=params(),
        cost_estimate=light(),
        name="wkv_backward",
    )(d, r, k, v, w, graw, wkv, dm, w_out, own, ones, sums, start, ends, adj, *pins)


def call_mix_backward(
    rank, length, x, rows, lm, dm, dr, dk, dv, dg, dpre, wn, ww, fn, fw, more, place, parts, decays, seqs, pins
):
    tokens, width = x.shape
    cw = dr.shape[1]
    count = tokens // length
    edge = 16
    tile = lambda n: pl.BlockSpec((length, n), lambda t, place: (count - 1 - t, 0))
    before = pl.BlockSpec((edge, width), lambda t, place: (jnp.maximum((count - 1 - t) * (length // edge) - 1, 0), 0))
    fixed = lambda a: pl.BlockSpec(a.shape, lambda t, place: (0, 0))
    packed = 16 + 10 * rank + decays + more.shape[0]
    specs, shapes = two_halves(tokens, width, length, seqs, backward=True)
    return pl.pallas_call(
        lambda *refs: mix_backward(rank, len(specs), *refs),
        grid_spec=pltpu.PrefetchScalarGridSpec(
            num_scalar_prefetch=1,
            grid=(count,),
            in_specs=[tile(width), before, fixed(rows), tile(lm.shape[1]), tile(dm.shape[1])] + [tile(cw)] * 5
            + [fixed(a) for a in (wn, ww, fn, fw, more)] + pinned(parts) + pinned(pins),
            out_specs=[pl.BlockSpec((packed, width), lambda t, place: (0, 0))] + specs,
            scratch_shapes=[pltpu.VMEM((n, width), F32) for n in (8 * 8, wn.shape[0], wn.shape[0], fn.shape[0])]
            + [pltpu.VMEM((length, width), BF16), pltpu.VMEM((8, width), F32)]
            + [pltpu.VMEM((length, width), F32)] * 4 + part_scratch(parts),
        ),
        out_shape=[jax.ShapeDtypeStruct((packed, width), BF16)] + shapes,
        compiler_params=params(),
        cost_estimate=light(),
        name="mix_backward",
    )(place, x, x, rows, lm, dm, dr, dk, dv, dg, dpre, wn, ww, fn, fw, more, *parts, *pins)


def gather_group(block):
    return lax.all_gather(block, TP, axis=0, tiled=True)


SWAP = [(0, 1), (1, 0)]


def reduce_halves(mine, other, pins):
    total = call_add(mine, lax.ppermute(other, "seq", SWAP), pins)
    return reduce_chan(total), total


def reduce_chan(total):
    chans = lax.axis_size("chan")
    return lax.all_to_all(total.reshape(chans, -1, total.shape[1]), "chan", 0, 0, tiled=True)


def add_up(blocks):
    return jnp.sum(blocks.astype(F32), 0)


def reduce_group(parts, pins=()):
    if len(parts) == 2:
        return reduce_halves(*parts, pins)
    total = lax.psum_scatter(parts[0], "seq", scatter_dimension=0, tiled=True)
    return reduce_chan(total), total


def after(a, before):
    corner = before[(slice(0, 1),) * before.ndim].reshape((1,) * a.ndim)
    return a + (corner.astype(F32) * 0.0).astype(a.dtype)


def after_all(a, others):
    for other in others:
        a = after(a, other)
    return a


def next_row(row, by):
    count = lax.axis_size(TP)
    return lax.ppermute(row, TP, [(i, i + by) for i in range(count) if 0 <= i + by < count])


def shift_down(values, first_row):
    return jnp.concatenate([first_row, values[:-1]], 0)


def unit_rows(values):
    center = values - jnp.mean(values, -1, keepdims=True)
    scale = lax.rsqrt(jnp.mean(center * center, -1, keepdims=True) + LAYER_EPSILON)
    return center * scale, scale


def on_device(
    sequence_elements,
    segment_predecessor_entries,
    opening_recurrences,
    first_layernorm_gain,
    first_layernorm_shift_term,
    lag_blend_coefficients,
    lag_narrowing_factor,
    lag_widening_factors,
    fading_exponent_baseline,
    fading_narrowing_factor,
    fading_widening_factor,
    present_reward,
    acceptor_projection,
    address_projection,
    content_projection,
    valve_projection,
    timemix_result_projection,
    subspace_cluster_gain,
    subspace_cluster_shift_term,
    second_layernorm_gain,
    second_layernorm_shift_term,
    feedforward_lag_blends,
    feedforward_address_projection,
    feedforward_acceptor_projection,
    feedforward_content_projection,
    result_adjoint,
    final_recurrence_adjoint,
):
    segs, seqs, chans = lax.axis_size("seg"), lax.axis_size("seq"), lax.axis_size("chan")
    group = seqs * chans
    p = lax.axis_index(TP)
    x = sequence_elements[0]
    length, width = x.shape
    tokens = group * length
    cw = width // group
    heads = cw // HEAD
    rank = lag_widening_factors.shape[1] // 5
    ranks, decays = 5 * rank, fading_widening_factor.shape[1]

    def columns(a, axis=-1):
        return lax.dynamic_slice_in_dim(a, p * cw, cw, axis % a.ndim)

    me, seg = lax.axis_index("seq"), lax.axis_index("seg")
    block = width // (segs * group)
    rows_seg = width // segs
    flips = [[(s, s ^ m) for s in range(segs)] for m in range(segs)]

    def seg_parts(a):
        return [a] + [lax.ppermute(a, "seg", flips[m]) for m in range(1, segs)]

    def own_part(a, axis):
        size = a.shape[axis] // seqs
        return lax.dynamic_slice_in_dim(a, me * size, size, axis)

    def reduce_segs(piece):
        sent = [piece(seg ^ m) for m in range(1, segs)]
        return sum((lax.ppermute(a, "seg", flips[m + 1]).astype(F32) for m, a in enumerate(sent)), piece(seg).astype(F32)), sent

    def reduce_rows(a):
        return lax.psum_scatter(a, "seg", scatter_dimension=0, tiled=True)

    x_all = gather_group(x)
    four = seg_parts(
        jnp.concatenate(
            [columns(a) for a in (acceptor_projection, address_projection, content_projection, valve_projection)], 1
        )
    )
    share = group // segs
    out_rows = after(lax.dynamic_slice_in_dim(timemix_result_projection, (p % share) * cw, cw, 0), four[-1])
    out_parts = [
        lax.ppermute(out_rows, ALL, [((j // share) * group + j, ((j // share) ^ m) * group + j) for j in range(group)])
        for m in range(1, segs)
    ]
    ffn_part = jnp.concatenate([own_part(a, 1) for a in (feedforward_address_projection, feedforward_content_projection)], 1)
    w_ffn = lax.all_gather(after_all(ffn_part, four[1:]), "seg", axis=0, tiled=True)
    cot = after(result_adjoint[0], x_all)
    adjoints = final_recurrence_adjoint[0, 0]
    if seqs == 2:
        adjoints = adjoints.reshape(HEAD, seqs, chans, cw).transpose(2, 0, 1, 3).reshape(chans, HEAD, seqs * cw)
        high = adjoints.astype(BF16)
        adjoints = jnp.concatenate([high, (adjoints - high.astype(F32)).astype(BF16)], 1).reshape(chans, -1, width)
        sent = jnp.concatenate([jnp.broadcast_to(cot[None], (chans, length, width)), adjoints], 1)
        cot_mine = lax.all_to_all(sent, "chan", 0, 0, tiled=True)
        cot_other = lax.ppermute(cot_mine, "seq", SWAP)

        def state_part(a):
            a = a[:, length:].reshape(chans, 2, HEAD, seqs, cw).astype(F32)
            return lax.dynamic_index_in_dim(a[:, 0] + a[:, 1], me, 2, False)

        low, high = state_part(cot_mine), state_part(cot_other)
        adjoints = jnp.where(me == 0, jnp.concatenate([low, high]), jnp.concatenate([high, low]))
    else:
        cot_mine = cot_other = gather_group(cot).reshape(group, length, width)
        adjoints = lax.all_to_all(adjoints.reshape(HEAD, group, cw).transpose(1, 0, 2), TP, 0, 0, tiled=True)

    rows = jnp.concatenate(
        [
            first_layernorm_gain[None], first_layernorm_shift_term[None], lag_blend_coefficients.T,
            segment_predecessor_entries[0, 0][None], fading_exponent_baseline[None], present_reward[None],
            subspace_cluster_gain[None], subspace_cluster_shift_term[None], jnp.zeros((11, width), F32),
        ]
    )
    own = lax.dynamic_slice(rows, (FIRST + 1, p * cw), (8, cw))
    wn, ww, fn = lag_narrowing_factor.T, lag_widening_factors.T, fading_narrowing_factor.T
    fw = columns(fading_widening_factor.T)
    head_of = np.arange(cw) // HEAD
    ones = jnp.asarray(head_of[:, None] == head_of[None, :], BF16)
    start = columns(opening_recurrences[0])
    place = jnp.stack([seg, me]).astype(jnp.int32)

    gated, xk, xv, xr, xg, r, k, v, w, graw, wkv, lm, dm, ends = call_forward(
        rank, length, x_all, rows, own, wn, ww, fn, fw, ones, start, place, four, ()
    )
    *out, w_out = call_out(
        place, gated, out_rows, out_parts, (seg == p // share).astype(jnp.int32), seqs, [cot_mine]
    )
    out_blocks, _ = reduce_group(out)

    mix_key, mix_recept = feedforward_lag_blends[:, 0], feedforward_lag_blends[:, 1]
    first_row = segment_predecessor_entries[0, 1][None]
    ffn_rows = jnp.concatenate(
        [second_layernorm_gain[None], second_layernorm_shift_term[None], first_row, feedforward_lag_blends.T, jnp.zeros((3, width), F32)]
    )
    residual, ffn_unit, ffn_scale, ffn_normed, normed_low = call_ffn_norm(
        x, out_blocks, ffn_rows, [w_ffn]
    )
    ffn_scale = ffn_scale[:, :1]
    normed_all = gather_group(normed_low)
    gate_part = after(own_part(feedforward_acceptor_projection, 1), normed_all)
    gate_mine = lax.all_gather(gate_part, "seg", axis=0, tiled=True)
    before = lax.dynamic_slice_in_dim(normed_all, jnp.maximum(p * length - 1, 0), 1, 0).astype(F32)
    previous = jnp.where(p == 0, first_row, before)
    ffn_delta = shift_down(ffn_normed, previous) - ffn_normed
    recept_in = (ffn_normed + ffn_delta * mix_recept).astype(BF16)
    cot = result_adjoint[0].astype(F32)
    if seqs == 2:
        gate_other = lax.ppermute(gate_mine, "seq", SWAP)
    else:
        gate_mine = gate_other = lax.all_gather(gate_mine, "seq", axis=1, tiled=True)

    key_in, recept_all, hidden, squared, *values = call_ffn_forward(normed_all, ffn_rows, w_ffn, place, seqs, ())
    value_blocks, sent = reduce_group(values)
    d_mine = call_ffn_gate(recept_all, cot_mine, cot_other, gate_mine, place, [sent])
    d_other = lax.ppermute(d_mine, "seq", SWAP) if seqs == 2 else d_mine
    d_values, d_hidden, *d_key = call_ffn_backward(d_mine, d_other, hidden, w_ffn, place, seqs, [value_blocks])
    key_blocks, sent = reduce_group(d_key)
    grad_ffn_value = reduce_rows(call_grad(d_values, squared, [sent]))

    output, d_gate_cut, d_fr = call_ffn_local(
        place, recept_in, value_blocks, result_adjoint[0], residual, gate_mine, gate_other, group, ()
    )
    d_fk = add_up(key_blocks)
    d_fdelta = d_fk * mix_key + d_fr * mix_recept
    d_normed = d_fk + d_fr - d_fdelta + jnp.concatenate([d_fdelta[1:], next_row(d_fdelta[:1], -1)], 0)
    g = d_normed * second_layernorm_gain
    d_residual = cot + ffn_scale * (
        g - jnp.mean(g, -1, keepdims=True) - ffn_unit * jnp.mean(g * ffn_unit, -1, keepdims=True)
    )
    d_att_own = after(d_residual.astype(BF16), grad_ffn_value)
    d_att = gather_group(d_att_own)
    grad_ffn_key = call_grad(key_in, d_hidden, [d_att_own])
    ffn_sums = jnp.stack(
        [
            jnp.sum(d_normed * ffn_unit, 0), jnp.sum(d_normed, 0),
            jnp.sum(ffn_delta * d_fk, 0), jnp.sum(ffn_delta * d_fr, 0),
        ]
    )

    def join_hidden(a):
        return lax.all_to_all(a, "seq", 0, 1, tiled=True).astype(F32)

    ends_high = ends.astype(BF16)
    ends_low = (ends - ends_high.astype(F32)).astype(BF16)
    moved = after(jnp.concatenate([d_gate_cut, ends_high, ends_low], 1), d_att)
    moved = lax.all_to_all(moved, TP, 0, 0, tiled=True)
    d_gate_own = moved[:, :length].reshape(tokens, cw)
    end_states = moved[:, length : length + HEAD].astype(F32) + moved[:, length + HEAD :].astype(F32)
    own_sums, decay_up, dr, dk, dv, dg, d_pre = call_wkv_backward(
        length, d_att, r, k, v, w, graw, wkv, dm, w_out, own, ones, sum_table(length), start, ends, adjoints,
        [grad_ffn_key],
    )
    grads = call_grads([xr, xk, xv, xg, recept_all], [dr, dk, dv, dg, d_gate_own], gated, d_att, segs, ())
    summed = reduce_rows(grads.reshape(-1, cw)).reshape(6, rows_seg, cw)
    more = jnp.concatenate([jnp.sum(own_sums.reshape(4, 8, cw), 1), decay_up[:decays]], 0)
    more = lax.dynamic_update_slice(jnp.zeros((16 * -(-(8 + decays) // 16), width), F32), more, (4, p * cw))
    more = lax.dynamic_update_slice(more, ffn_sums, (0, 0)).astype(BF16)
    packed, *dx = call_mix_backward(
        rank, length, x_all, rows, lm, dm, dr, dk, dv, dg, d_pre, wn, ww, fn, fw, more, place, four, decays, seqs,
        [grads],
    )
    dx_blocks, _ = reduce_group(dx)
    dx_total = add_up(dx_blocks)
    input_grad = d_residual + dx_total

    five = summed[:5].reshape(5, group, block, cw).transpose(1, 0, 2, 3).reshape(group, -1, cw)
    grad_ffn_value = join_hidden(after(grad_ffn_value, dx_blocks))
    grad_ffn_key = join_hidden(after(reduce_rows(grad_ffn_key), dx_blocks))
    grad_out = summed[5].reshape(group, cw // segs, cw).transpose(1, 0, 2).reshape(cw // segs, width)
    grad_out = lax.ppermute(
        grad_out, ALL, [(i * group + j, segs * j + i) for i in range(segs) for j in range(group)]
    ).astype(F32)
    small, _ = reduce_segs(lambda s: lax.dynamic_slice_in_dim(packed, s * rows_seg, rows_seg, 1))
    count = small.shape[0]
    small = small.astype(BF16).reshape(count, group, block).transpose(1, 0, 2).reshape(group, -1, cw)
    mixed = after(jnp.concatenate([five, small], 1), dx_blocks)
    mixed = lax.all_to_all(mixed, TP, 0, 0, tiled=True)
    five, small = mixed[:, : 5 * block], mixed[:, 5 * block :]
    five = five.reshape(group, 5, block, cw).transpose(1, 2, 0, 3).reshape(5, block, width).astype(F32)
    small = jnp.sum(small.astype(F32).reshape(group, count, block), 0)
    norm_gain, norm_bias, shift_mix = small[0], small[1], small[2:8].T
    at = 16
    shift_down_grad, at = small[at : at + ranks].T, at + ranks
    shift_up_grad, at = small[at : at + ranks].T, at + ranks
    d_down, at = small[at : at + decays].T, at + decays
    ffn_gain, ffn_bias, ffn_shift_mix = small[at], small[at + 1], small[at + 2 : at + 4].T
    decay_base, reward, group_gain, group_bias = (small[at + 4 + i] for i in range(4))
    d_up = small[at + 8 : at + 8 + decays].T
    end_states = end_states.transpose(1, 0, 2).reshape(HEAD, width)
    return (
        output[None],
        end_states[None, None],
        input_grad[None],
        norm_gain,
        norm_bias,
        shift_mix,
        shift_down_grad,
        shift_up_grad,
        decay_base,
        d_down,
        d_up,
        reward,
        five[0],
        five[1],
        five[2],
        five[3],
        grad_out,
        group_gain,
        group_bias,
        ffn_gain,
        ffn_bias,
        ffn_shift_mix,
        grad_ffn_key,
        five[4],
        grad_ffn_value,
    )


def solution(mesh):
    rows, tokens = P("seg", None), P("seg", TP, None)
    matrix = P("seg", "chan")
    vector_out, matrix_out = P(ALL), P(ALL, None)
    ffn_out = P(("seg", "seq"), "chan")
    return jax.shard_map(
        on_device,
        mesh=mesh,
        in_specs=(tokens, P("seg", None, None), P("seg", None, None)) + (P(),) * 9 + (rows,) * 5 + (P(),) * 5
        + (matrix, rows, matrix, tokens, P("seg", TP, None, None)),
        out_specs=(tokens, P("seg", TP, None, None), tokens) + (vector_out,) * 2 + (matrix_out,) * 3 + (vector_out,)
        + (matrix_out,) * 2 + (vector_out,) + (matrix_out,) * 5 + (vector_out,) * 4
        + (matrix_out, ffn_out, matrix_out, ffn_out),
        check_vma=False,
    )
```

```python
import jax
import jax.numpy as jnp
import numpy as np
from jax import lax
from jax.experimental import pallas as pl
from jax.experimental.pallas import tpu as pltpu
from jax.sharding import PartitionSpec as P

HEAD = 64
TP = ("seq", "chan")
ALL = ("seg", "seq", "chan")
LAYER_EPSILON = 1e-05
GROUP_EPSILON = 0.00064
F32 = jnp.float32
BF16 = jnp.bfloat16
CHUNK = 512
TOKENS = 128
VMEM = 56 * 2**20


def dot(a, b, dims):
    return lax.dot_general(
        a.astype(BF16), b.astype(BF16), (dims, ((), ())), preferred_element_type=F32
    )


def nn(a, b):
    return dot(a, b, ((1,), (0,)))


def nt(a, b):
    return dot(a, b, ((1,), (1,)))


def tn(a, b):
    return dot(a, b, ((0,), (0,)))


def iota(shape, axis):
    return lax.broadcasted_iota(jnp.int32, shape, axis)


def head_sum(values, ones):
    high = values.astype(BF16)
    low = (values - high.astype(F32)).astype(BF16)
    return nn(high, ones) + nn(low, ones)


def pyramid(w):
    length = w.shape[0]
    row = iota(w.shape, 0)
    before, after, total = jnp.zeros_like(w), jnp.zeros_like(w), w
    levels = []
    half = 1
    while half < length:
        upper = (row & half) != 0
        levels.append((half, upper, jnp.where(upper, before, after)))
        sibling = jnp.where(upper, pltpu.roll(total, half, 0), pltpu.roll(total, length - half, 0))
        before = jnp.where(upper, before + sibling, before)
        after = jnp.where(upper, after, after + sibling)
        total = total + sibling
        half *= 2
    return levels, before, after, total


def split_heads(values, heads):
    if heads == 1:
        return [values.astype(BF16)]
    lane = iota(values.shape, 1) // HEAD
    return [jnp.where(lane == head, values, 0.0).astype(BF16) for head in range(heads)]


def row_stats(x_ref):
    rows, width = x_ref.shape
    step = 128
    total = jnp.zeros((rows, step), F32)
    for at in range(0, width, step):
        total = total + x_ref[:, at : at + step].astype(F32)
    mean = jnp.sum(total, 1, keepdims=True) / width
    total = jnp.zeros((rows, step), F32)
    for at in range(0, width, step):
        center = x_ref[:, at : at + step].astype(F32) - mean
        total = total + center * center
    return mean, lax.rsqrt(jnp.sum(total, 1, keepdims=True) / width + LAYER_EPSILON)


def fold(values):
    rows, width = values.shape
    return jnp.sum(values.reshape(rows // 8, 8, width), 0)


def rank_blocks(values, rank):
    lane = iota(values.shape, 1) // rank
    return jnp.concatenate([jnp.where(lane == j, values, 0.0).astype(BF16) for j in range(5)], 0)


def spread(states, same):
    flat = states.T
    return jnp.concatenate([flat] * (flat.shape[0] // HEAD), 1) * same


def compact(state):
    return sum(state[:, at : at + HEAD] for at in range(0, state.shape[1], HEAD)).T


def part_copies(place_ref, parts, full_ref, sem):
    rows = parts[0].shape[0]
    copies = []
    for m, part in enumerate(parts):
        at = pl.multiple_of((place_ref[0] ^ m) * rows, rows)
        copies.append(pltpu.make_async_copy(part, full_ref.at[pl.ds(at, rows), :], sem.at[m]))
    return copies


def load_parts(place_ref, parts, full_ref, sem):
    for copy in part_copies(place_ref, parts, full_ref, sem):
        copy.start()


def wait_parts(place_ref, parts, full_ref, sem):
    @pl.when(pl.program_id(0) == 0)
    def _():
        for copy in part_copies(place_ref, parts, full_ref, sem):
            copy.wait()


GAIN, BIAS, MIX, FIRST = 0, 1, 2, 8


def mix_forward(
    rank, x_ref, rows_ref, own_ref, wn_ref, ww_ref, fn_ref, fw_ref,
    ones_ref, start_ref, place_ref, part0, part1, part2, part3, *refs,
):
    (
        gated_ref, xk_ref, xv_ref, xr_ref, xg_ref, r_ref, k_ref, v_ref, w_ref, graw_ref, wkv_ref, lm_ref, dm_ref,
        ends_ref, normed_ref, delta_ref, carry_ref, state_ref, four_ref, sem,
    ) = refs[-20:]
    step = pl.program_id(0)
    length, width = x_ref.shape
    own = own_ref.shape[1]
    heads = own // HEAD

    @pl.when(step == 0)
    def _():
        carry_ref[...] = jnp.broadcast_to(rows_ref[FIRST : FIRST + 1, :], carry_ref.shape)
        state_ref[...] = spread(start_ref[...], ones_ref[...].astype(F32))
        load_parts(place_ref, (part0, part1, part2, part3), four_ref, sem)

    mean, scale = row_stats(x_ref)
    first = iota((length, CHUNK), 0) == 0
    narrow = jnp.zeros((length, wn_ref.shape[0]), F32)
    for at in range(0, width, CHUNK):
        c = slice(at, at + CHUNK)
        normed = (x_ref[:, c].astype(F32) - mean) * scale * rows_ref[GAIN : GAIN + 1, c] + rows_ref[BIAS : BIAS + 1, c]
        delta = jnp.where(first, carry_ref[0:1, c], pltpu.roll(normed, 1, 0)) - normed
        carry_ref[0:1, c] = normed[length - 1 : length, :]
        normed_ref[:, c] = normed
        delta_ref[:, c] = delta
        narrow = narrow + nt(normed + delta * rows_ref[MIX : MIX + 1, c], wn_ref[:, c])
    middle = jnp.tanh(narrow)
    lm_ref[...] = middle
    blocks = rank_blocks(middle, rank)
    decay_in = jnp.zeros((length, fn_ref.shape[0]), F32)
    for at in range(0, width, CHUNK):
        c = slice(at, at + CHUNK)
        normed, delta = normed_ref[:, c], delta_ref[:, c]
        modifiers = nn(blocks, ww_ref[:, c])
        for j, ref in enumerate((None, xk_ref, xv_ref, xr_ref, xg_ref)):
            modifier = modifiers[j * length : (j + 1) * length, :]
            mixed = (normed + delta * (rows_ref[MIX + 1 + j : MIX + 2 + j, c] + modifier)).astype(BF16)
            if ref is None:
                decay_in = decay_in + nt(mixed, fn_ref[:, c])
            else:
                ref[:, c] = mixed
    decay_mid = jnp.tanh(decay_in)
    dm_ref[...] = decay_mid
    w = -jnp.exp(own_ref[0:1, :] + nn(decay_mid, fw_ref[...]))
    w_ref[...] = w
    wait_parts(place_ref, (part0, part1, part2, part3), four_ref, sem)
    r = nn(xr_ref[...], four_ref[:, :own]).astype(BF16)
    k = nn(xk_ref[...], four_ref[:, own : 2 * own]).astype(BF16)
    v = nn(xv_ref[...], four_ref[:, 2 * own : 3 * own]).astype(BF16)
    graw = nn(xg_ref[...], four_ref[:, 3 * own :])
    r_ref[...], k_ref[...], v_ref[...], graw_ref[...] = r, k, v, graw

    ones = ones_ref[...]
    for at in range(0, length, TOKENS):
        one_chunk(
            slice(at, at + TOKENS), r, k, v, w, graw, heads, ones, own_ref, wkv_ref, gated_ref, ends_ref.at[at // TOKENS],
            state_ref,
        )


def one_chunk(c, r, k, v, w, graw, heads, ones, own_ref, wkv_ref, gated_ref, end_ref, state_ref):
    v, w, graw = v[c, :], w[c, :], graw[c, :]
    rf, kf, vf = r[c, :].astype(F32), k[c, :].astype(F32), v.astype(F32)
    length = w.shape[0]
    levels, before, after, total = pyramid(w)
    row, col = iota((length, length), 0), iota((length, length), 1)
    apart = jnp.where(row > col, row ^ col, 0)
    scores = [jnp.zeros((length, length), F32)] * heads
    for half, upper, exponent in levels:
        scaled = jnp.where(upper, rf, kf) * jnp.exp(exponent)
        flat = scaled.astype(BF16)
        here = (apart >= half) & (apart < 2 * half)
        for head, one in enumerate(split_heads(scaled, heads)):
            scores[head] = jnp.where(here, nt(one, flat), scores[head])
    wkv = nn(jnp.concatenate([s.astype(BF16) for s in scores], 1), jnp.concatenate(split_heads(vf, heads), 0))
    state = state_ref[...]
    wkv = wkv + nt(rf * jnp.exp(before), state) + head_sum(rf * own_ref[1:2, :] * kf, ones) * vf
    wkv_ref[c, :] = wkv
    state = state * jnp.exp(total[0:1, :]) + tn(v, kf * jnp.exp(after)) * ones.astype(F32)
    state_ref[...] = state
    end_ref[...] = compact(state)

    center = wkv - head_sum(wkv, ones) / HEAD
    variance = head_sum(center * center, ones) / HEAD
    grouped = center * lax.rsqrt(variance + GROUP_EPSILON) * own_ref[2:3, :] + own_ref[3:4, :]
    gated_ref[c, :] = (grouped * graw * jax.nn.sigmoid(graw)).astype(BF16)


def state_cotangent(place_ref, mine_ref, other_ref, own):
    if mine_ref.dtype == F32:
        return mine_ref[0]
    tile = pl.num_programs(0) - 1 - pl.program_id(0)
    is_mine = tile // (pl.num_programs(0) // 2) == place_ref[1]
    wide = 2 * own
    parts = []
    for at in range(0, mine_ref.shape[2], wide):
        q = pl.ds(pl.multiple_of(place_ref[1] * own + at, own), own)
        parts.append(jnp.where(is_mine, mine_ref[0, :, q].astype(F32), other_ref[0, :, q].astype(F32)))
    both = jnp.concatenate(parts, 0)
    return both[:HEAD] + both[HEAD:]


def wkv_backward(
    place_ref, d_ref, r_ref, k_ref, v_ref, w_ref, graw_ref, wkv_ref, dm_ref, w_out_ref, own_ref, ones_ref, sums_ref,
    start_ref, ends_ref, adj_ref, *refs,
):
    own_sums_ref, decay_up_ref, dr_ref, dk_ref, dv_ref, dg_ref, dpre_ref, state_ref = refs[-8:]
    step = pl.program_id(0)
    length, own = r_ref.shape
    heads = own // HEAD
    ones = ones_ref[...]

    @pl.when(step == 0)
    def _():
        for ref in (state_ref, own_sums_ref, decay_up_ref):
            ref[...] = jnp.zeros_like(ref)

    reward, gain, bias = own_ref[1:2, :], own_ref[2:3, :], own_ref[3:4, :]
    wkv, graw, d_gated = wkv_ref[...], graw_ref[...], nt(d_ref[...], w_out_ref[...])
    center = wkv - head_sum(wkv, ones) / HEAD
    scale = lax.rsqrt(head_sum(center * center, ones) / HEAD + GROUP_EPSILON)
    normed = center * scale
    sigma = jax.nn.sigmoid(graw)
    d_grouped = d_gated * graw * sigma
    dg_ref[...] = (d_gated * (normed * gain + bias) * sigma * (1.0 + graw * (1.0 - sigma))).astype(BF16)
    d_normed = d_grouped * gain
    do = scale * (d_normed - head_sum(d_normed, ones) / HEAD - normed * (head_sum(d_normed * normed, ones) / HEAD))

    rb, kb, vb, dob = r_ref[...], k_ref[...], v_ref[...], do.astype(BF16)
    r, k, v, w = rb.astype(F32), kb.astype(F32), vb.astype(F32), w_ref[...]
    levels, before, after, total = pyramid(w)
    same = ones.astype(F32)
    d_state = state_ref[...] + spread(state_cotangent(place_ref, adj_ref, refs[0], own), same)
    state = spread(jnp.where(step == pl.num_programs(0) - 1, start_ref[...], ends_ref[0]), same)
    d_flat, flat = d_state.astype(BF16), state.astype(BF16)
    from_start, to_end, decay = jnp.exp(before), jnp.exp(after), jnp.exp(total[0:1, :])
    dr = from_start * nn(dob, flat)
    dk = to_end * nn(vb, d_flat)
    dv = nt(k * to_end, d_flat)
    through = [r * dr, k * dk]
    state_ref[...] = d_state * decay + tn(dob, r * from_start) * same
    whole = decay * jnp.sum(state * d_state, 0, keepdims=True)

    row, col = iota((length, length), 0), iota((length, length), 1)
    apart = row ^ col
    do_heads, v_heads = split_heads(do, heads), split_heads(v, heads)
    d_scores = [
        jnp.where(row > col, nt(do_heads[h], vb), jnp.where(row < col, nt(v_heads[h], dob), 0.0)).astype(BF16)
        for h in range(heads)
    ]
    scores = [jnp.zeros((length, length), F32)] * heads
    for half, upper, exponent in levels:
        factor = jnp.exp(exponent)
        scaled = jnp.where(upper, r, k) * factor
        mine = split_heads(scaled, heads)
        here = (apart >= half) & (apart < 2 * half)
        late = here & (row < col)
        for h in range(heads):
            scores[h] = jnp.where(late, nt(mine[h], scaled), scores[h])
        pulled = nn(
            jnp.concatenate([jnp.where(here, d, 0.0).astype(BF16) for d in d_scores], 1), jnp.concatenate(mine, 0)
        )
        if half > 1:
            through.append(scaled * pulled)
        pulled = pulled * factor
        dr = dr + jnp.where(upper, pulled, 0.0)
        dk = dk + jnp.where(upper, 0.0, pulled)
    dv = dv + nn(jnp.concatenate([s.astype(BF16) for s in scores], 1), jnp.concatenate(do_heads, 0))
    met = head_sum(v * do, ones)
    dr = dr + reward * k * met
    dk = dk + reward * r * met
    dv = dv + head_sum(r * reward * k, ones) * do
    d_log = whole + nn(sums_ref[...], jnp.concatenate([q.astype(BF16) for q in through], 0))
    d_pre = d_log * w
    dr_ref[...], dk_ref[...], dv_ref[...] = dr.astype(BF16), dk.astype(BF16), dv.astype(BF16)
    dpre_ref[...] = d_pre
    decay_up_ref[...] += tn(dm_ref[...], d_pre)
    for i, part in enumerate((d_pre, r * k * met, d_grouped * normed, d_grouped)):
        own_sums_ref[8 * i : 8 * i + 8, :] += fold(part)


def sum_table(length):
    row, col = np.arange(length)[:, None], np.arange(length)[None, :]
    tables = [col > row, col < row]
    half = 2
    while half < length:
        inside = (row // half) == (col // half)
        upper = (row // half) % 2 == 1
        tables.append(inside & np.where(upper, col > row, col < row))
        half *= 2
    return jnp.asarray(np.concatenate(tables, 1), BF16)


def mix_backward(rank, halves, *refs):
    (
        place_ref, x_ref, edge_ref, rows_ref, lm_ref, dm_ref, dr_ref, dk_ref, dv_ref, dg_ref, dpre_ref,
        wn_ref, ww_ref, fn_ref, fw_ref, more_ref, part0, part1, part2, part3,
    ) = refs[:20]
    packed_ref = refs[-13 - halves]
    outs = refs[-12 - halves : -12]
    (
        row_sums_ref, up_ref, down_ref, decay_down_ref, dx_ref, carry_ref, sum_ref, coef_ref, normed_ref, delta_ref,
        four_ref, sem,
    ) = refs[-12:]
    step = pl.program_id(0)
    from_first = pl.num_programs(0) - 1 - step
    length, width = x_ref.shape

    @pl.when(step == 0)
    def _():
        load_parts(place_ref, (part0, part1, part2, part3), four_ref, sem)
        for ref in (carry_ref, row_sums_ref, up_ref, down_ref, decay_down_ref):
            ref[...] = jnp.zeros_like(ref)

    own = dr_ref.shape[1]
    mean, scale = row_stats(x_ref)
    edge = edge_ref.shape[0]
    edge_mean, edge_scale = row_stats(edge_ref)
    middle, decay_mid = lm_ref[...], dm_ref[...]
    blocks = rank_blocks(middle, rank)
    d_pre = dpre_ref[...]
    d_decay = (nt(d_pre, fw_ref[...]) * (1.0 - decay_mid * decay_mid)).astype(BF16)
    sources = ((d_decay, None), (dk_ref[...], own), (dv_ref[...], 2 * own), (dr_ref[...], 0), (dg_ref[...], 3 * own))
    first = iota((length, CHUNK), 0) == 0
    last = iota((length, CHUNK), 0) == length - 1
    d_mid = jnp.zeros((5 * length, wn_ref.shape[0]), F32)
    wait_parts(place_ref, (part0, part1, part2, part3), four_ref, sem)
    for at in range(0, width, CHUNK):
        c = slice(at, at + CHUNK)
        gain, bias = rows_ref[GAIN : GAIN + 1, c], rows_ref[BIAS : BIAS + 1, c]
        normed = (x_ref[:, c].astype(F32) - mean) * scale * gain + bias
        edge_normed = (edge_ref[:, c].astype(F32) - edge_mean) * edge_scale * gain + bias
        before = jnp.where(from_first == 0, rows_ref[FIRST : FIRST + 1, c], edge_normed[edge - 1 : edge, :])
        delta = jnp.where(first, before, pltpu.roll(normed, 1, 0)) - normed
        normed_ref[:, c] = normed
        delta_ref[:, c] = delta
        modifiers = nn(blocks, ww_ref[:, c])
        total = jnp.zeros_like(normed)
        by_coef = jnp.zeros_like(normed)
        d_mods = []
        for j, (d, begin) in enumerate(sources):
            d_mixed = nt(d, four_ref[c, begin : begin + own]) if j else nn(d, fn_ref[:, c])
            coef = rows_ref[MIX + 1 + j : MIX + 2 + j, c] + modifiers[j * length : (j + 1) * length, :]
            if j == 0:
                decay_down_ref[:, c] += tn(d_decay, normed + delta * coef)
            d_mod = delta * d_mixed
            row_sums_ref[8 * (MIX + 1 + j) : 8 * (MIX + 2 + j), c] += fold(d_mod)
            d_mods.append(d_mod.astype(BF16))
            total = total + d_mixed
            by_coef = by_coef + d_mixed * coef
        d_mods = jnp.concatenate(d_mods, 0)
        up_ref[:, c] += tn(blocks, d_mods)
        d_mid = d_mid + nt(d_mods, ww_ref[:, c])
        sum_ref[:, c] = total
        coef_ref[:, c] = by_coef
    lane = iota(middle.shape, 1) // rank
    d_low = jnp.zeros_like(middle)
    for j in range(5):
        d_low = jnp.where(lane == j, d_mid[j * length : (j + 1) * length, :], d_low)
    d_low = (d_low * (1.0 - middle * middle)).astype(BF16)
    sum_g = jnp.zeros((length, CHUNK), F32)
    sum_gn = jnp.zeros((length, CHUNK), F32)
    for at in range(0, width, CHUNK):
        c = slice(at, at + CHUNK)
        normed, delta = normed_ref[:, c], delta_ref[:, c]
        mix = rows_ref[MIX : MIX + 1, c]
        d_in = nn(d_low, wn_ref[:, c])
        down_ref[:, c] += tn(d_low, normed + delta * mix)
        row_sums_ref[8 * MIX : 8 * MIX + 8, c] += fold(delta * d_in)
        d_delta = coef_ref[:, c] + d_in * mix
        above = jnp.where(last, carry_ref[0:1, c], pltpu.roll(d_delta, length - 1, 0))
        carry_ref[0:1, c] = d_delta[0:1, :]
        d_normed = sum_ref[:, c] + d_in - d_delta + above
        unit = (x_ref[:, c].astype(F32) - mean) * scale
        row_sums_ref[8 * GAIN : 8 * GAIN + 8, c] += fold(d_normed * unit)
        row_sums_ref[8 * BIAS : 8 * BIAS + 8, c] += fold(d_normed)
        g = d_normed * rows_ref[GAIN : GAIN + 1, c]
        sum_g = sum_g + g
        sum_gn = sum_gn + g * unit
        sum_ref[:, c] = g
    mean_g = jnp.sum(sum_g, 1, keepdims=True) / width
    mean_gn = jnp.sum(sum_gn, 1, keepdims=True) / width
    for at in range(0, width, CHUNK):
        c = slice(at, at + CHUNK)
        unit = (x_ref[:, c].astype(F32) - mean) * scale
        dx_ref[:, c] = (scale * (sum_ref[:, c] - mean_g - unit * mean_gn)).astype(BF16)
    store_half(place_ref, dx_ref, outs, from_first)

    @pl.when(step == pl.num_programs(0) - 1)
    def _():
        at = 16
        packed_ref[0:at, :] = jnp.zeros((at, width), BF16)
        for i in range(8):
            packed_ref[i : i + 1, :] = jnp.sum(row_sums_ref[8 * i : 8 * i + 8, :], 0, keepdims=True).astype(BF16)
        more = more_ref.shape[0]
        decays = packed_ref.shape[0] - at - 10 * rank - more
        for ref, size in ((down_ref, 5 * rank), (up_ref, 5 * rank), (decay_down_ref, decays), (more_ref, more)):
            packed_ref[at : at + size, :] = ref[0:size, :].astype(BF16)
            at += size


def whole(a):
    return pl.BlockSpec(a.shape, lambda t: (0,) * a.ndim)


def params(**more):
    return pltpu.CompilerParams(
        dimension_semantics=("arbitrary",), vmem_limit_bytes=VMEM, **more
    )


def light():
    return pl.CostEstimate(flops=0, bytes_accessed=0, transcendentals=0)


def pinned(pins):
    return [pl.BlockSpec(memory_space=pl.ANY)] * len(pins)


def part_specs(parts):
    return [pl.BlockSpec(memory_space=pltpu.SMEM)] + [pl.BlockSpec(memory_space=pl.ANY)] * len(parts)


def part_scratch(parts):
    rows, columns = parts[0].shape
    return [pltpu.VMEM((len(parts) * rows, columns), BF16), pltpu.SemaphoreType.DMA((len(parts),))]


def call_forward(rank, length, x, rows, own, wn, ww, fn, fw, ones, start, place, parts, pins):
    tokens, width = x.shape
    cw = own.shape[1]
    count = tokens // length
    tile = lambda n: pl.BlockSpec((length, n), lambda t: (t, 0))
    shape = lambda n, dtype: jax.ShapeDtypeStruct((tokens, n), dtype)
    fixed = (rows, own, wn, ww, fn, fw, ones, start)
    return pl.pallas_call(
        lambda *refs: mix_forward(rank, *refs),
        grid=(count,),
        in_specs=[tile(width)] + [whole(a) for a in fixed] + part_specs(parts) + pinned(pins),
        out_specs=[tile(cw)] + [tile(width)] * 4 + [tile(cw)] * 6 + [tile(wn.shape[0]), tile(fn.shape[0])]
        + [pl.BlockSpec((length // TOKENS, HEAD, cw), lambda t: (t, 0, 0))],
        out_shape=[shape(cw, BF16)] + [shape(width, BF16)] * 4 + [shape(cw, BF16)] * 3 + [shape(cw, F32)] * 3
        + [shape(wn.shape[0], F32), shape(fn.shape[0], F32), jax.ShapeDtypeStruct((tokens // TOKENS, HEAD, cw), F32)],
        scratch_shapes=[
            pltpu.VMEM((length, width), F32), pltpu.VMEM((length, width), F32), pltpu.VMEM((8, width), F32),
            pltpu.VMEM((cw, cw), F32),
        ]
        + part_scratch(parts),
        compiler_params=params(),
        cost_estimate=light(),
        name="mix_forward",
    )(x, *fixed, place, *parts, *pins)


def two_halves(tokens, width, length, seqs, backward=False):
    half = tokens // length // 2
    order = (lambda t: tokens // length - 1 - t) if backward else (lambda t: t)
    if seqs != 2:
        return [pl.BlockSpec((length, width), lambda t, place: (order(t), 0))], [jax.ShapeDtypeStruct((tokens, width), BF16)]
    mine = lambda t, place: (jnp.clip(order(t) - place[1] * half, 0, half - 1), 0)
    other = lambda t, place: (jnp.clip(order(t) - (1 - place[1]) * half, 0, half - 1), 0)
    return (
        [pl.BlockSpec((length, width), mine), pl.BlockSpec((length, width), other)],
        [jax.ShapeDtypeStruct((tokens // 2, width), BF16)] * 2,
    )


def store_half(place_ref, value_ref, outs, tile=None):
    if len(outs) == 1:
        outs[0][...] = value_ref[...]
        return
    tile = pl.program_id(0) if tile is None else tile
    is_mine = tile // (pl.num_programs(0) // 2) == place_ref[1]

    @pl.when(is_mine)
    def _():
        outs[0][...] = value_ref[...]

    @pl.when(jnp.logical_not(is_mine))
    def _():
        outs[1][...] = value_ref[...]


def ffn_forward(halves, place_ref, x_ref, edge_ref, rows_ref, w_all, *refs):
    key_ref, recept_ref, hidden_ref, squared_ref = refs[-7 - halves : -3 - halves]
    outs = refs[-3 - halves : -3]
    w_ref, value_ref, sem = refs[-3:]
    length, width = x_ref.shape
    units = hidden_ref.shape[1]
    edge = edge_ref.shape[0]
    load = pltpu.make_async_copy(w_all, w_ref, sem)

    @pl.when(pl.program_id(0) == 0)
    def _():
        load.start()

    first = iota((length, CHUNK), 0) == 0
    for at in range(0, width, CHUNK):
        c = slice(at, at + CHUNK)
        normed = x_ref[:, c].astype(F32)
        before = jnp.where(pl.program_id(0) == 0, rows_ref[2:3, c], edge_ref[edge - 1 : edge, c].astype(F32))
        delta = jnp.where(first, before, pltpu.roll(normed, 1, 0)) - normed
        key_ref[:, c] = (normed + delta * rows_ref[3:4, c]).astype(BF16)
        recept_ref[:, c] = (normed + delta * rows_ref[4:5, c]).astype(BF16)

    @pl.when(pl.program_id(0) == 0)
    def _():
        load.wait()

    hidden = jnp.maximum(nn(key_ref[...], w_ref[:, :units]), 0.0)
    hidden_ref[...] = hidden
    squared = (hidden * hidden).astype(BF16)
    squared_ref[...] = squared
    for at in range(0, width, CHUNK):
        c = slice(at, at + CHUNK)
        value_ref[:, c] = nt(squared, w_ref[c, units:]).astype(BF16)
    store_half(place_ref, value_ref, outs)


def call_ffn_forward(x, rows, w, place, seqs, pins):
    tokens, width = x.shape
    length, edge = 256, 16
    units = w.shape[1] // 2
    tile = lambda n: pl.BlockSpec((length, n), lambda t, place: (t, 0))
    shape = lambda n, dtype: jax.ShapeDtypeStruct((tokens, n), dtype)
    specs, shapes = two_halves(tokens, width, length, seqs)
    return pl.pallas_call(
        lambda *refs: ffn_forward(len(specs), *refs),
        grid_spec=pltpu.PrefetchScalarGridSpec(
            num_scalar_prefetch=1,
            grid=(tokens // length,),
            in_specs=[
                tile(width),
                pl.BlockSpec((edge, width), lambda t, place: (jnp.maximum(t * (length // edge) - 1, 0), 0)),
                pl.BlockSpec(rows.shape, lambda t, place: (0, 0)),
            ]
            + pinned([w]) + pinned(pins),
            out_specs=[tile(width)] * 2 + [tile(units)] * 2 + specs,
            scratch_shapes=[
                pltpu.VMEM(w.shape, BF16), pltpu.VMEM((length, width), BF16), pltpu.SemaphoreType.DMA,
            ],
        ),
        out_shape=[shape(width, BF16)] * 2 + [shape(units, F32), shape(units, BF16)] + shapes,
        compiler_params=params(),
        cost_estimate=light(),
        name="ffn_forward",
    )(place, x, x, rows, w, *pins)


def call_ffn_gate(recept, cot_mine, cot_other, gate, place, pins):
    tokens, width = recept.shape
    length = 256
    half = gate.shape[1]
    step = min(CHUNK, half)
    rows = 128
    tiles, per = tokens // length, length // rows
    split = cot_mine.shape[0] < tiles * per

    def kernel(place_ref, recept_ref, mine_ref, other_ref, gate_ref, *refs):
        recept = recept_ref[...]
        is_mine = pl.program_id(0) // (tiles // 2) == place_ref[1]
        for at in range(0, half, step):
            c = slice(at, at + step)
            gate = jax.nn.sigmoid(nn(recept, gate_ref[:, c]))
            for i in range(per):
                r = slice(i * rows, (i + 1) * rows)
                cot = jnp.where(is_mine, mine_ref[i, :, c].astype(F32), other_ref[i, :, c].astype(F32))
                refs[-1][r, c] = (cot * gate[r, :]).astype(BF16)

    column = (lambda place: place[1]) if half < width else (lambda place: 0)

    def cot_spec(core):
        if not split:
            return pl.BlockSpec((per, rows, half), lambda t, place: (t, 0, column(place)))
        at = lambda t, place: jnp.clip(t - core(place) * (tiles // 2), 0, tiles // 2 - 1)
        return pl.BlockSpec((per, rows, half), lambda t, place: (at(t, place), 0, column(place)))

    return pl.pallas_call(
        kernel,
        grid_spec=pltpu.PrefetchScalarGridSpec(
            num_scalar_prefetch=1,
            grid=(tiles,),
            in_specs=[
                pl.BlockSpec((length, width), lambda t, place: (t, 0)),
                cot_spec(lambda place: place[1]), cot_spec(lambda place: 1 - place[1]),
                pl.BlockSpec(gate.shape, lambda t, place: (0, 0), pipeline_mode=pl.Buffered(1)),
            ]
            + pinned(pins),
            out_specs=pl.BlockSpec((length, half), lambda t, place: (t, 0)),
        ),
        out_shape=jax.ShapeDtypeStruct((tokens, half), BF16),
        compiler_params=params(),
        cost_estimate=light(),
        name="ffn_gate",
    )(place, recept, cot_mine, cot_other, gate, *pins)


def ffn_backward(halves, place_ref, mine_ref, other_ref, hidden_ref, w_all, *refs):
    d_hidden_ref = refs[-5 - halves]
    outs = refs[-4 - halves : -4]
    w_ref, d_values_ref, value_ref, sem = refs[-4:]
    width = d_values_ref.shape[1]
    half = mine_ref.shape[1]
    units = hidden_ref.shape[1]
    load = pltpu.make_async_copy(w_all, w_ref, sem)

    @pl.when(pl.program_id(0) == 0)
    def _():
        load.start()

    cores = ((mine_ref, place_ref[1]), (other_ref, 1 - place_ref[1])) if half < width else ((mine_ref, 0),)
    for ref, core in cores:
        d_values_ref[:, pl.ds(pl.multiple_of(core * half, half), half)] = ref[...]

    @pl.when(pl.program_id(0) == 0)
    def _():
        load.wait()

    d_hidden = (nn(d_values_ref[...], w_ref[:, units:]) * 2.0 * hidden_ref[...]).astype(BF16)
    d_hidden_ref[...] = d_hidden
    for at in range(0, width, CHUNK):
        c = slice(at, at + CHUNK)
        value_ref[:, c] = nt(d_hidden, w_ref[c, :units]).astype(BF16)
    store_half(place_ref, value_ref, outs)


def call_ffn_backward(mine, other, hidden, w, place, seqs, pins):
    tokens, half = mine.shape
    width = w.shape[0]
    length = 256
    units = hidden.shape[1]
    tile = lambda n: pl.BlockSpec((length, n), lambda t, place: (t, 0))
    shape = lambda n: jax.ShapeDtypeStruct((tokens, n), BF16)
    specs, shapes = two_halves(tokens, width, length, seqs)
    return pl.pallas_call(
        lambda *refs: ffn_backward(len(specs), *refs),
        grid_spec=pltpu.PrefetchScalarGridSpec(
            num_scalar_prefetch=1,
            grid=(tokens // length,),
            in_specs=[tile(half), tile(half), tile(units)] + pinned([w]) + pinned(pins),
            out_specs=[tile(units)] + specs,
            scratch_shapes=[
                pltpu.VMEM(w.shape, BF16), pltpu.VMEM((length, width), BF16), pltpu.VMEM((length, width), BF16),
                pltpu.SemaphoreType.DMA,
            ],
        ),
        out_shape=[shape(units)] + shapes,
        compiler_params=params(),
        cost_estimate=light(),
        name="ffn_backward",
    )(place, mine, other, hidden, w, *pins)


def call_grad(x, d, pins):
    tokens, width = x.shape
    units = d.shape[1]
    columns = 512 if tokens <= 1024 else 256

    def kernel(x_ref, d_ref, *refs):
        refs[-1][...] = tn(x_ref[...], d_ref[...]).astype(BF16)

    return pl.pallas_call(
        kernel,
        grid=(width // columns,),
        in_specs=[
            pl.BlockSpec((tokens, columns), lambda t: (0, t)),
            pl.BlockSpec(d.shape, lambda t: (0, 0), pipeline_mode=pl.Buffered(1)),
        ]
        + pinned(pins),
        out_specs=pl.BlockSpec((columns, units), lambda t: (t, 0)),
        out_shape=jax.ShapeDtypeStruct((width, units), BF16),
        compiler_params=params(),
        cost_estimate=light(),
        name="grad",
    )(x, d, *pins)


def call_grad_halves(place, mine, other, d):
    tokens, half = mine.shape
    units = d.shape[1]
    columns = 512
    per = half // columns

    def kernel(place_ref, mine_ref, other_ref, d_ref, out_ref):
        @pl.when(pl.program_id(0) < per)
        def _():
            out_ref[...] = tn(mine_ref[...], d_ref[...]).astype(BF16)

        @pl.when(pl.program_id(0) >= per)
        def _():
            out_ref[...] = tn(other_ref[...], d_ref[...]).astype(BF16)

    def to(t, place):
        return (jnp.where(t < per, place[1] * per + t, (1 - place[1]) * per + t - per), 0)

    return pl.pallas_call(
        kernel,
        grid_spec=pltpu.PrefetchScalarGridSpec(
            num_scalar_prefetch=1,
            grid=(2 * per,),
            in_specs=[
                pl.BlockSpec((tokens, columns), lambda t, place: (0, jnp.minimum(t, per - 1))),
                pl.BlockSpec((tokens, columns), lambda t, place: (0, jnp.maximum(t - per, 0))),
                pl.BlockSpec(d.shape, lambda t, place: (0, 0), pipeline_mode=pl.Buffered(1)),
            ],
            out_specs=pl.BlockSpec((columns, units), to),
        ),
        out_shape=jax.ShapeDtypeStruct((2 * half, units), BF16),
        compiler_params=params(),
        cost_estimate=light(),
        name="grad_halves",
    )(place, mine, other, d)


def call_grads(xs, ds, gated, d_att, segs, pins):
    tokens, width = d_att.shape
    cw = gated.shape[1]
    rows, count = width // segs, len(xs)
    columns = 512 if tokens <= 1024 else 128
    per, cut = rows // columns, cw // segs

    def kernel(*refs):
        x_refs, d_refs, gated_ref, att_ref, out_ref = refs[:count], refs[count : 2 * count], refs[-3 - len(pins)], refs[-2 - len(pins)], refs[-1]
        s, at = pl.program_id(0) // per, pl.program_id(0) % per
        for j in range(count):
            out_ref[s, j, pl.ds(pl.multiple_of(at * columns, columns), columns), :] = tn(
                x_refs[j][...], d_refs[j][...]
            ).astype(BF16)
        result = tn(gated_ref[...], att_ref[...]).astype(BF16)
        each = columns // cw
        for i in range(each):
            to = pl.multiple_of((pl.program_id(0) * each + i) * cut, cut)
            for m in range(segs):
                out_ref[m, count, pl.ds(to, cut), :] = result[m * cut : (m + 1) * cut, i * cw : (i + 1) * cw]

    block = pl.BlockSpec((tokens, columns), lambda t: (0, t))
    fixed = pl.BlockSpec((tokens, cw), lambda t: (0, 0), pipeline_mode=pl.Buffered(1))
    shape = (segs, count + 1, rows, cw)
    return pl.pallas_call(
        kernel,
        grid=(width // columns,),
        in_specs=[block] * count + [fixed] * count + [fixed, block] + pinned(pins),
        out_specs=pl.BlockSpec(shape, lambda t: (0, 0, 0, 0)),
        out_shape=jax.ShapeDtypeStruct(shape, BF16),
        compiler_params=params(),
        cost_estimate=light(),
        name="grads",
    )(*xs, *ds, gated, d_att, *pins)


def call_ffn_norm(x, blocks, rows, pins):
    length, width = x.shape
    count = blocks.shape[0]

    def kernel(x_ref, blocks_ref, rows_ref, *refs):
        sum_ref, unit_ref, scale_ref, normed_ref, low_ref = refs[-5:]
        lanes = 128
        total = jnp.zeros((length, lanes), F32)
        for at in range(0, width, lanes):
            c = slice(at, at + lanes)
            value = x_ref[:, c].astype(F32)
            for i in range(count):
                value = value + blocks_ref[i, :, c].astype(F32)
            sum_ref[:, c] = value
            total = total + value
        mean = jnp.sum(total, 1, keepdims=True) / width
        total = jnp.zeros((length, lanes), F32)
        for at in range(0, width, lanes):
            center = sum_ref[:, at : at + lanes] - mean
            total = total + center * center
        scale = lax.rsqrt(jnp.sum(total, 1, keepdims=True) / width + LAYER_EPSILON)
        scale_ref[...] = jnp.broadcast_to(scale, scale_ref.shape)
        for at in range(0, width, lanes):
            c = slice(at, at + lanes)
            unit = (sum_ref[:, c] - mean) * scale
            unit_ref[:, c] = unit
            normed = unit * rows_ref[0:1, c] + rows_ref[1:2, c]
            normed_ref[:, c] = normed
            low_ref[:, c] = normed.astype(BF16)

    shape = lambda n, dtype: jax.ShapeDtypeStruct((length, n), dtype)
    return pl.pallas_call(
        kernel,
        grid=(1,),
        in_specs=[whole(x), whole(blocks), whole(rows)] + pinned(pins),
        out_specs=[pl.BlockSpec((length, n), lambda t: (0, 0)) for n in (width, width, 128, width, width)],
        out_shape=[shape(width, F32), shape(width, F32), shape(128, F32), shape(width, F32), shape(width, BF16)],
        compiler_params=params(),
        cost_estimate=light(),
        name="ffn_norm",
    )(x, blocks, rows, *pins)


def call_ffn_local(place, recept_in, blocks, cot, residual, gate_mine, gate_other, group, pins):
    length, width = recept_in.shape
    count, half = blocks.shape[0], gate_mine.shape[1]
    cw = width // group
    step = min(CHUNK, half)

    def kernel(place_ref, recept_ref, blocks_ref, cot_ref, residual_ref, mine_ref, other_ref, *refs):
        out_ref, cut_ref, d_ref, gate_ref = refs[-4:]
        recept = recept_ref[...]
        cores = ((mine_ref, place_ref[1]), (other_ref, 1 - place_ref[1])) if half < width else ((mine_ref, 0),)
        for ref, core in cores:
            for at in range(0, half, step):
                c = pl.ds(pl.multiple_of(core * half + at, step), step)
                gate = jax.nn.sigmoid(nn(recept, ref[:, at : at + step]))
                values = sum(blocks_ref[i, :, c].astype(F32) for i in range(count))
                out_ref[:, c] = (residual_ref[:, c] + gate * values).astype(BF16)
                gate_ref[:, c] = (cot_ref[:, c].astype(F32) * values * gate * (1.0 - gate)).astype(BF16)
        for i in range(group):
            cut_ref[i] = gate_ref[:, i * cw : (i + 1) * cw]
        for at in range(0, width, CHUNK):
            c = slice(at, at + CHUNK)
            d = jnp.zeros((length, CHUNK), F32)
            for ref, core in cores:
                d = d + nt(gate_ref[:, pl.ds(pl.multiple_of(core * half, half), half)], ref[c, :])
            d_ref[:, c] = d

    fixed = lambda a: pl.BlockSpec(a.shape, lambda t, place: (0,) * a.ndim)
    shapes = [(length, width), (group, length, cw), (length, width)]
    return pl.pallas_call(
        kernel,
        grid_spec=pltpu.PrefetchScalarGridSpec(
            num_scalar_prefetch=1,
            grid=(1,),
            in_specs=[fixed(a) for a in (recept_in, blocks, cot, residual, gate_mine, gate_other)] + pinned(pins),
            out_specs=[pl.BlockSpec(s, lambda t, place, n=len(s): (0,) * n) for s in shapes],
            scratch_shapes=[pltpu.VMEM((length, width), BF16)],
        ),
        out_shape=[jax.ShapeDtypeStruct(s, dtype) for s, dtype in zip(shapes, (BF16, BF16, F32))],
        compiler_params=params(),
        cost_estimate=light(),
        name="ffn_local",
    )(place, recept_in, blocks, cot, residual, gate_mine, gate_other, *pins)


def call_out(place, gated, own, parts, sender, seqs, pins):
    tokens, cw = gated.shape
    width = own.shape[1]
    length = 256
    specs, shapes = two_halves(tokens, width, length, seqs)

    def kernel(place_ref, gated_ref, own_ref, *refs):
        w_ref, value_ref = refs[-2:]

        @pl.when(pl.program_id(0) == 0)
        def _():
            received = refs[0][...]
            for ref in refs[1 : len(parts)]:
                received = received + ref[...]
            w_ref[...] = jnp.where(place_ref[2] == 1, own_ref[...], received)

        for at in range(0, width, CHUNK):
            c = slice(at, at + CHUNK)
            value_ref[:, c] = nn(gated_ref[...], w_ref[:, c]).astype(BF16)
        store_half(place_ref, value_ref, refs[-2 - len(specs) : -2])

    fixed = lambda a: pl.BlockSpec(a.shape, lambda t, place: (0, 0))

    return pl.pallas_call(
        kernel,
        grid_spec=pltpu.PrefetchScalarGridSpec(
            num_scalar_prefetch=1,
            grid=(tokens // length,),
            in_specs=[pl.BlockSpec((length, cw), lambda t, place: (t, 0))] + [fixed(a) for a in (own, *parts)]
            + pinned(pins),
            out_specs=specs + [pl.BlockSpec((cw, width), lambda t, place: (0, 0))],
            scratch_shapes=[pltpu.VMEM((length, width), BF16)],
        ),
        out_shape=shapes + [jax.ShapeDtypeStruct((cw, width), BF16)],
        compiler_params=params(),
        cost_estimate=light(),
        name="out_projection",
    )(jnp.concatenate([place, sender.reshape(1)]), gated, own, *parts, *pins)


def call_add(mine, other, pins):
    rows, width = mine.shape
    length = 256

    def kernel(a_ref, b_ref, *refs):
        refs[-1][...] = (a_ref[...].astype(F32) + b_ref[...].astype(F32)).astype(BF16)

    tile = pl.BlockSpec((length, width), lambda t: (t, 0))
    return pl.pallas_call(
        kernel,
        grid=(rows // length,),
        in_specs=[tile, tile] + pinned(pins),
        out_specs=tile,
        out_shape=jax.ShapeDtypeStruct((rows, width), BF16),
        compiler_params=params(),
        cost_estimate=light(),
        name="add",
    )(mine, other, *pins)


def call_wkv_backward(
    length, d, r, k, v, w, graw, wkv, dm, w_out, own, ones, sums, start, ends, adjoints, place, pins
):
    tokens, cw = r.shape
    count = tokens // length
    tile = lambda n: pl.BlockSpec((length, n), lambda t, place: (count - 1 - t, 0))
    fixed = lambda a: pl.BlockSpec(a.shape, lambda t, place: (0, 0))
    shape = lambda dtype: jax.ShapeDtypeStruct((tokens, cw), dtype)
    wide = dm.shape[1]

    def folded(a, core):
        rows = a.shape[1] - length
        at = lambda t, place: jnp.clip(count - 1 - t - core(place) * (count // 2), 0, count // 2 - 1)
        return pl.BlockSpec((1, rows, a.shape[2]), lambda t, place: (at(t, place), length // rows, 0))

    if len(adjoints) == 2:
        states = [folded(adjoints[0], lambda place: place[1]), folded(adjoints[1], lambda place: 1 - place[1])]
    else:
        states = [pl.BlockSpec((1, HEAD, cw), lambda t, place: (count - 1 - t, 0, 0))]
    return pl.pallas_call(
        wkv_backward,
        grid_spec=pltpu.PrefetchScalarGridSpec(
            num_scalar_prefetch=1,
            grid=(count,),
            in_specs=[tile(d.shape[1])] + [tile(cw)] * 6 + [tile(wide)]
            + [fixed(a) for a in (w_out, own, ones, sums, start)]
            + [pl.BlockSpec((1, HEAD, cw), lambda t, place: (jnp.maximum(count - 2 - t, 0), 0, 0))]
            + states + pinned(pins),
            out_specs=[pl.BlockSpec((32, cw), lambda t, place: (0, 0)), pl.BlockSpec((wide, cw), lambda t, place: (0, 0))]
            + [tile(cw)] * 5,
            scratch_shapes=[pltpu.VMEM((cw, cw), F32)],
        ),
        out_shape=[jax.ShapeDtypeStruct((32, cw), F32), jax.ShapeDtypeStruct((wide, cw), F32)]
        + [shape(BF16)] * 4 + [shape(F32)],
        compiler_params=params(),
        cost_estimate=light(),
        name="wkv_backward",
    )(place, d, r, k, v, w, graw, wkv, dm, w_out, own, ones, sums, start, ends, *adjoints, *pins)


def call_mix_backward(
    rank, length, x, rows, lm, dm, dr, dk, dv, dg, dpre, wn, ww, fn, fw, more, place, parts, decays, seqs, pins
):
    tokens, width = x.shape
    cw = dr.shape[1]
    count = tokens // length
    edge = 16
    tile = lambda n: pl.BlockSpec((length, n), lambda t, place: (count - 1 - t, 0))
    before = pl.BlockSpec((edge, width), lambda t, place: (jnp.maximum((count - 1 - t) * (length // edge) - 1, 0), 0))
    fixed = lambda a: pl.BlockSpec(a.shape, lambda t, place: (0, 0))
    packed = 16 + 10 * rank + decays + more.shape[0]
    specs, shapes = two_halves(tokens, width, length, seqs, backward=True)
    return pl.pallas_call(
        lambda *refs: mix_backward(rank, len(specs), *refs),
        grid_spec=pltpu.PrefetchScalarGridSpec(
            num_scalar_prefetch=1,
            grid=(count,),
            in_specs=[tile(width), before, fixed(rows), tile(lm.shape[1]), tile(dm.shape[1])] + [tile(cw)] * 5
            + [fixed(a) for a in (wn, ww, fn, fw, more)] + pinned(parts) + pinned(pins),
            out_specs=[pl.BlockSpec((packed, width), lambda t, place: (0, 0))] + specs,
            scratch_shapes=[pltpu.VMEM((n, width), F32) for n in (8 * 8, wn.shape[0], wn.shape[0], fn.shape[0])]
            + [pltpu.VMEM((length, width), BF16), pltpu.VMEM((8, width), F32)]
            + [pltpu.VMEM((length, width), F32)] * 4 + part_scratch(parts),
        ),
        out_shape=[jax.ShapeDtypeStruct((packed, width), BF16)] + shapes,
        compiler_params=params(),
        cost_estimate=light(),
        name="mix_backward",
    )(place, x, x, rows, lm, dm, dr, dk, dv, dg, dpre, wn, ww, fn, fw, more, *parts, *pins)


def gather_group(block):
    return lax.all_gather(block, TP, axis=0, tiled=True)


SWAP = [(0, 1), (1, 0)]


def reduce_halves(mine, other, pins):
    total = call_add(mine, lax.ppermute(other, "seq", SWAP), pins)
    return reduce_chan(total), total


def reduce_chan(total):
    chans = lax.axis_size("chan")
    return lax.all_to_all(total.reshape(chans, -1, total.shape[1]), "chan", 0, 0, tiled=True)


def add_up(blocks):
    return jnp.sum(blocks.astype(F32), 0)


def reduce_group(parts, pins=()):
    if len(parts) == 2:
        return reduce_halves(*parts, pins)
    total = lax.psum_scatter(parts[0], "seq", scatter_dimension=0, tiled=True)
    return reduce_chan(total), total


def after(a, before):
    corner = before[(slice(0, 1),) * before.ndim].reshape((1,) * a.ndim)
    return a + (corner.astype(F32) * 0.0).astype(a.dtype)


def after_all(a, others):
    for other in others:
        a = after(a, other)
    return a


def next_row(row, by):
    count = lax.axis_size(TP)
    return lax.ppermute(row, TP, [(i, i + by) for i in range(count) if 0 <= i + by < count])


def shift_down(values, first_row):
    return jnp.concatenate([first_row, values[:-1]], 0)


def unit_rows(values):
    center = values - jnp.mean(values, -1, keepdims=True)
    scale = lax.rsqrt(jnp.mean(center * center, -1, keepdims=True) + LAYER_EPSILON)
    return center * scale, scale


def on_device(
    sequence_elements,
    segment_predecessor_entries,
    opening_recurrences,
    first_layernorm_gain,
    first_layernorm_shift_term,
    lag_blend_coefficients,
    lag_narrowing_factor,
    lag_widening_factors,
    fading_exponent_baseline,
    fading_narrowing_factor,
    fading_widening_factor,
    present_reward,
    acceptor_projection,
    address_projection,
    content_projection,
    valve_projection,
    timemix_result_projection,
    subspace_cluster_gain,
    subspace_cluster_shift_term,
    second_layernorm_gain,
    second_layernorm_shift_term,
    feedforward_lag_blends,
    feedforward_address_projection,
    feedforward_acceptor_projection,
    feedforward_content_projection,
    result_adjoint,
    final_recurrence_adjoint,
):
    segs, seqs, chans = lax.axis_size("seg"), lax.axis_size("seq"), lax.axis_size("chan")
    group = seqs * chans
    p = lax.axis_index(TP)
    x = sequence_elements[0]
    length, width = x.shape
    tokens = group * length
    cw = width // group
    heads = cw // HEAD
    rank = lag_widening_factors.shape[1] // 5
    ranks, decays = 5 * rank, fading_widening_factor.shape[1]

    def columns(a, axis=-1):
        return lax.dynamic_slice_in_dim(a, p * cw, cw, axis % a.ndim)

    me, seg = lax.axis_index("seq"), lax.axis_index("seg")
    block = width // (segs * group)
    rows_seg = width // segs
    flips = [[(s, s ^ m) for s in range(segs)] for m in range(segs)]

    def seg_parts(a):
        return [a] + [lax.ppermute(a, "seg", flips[m]) for m in range(1, segs)]

    def own_part(a, axis):
        size = a.shape[axis] // seqs
        return lax.dynamic_slice_in_dim(a, me * size, size, axis)

    def reduce_segs(piece):
        sent = [piece(seg ^ m) for m in range(1, segs)]
        return sum((lax.ppermute(a, "seg", flips[m + 1]).astype(F32) for m, a in enumerate(sent)), piece(seg).astype(F32)), sent

    def reduce_rows(a):
        return lax.psum_scatter(a, "seg", scatter_dimension=0, tiled=True)

    x_all = gather_group(x)
    four = seg_parts(
        jnp.concatenate(
            [columns(a) for a in (acceptor_projection, address_projection, content_projection, valve_projection)], 1
        )
    )
    share = group // segs
    out_rows = after(lax.dynamic_slice_in_dim(timemix_result_projection, (p % share) * cw, cw, 0), four[-1])
    out_parts = [
        lax.ppermute(out_rows, ALL, [((j // share) * group + j, ((j // share) ^ m) * group + j) for j in range(group)])
        for m in range(1, segs)
    ]
    ffn_part = jnp.concatenate([own_part(a, 1) for a in (feedforward_address_projection, feedforward_content_projection)], 1)
    w_ffn = lax.all_gather(after_all(ffn_part, four[1:]), "seg", axis=0, tiled=True)
    cot = after(result_adjoint[0], x_all)
    adjoints = final_recurrence_adjoint[0, 0]
    if seqs == 2:
        adjoints = adjoints.reshape(HEAD, seqs, chans, cw).transpose(2, 0, 1, 3).reshape(chans, HEAD, seqs * cw)
        high = adjoints.astype(BF16)
        adjoints = jnp.concatenate([high, (adjoints - high.astype(F32)).astype(BF16)], 1)
        fold_rows = 2 * HEAD * seqs * cw // width
        adjoints = adjoints.reshape(chans, -1, fold_rows, seqs * cw).transpose(0, 2, 1, 3).reshape(chans, fold_rows, width)
        sent = jnp.concatenate([jnp.broadcast_to(cot[None], (chans, length, width)), adjoints], 1)
        cot_mine = lax.all_to_all(sent, "chan", 0, 0, tiled=True)
        cot_other = lax.ppermute(cot_mine, "seq", SWAP)

        adjoints = (cot_mine, cot_other)
    else:
        cot_mine = cot_other = gather_group(cot).reshape(group, length, width)
        adjoints = (lax.all_to_all(adjoints.reshape(HEAD, group, cw).transpose(1, 0, 2), TP, 0, 0, tiled=True),)

    rows = jnp.concatenate(
        [
            first_layernorm_gain[None], first_layernorm_shift_term[None], lag_blend_coefficients.T,
            segment_predecessor_entries[0, 0][None], fading_exponent_baseline[None], present_reward[None],
            subspace_cluster_gain[None], subspace_cluster_shift_term[None], jnp.zeros((11, width), F32),
        ]
    )
    own = lax.dynamic_slice(rows, (FIRST + 1, p * cw), (8, cw))
    wn, ww, fn = lag_narrowing_factor.T, lag_widening_factors.T, fading_narrowing_factor.T
    fw = columns(fading_widening_factor.T)
    head_of = np.arange(cw) // HEAD
    ones = jnp.asarray(head_of[:, None] == head_of[None, :], BF16)
    start = columns(opening_recurrences[0])
    place = jnp.stack([seg, me]).astype(jnp.int32)

    gated, xk, xv, xr, xg, r, k, v, w, graw, wkv, lm, dm, ends = call_forward(
        rank, 2 * length, x_all, rows, own, wn, ww, fn, fw, ones, start, place, four, ()
    )
    *out, w_out = call_out(
        place, gated, out_rows, out_parts, (seg == p // share).astype(jnp.int32), seqs, [cot_mine]
    )
    out_blocks, _ = reduce_group(out)

    mix_key, mix_recept = feedforward_lag_blends[:, 0], feedforward_lag_blends[:, 1]
    first_row = segment_predecessor_entries[0, 1][None]
    ffn_rows = jnp.concatenate(
        [second_layernorm_gain[None], second_layernorm_shift_term[None], first_row, feedforward_lag_blends.T, jnp.zeros((3, width), F32)]
    )
    residual, ffn_unit, ffn_scale, ffn_normed, normed_low = call_ffn_norm(
        x, out_blocks, ffn_rows, [w_ffn]
    )
    ffn_scale = ffn_scale[:, :1]
    normed_all = gather_group(normed_low)
    gate_part = after(own_part(feedforward_acceptor_projection, 1), normed_all)
    gate_mine = lax.all_gather(gate_part, "seg", axis=0, tiled=True)
    before = lax.dynamic_slice_in_dim(normed_all, jnp.maximum(p * length - 1, 0), 1, 0).astype(F32)
    previous = jnp.where(p == 0, first_row, before)
    ffn_delta = shift_down(ffn_normed, previous) - ffn_normed
    recept_in = (ffn_normed + ffn_delta * mix_recept).astype(BF16)
    cot = result_adjoint[0].astype(F32)
    if seqs == 2:
        gate_other = lax.ppermute(gate_mine, "seq", SWAP)
    else:
        gate_mine = gate_other = lax.all_gather(gate_mine, "seq", axis=1, tiled=True)

    key_in, recept_all, hidden, squared, *values = call_ffn_forward(normed_all, ffn_rows, w_ffn, place, seqs, ())
    value_blocks, sent = reduce_group(values)
    d_mine = call_ffn_gate(recept_all, cot_mine, cot_other, gate_mine, place, [sent])
    d_other = lax.ppermute(d_mine, "seq", SWAP) if seqs == 2 else d_mine
    if seqs == 2:
        grad_ffn_value = call_grad_halves(place, d_mine, d_other, squared)
    else:
        grad_ffn_value = call_grad(d_mine, squared, ())
    d_hidden, *d_key = call_ffn_backward(
        d_mine, d_other, hidden, w_ffn, place, seqs, [value_blocks, grad_ffn_value]
    )
    grad_ffn_value = reduce_rows(grad_ffn_value)
    key_blocks, _ = reduce_group(d_key)

    output, d_gate_cut, d_fr = call_ffn_local(
        place, recept_in, value_blocks, result_adjoint[0], residual, gate_mine, gate_other, group, ()
    )
    d_fk = add_up(key_blocks)
    d_fdelta = d_fk * mix_key + d_fr * mix_recept
    d_normed = d_fk + d_fr - d_fdelta + jnp.concatenate([d_fdelta[1:], next_row(d_fdelta[:1], -1)], 0)
    g = d_normed * second_layernorm_gain
    d_residual = cot + ffn_scale * (
        g - jnp.mean(g, -1, keepdims=True) - ffn_unit * jnp.mean(g * ffn_unit, -1, keepdims=True)
    )
    d_att_own = after(d_residual.astype(BF16), grad_ffn_value)
    d_att = gather_group(d_att_own)
    grad_ffn_key = call_grad(key_in, d_hidden, [d_att_own])
    ffn_sums = jnp.stack(
        [
            jnp.sum(d_normed * ffn_unit, 0), jnp.sum(d_normed, 0),
            jnp.sum(ffn_delta * d_fk, 0), jnp.sum(ffn_delta * d_fr, 0),
        ]
    )

    def join_hidden(a):
        if seqs != 2:
            return lax.all_to_all(a, "seq", 0, 1, tiled=True).astype(F32)
        part = a.shape[0] // 2
        kept = lax.dynamic_slice_in_dim(a, me * part, part, 0).astype(F32)
        came = lax.ppermute(lax.dynamic_slice_in_dim(a, (1 - me) * part, part, 0), "seq", SWAP).astype(F32)
        return jnp.where(me == 0, jnp.concatenate([kept, came], 1), jnp.concatenate([came, kept], 1))

    ends_high = ends.astype(BF16)
    ends_low = (ends - ends_high.astype(F32)).astype(BF16)
    moved = after_all(jnp.concatenate([d_gate_cut, ends_high, ends_low], 1), [d_att, grad_ffn_key])
    moved = lax.all_to_all(moved, TP, 0, 0, tiled=True)
    d_gate_own = moved[:, :length].reshape(tokens, cw)
    end_states = moved[:, length : length + HEAD].astype(F32) + moved[:, length + HEAD :].astype(F32)
    own_sums, decay_up, dr, dk, dv, dg, d_pre = call_wkv_backward(
        length, d_att, r, k, v, w, graw, wkv, dm, w_out, own, ones, sum_table(length), start, ends, adjoints, place,
        [grad_ffn_key],
    )
    grads = call_grads([xr, xk, xv, xg, recept_all], [dr, dk, dv, dg, d_gate_own], gated, d_att, segs, ())
    summed = reduce_rows(grads.reshape(-1, cw)).reshape(6, rows_seg, cw)
    more = jnp.concatenate([jnp.sum(own_sums.reshape(4, 8, cw), 1), decay_up[:decays]], 0)
    more = lax.dynamic_update_slice(jnp.zeros((16 * -(-(8 + decays) // 16), width), F32), more, (4, p * cw))
    more = lax.dynamic_update_slice(more, ffn_sums, (0, 0)).astype(BF16)
    packed, *dx = call_mix_backward(
        rank, 2 * length, x_all, rows, lm, dm, dr, dk, dv, dg, d_pre, wn, ww, fn, fw, more, place, four, decays, seqs,
        [grads],
    )
    dx_blocks, _ = reduce_group(dx)
    dx_total = add_up(dx_blocks)
    input_grad = d_residual + dx_total

    five = summed[:5].reshape(5, group, block, cw).transpose(1, 0, 2, 3).reshape(group, -1, cw)
    grad_ffn_value = join_hidden(grad_ffn_value)
    grad_ffn_key = join_hidden(reduce_rows(grad_ffn_key))
    grad_out = summed[5].reshape(group, cw // segs, cw).transpose(1, 0, 2).reshape(cw // segs, width)
    grad_out = lax.ppermute(
        grad_out, ALL, [(i * group + j, segs * j + i) for i in range(segs) for j in range(group)]
    ).astype(F32)
    small, _ = reduce_segs(lambda s: lax.dynamic_slice_in_dim(packed, s * rows_seg, rows_seg, 1))
    count = small.shape[0]
    small = small.astype(BF16).reshape(count, group, block).transpose(1, 0, 2).reshape(group, -1, cw)
    mixed = after(jnp.concatenate([five, small], 1), dx_blocks)
    mixed = lax.all_to_all(mixed, TP, 0, 0, tiled=True)
    five, small = mixed[:, : 5 * block], mixed[:, 5 * block :]
    five = five.reshape(group, 5, block, cw).transpose(1, 2, 0, 3).reshape(5, block, width).astype(F32)
    small = jnp.sum(small.astype(F32).reshape(group, count, block), 0)
    norm_gain, norm_bias, shift_mix = small[0], small[1], small[2:8].T
    at = 16
    shift_down_grad, at = small[at : at + ranks].T, at + ranks
    shift_up_grad, at = small[at : at + ranks].T, at + ranks
    d_down, at = small[at : at + decays].T, at + decays
    ffn_gain, ffn_bias, ffn_shift_mix = small[at], small[at + 1], small[at + 2 : at + 4].T
    decay_base, reward, group_gain, group_bias = (small[at + 4 + i] for i in range(4))
    d_up = small[at + 8 : at + 8 + decays].T
    end_states = end_states.transpose(1, 0, 2).reshape(HEAD, width)
    return (
        output[None],
        end_states[None, None],
        input_grad[None],
        norm_gain,
        norm_bias,
        shift_mix,
        shift_down_grad,
        shift_up_grad,
        decay_base,
        d_down,
        d_up,
        reward,
        five[0],
        five[1],
        five[2],
        five[3],
        grad_out,
        group_gain,
        group_bias,
        ffn_gain,
        ffn_bias,
        ffn_shift_mix,
        grad_ffn_key,
        five[4],
        grad_ffn_value,
    )


def solution(mesh):
    rows, tokens = P("seg", None), P("seg", TP, None)
    matrix = P("seg", "chan")
    vector_out, matrix_out = P(ALL), P(ALL, None)
    ffn_out = P(("seg", "seq"), "chan")
    return jax.shard_map(
        on_device,
        mesh=mesh,
        in_specs=(tokens, P("seg", None, None), P("seg", None, None)) + (P(),) * 9 + (rows,) * 5 + (P(),) * 5
        + (matrix, rows, matrix, tokens, P("seg", TP, None, None)),
        out_specs=(tokens, P("seg", TP, None, None), tokens) + (vector_out,) * 2 + (matrix_out,) * 3 + (vector_out,)
        + (matrix_out,) * 2 + (vector_out,) + (matrix_out,) * 5 + (vector_out,) * 4
        + (matrix_out, ffn_out, matrix_out, ffn_out),
        check_vma=False,
    )
```

```python
import jax
import jax.numpy as jnp
import numpy as np
from jax import lax
from jax.experimental import pallas as pl
from jax.experimental.pallas import tpu as pltpu
from jax.sharding import PartitionSpec as P

HEAD = 64
TP = ("seq", "chan")
ALL = ("seg", "seq", "chan")
LAYER_EPSILON = 1e-05
GROUP_EPSILON = 0.00064
F32 = jnp.float32
BF16 = jnp.bfloat16
CHUNK = 256
TOKENS = 128
VMEM = 56 * 2**20


def dot(a, b, dims):
    return lax.dot_general(
        a.astype(BF16), b.astype(BF16), (dims, ((), ())), preferred_element_type=F32
    )


def nn(a, b):
    return dot(a, b, ((1,), (0,)))


def nt(a, b):
    return dot(a, b, ((1,), (1,)))


def tn(a, b):
    return dot(a, b, ((0,), (0,)))


def iota(shape, axis):
    return lax.broadcasted_iota(jnp.int32, shape, axis)


def head_sum(values, ones):
    high = values.astype(BF16)
    low = (values - high.astype(F32)).astype(BF16)
    return nn(high, ones) + nn(low, ones)


def pyramid(w):
    length = w.shape[0]
    row = iota(w.shape, 0)
    before, after, total = jnp.zeros_like(w), jnp.zeros_like(w), w
    levels = []
    half = 1
    while half < length:
        upper = (row & half) != 0
        levels.append((half, upper, jnp.where(upper, before, after)))
        sibling = jnp.where(upper, pltpu.roll(total, half, 0), pltpu.roll(total, length - half, 0))
        before = jnp.where(upper, before + sibling, before)
        after = jnp.where(upper, after, after + sibling)
        total = total + sibling
        half *= 2
    return levels, before, after, total


def split_heads(values, heads):
    if heads == 1:
        return [values.astype(BF16)]
    lane = iota(values.shape, 1) // HEAD
    return [jnp.where(lane == head, values, 0.0).astype(BF16) for head in range(heads)]


def row_stats(x_ref):
    rows, width = x_ref.shape
    step = 128
    total = jnp.zeros((rows, step), F32)
    for at in range(0, width, step):
        total = total + x_ref[:, at : at + step].astype(F32)
    mean = jnp.sum(total, 1, keepdims=True) / width
    total = jnp.zeros((rows, step), F32)
    for at in range(0, width, step):
        center = x_ref[:, at : at + step].astype(F32) - mean
        total = total + center * center
    return mean, lax.rsqrt(jnp.sum(total, 1, keepdims=True) / width + LAYER_EPSILON)


def fold(values):
    rows, width = values.shape
    return jnp.sum(values.reshape(rows // 8, 8, width), 0)


def rank_blocks(values, rank):
    lane = iota(values.shape, 1) // rank
    return jnp.concatenate([jnp.where(lane == j, values, 0.0).astype(BF16) for j in range(5)], 0)


def spread(states, same):
    flat = states.T
    return jnp.concatenate([flat] * (flat.shape[0] // HEAD), 1) * same


def compact(state):
    return sum(state[:, at : at + HEAD] for at in range(0, state.shape[1], HEAD)).T


def part_copies(place_ref, parts, full_ref, sem):
    rows = parts[0].shape[0]
    copies = []
    for m, part in enumerate(parts):
        at = pl.multiple_of((place_ref[0] ^ m) * rows, rows)
        copies.append(pltpu.make_async_copy(part, full_ref.at[pl.ds(at, rows), :], sem.at[m]))
    return copies


def load_parts(place_ref, parts, full_ref, sem):
    for copy in part_copies(place_ref, parts, full_ref, sem):
        copy.start()


def wait_parts(place_ref, parts, full_ref, sem):
    @pl.when(pl.program_id(0) == 0)
    def _():
        for copy in part_copies(place_ref, parts, full_ref, sem):
            copy.wait()


GAIN, BIAS, MIX, FIRST = 0, 1, 2, 8


def mix_forward(
    rank, x_ref, rows_ref, own_ref, wn_ref, ww_ref, fn_ref, fw_ref,
    ones_ref, start_ref, place_ref, part0, part1, part2, part3, *refs,
):
    (
        gated_ref, xk_ref, xv_ref, xr_ref, xg_ref, r_ref, k_ref, v_ref, w_ref, graw_ref, wkv_ref, lm_ref, dm_ref,
        ends_ref, normed_ref, delta_ref, carry_ref, state_ref, four_ref, sem,
    ) = refs[-20:]
    step = pl.program_id(0)
    length, width = x_ref.shape
    own = own_ref.shape[1]
    heads = own // HEAD

    @pl.when(step == 0)
    def _():
        carry_ref[...] = jnp.broadcast_to(rows_ref[FIRST : FIRST + 1, :], carry_ref.shape)
        state_ref[...] = spread(start_ref[...], ones_ref[...].astype(F32))
        load_parts(place_ref, (part0, part1, part2, part3), four_ref, sem)

    mean, scale = row_stats(x_ref)
    first = iota((length, CHUNK), 0) == 0
    narrow = jnp.zeros((length, wn_ref.shape[0]), F32)
    for at in range(0, width, CHUNK):
        c = slice(at, at + CHUNK)
        normed = (x_ref[:, c].astype(F32) - mean) * scale * rows_ref[GAIN : GAIN + 1, c] + rows_ref[BIAS : BIAS + 1, c]
        delta = jnp.where(first, carry_ref[0:1, c], pltpu.roll(normed, 1, 0)) - normed
        carry_ref[0:1, c] = normed[length - 1 : length, :]
        normed_ref[:, c] = normed
        delta_ref[:, c] = delta
        narrow = narrow + nt(normed + delta * rows_ref[MIX : MIX + 1, c], wn_ref[:, c])
    middle = jnp.tanh(narrow)
    lm_ref[...] = middle
    blocks = rank_blocks(middle, rank)
    decay_in = jnp.zeros((length, fn_ref.shape[0]), F32)
    for at in range(0, width, CHUNK):
        c = slice(at, at + CHUNK)
        normed, delta = normed_ref[:, c], delta_ref[:, c]
        modifiers = nn(blocks, ww_ref[:, c])
        for j, ref in enumerate((None, xk_ref, xv_ref, xr_ref, xg_ref)):
            modifier = modifiers[j * length : (j + 1) * length, :]
            mixed = (normed + delta * (rows_ref[MIX + 1 + j : MIX + 2 + j, c] + modifier)).astype(BF16)
            if ref is None:
                decay_in = decay_in + nt(mixed, fn_ref[:, c])
            else:
                ref[:, c] = mixed
    decay_mid = jnp.tanh(decay_in)
    dm_ref[...] = decay_mid
    w = -jnp.exp(own_ref[0:1, :] + nn(decay_mid, fw_ref[...]))
    w_ref[...] = w
    wait_parts(place_ref, (part0, part1, part2, part3), four_ref, sem)
    r = nn(xr_ref[...], four_ref[:, :own]).astype(BF16)
    k = nn(xk_ref[...], four_ref[:, own : 2 * own]).astype(BF16)
    v = nn(xv_ref[...], four_ref[:, 2 * own : 3 * own]).astype(BF16)
    graw = nn(xg_ref[...], four_ref[:, 3 * own :])
    r_ref[...], k_ref[...], v_ref[...], graw_ref[...] = r, k, v, graw

    ones = ones_ref[...]
    for at in range(0, length, TOKENS):
        one_chunk(
            slice(at, at + TOKENS), r, k, v, w, graw, heads, ones, own_ref, wkv_ref, gated_ref, ends_ref.at[at // TOKENS],
            state_ref,
        )


def one_chunk(c, r, k, v, w, graw, heads, ones, own_ref, wkv_ref, gated_ref, end_ref, state_ref):
    v, w, graw = v[c, :], w[c, :], graw[c, :]
    rf, kf, vf = r[c, :].astype(F32), k[c, :].astype(F32), v.astype(F32)
    length = w.shape[0]
    levels, before, after, total = pyramid(w)
    row, col = iota((length, length), 0), iota((length, length), 1)
    apart = jnp.where(row > col, row ^ col, 0)
    scores = [jnp.zeros((length, length), F32)] * heads
    for half, upper, exponent in levels:
        scaled = jnp.where(upper, rf, kf) * jnp.exp(exponent)
        flat = scaled.astype(BF16)
        here = (apart >= half) & (apart < 2 * half)
        for head, one in enumerate(split_heads(scaled, heads)):
            scores[head] = jnp.where(here, nt(one, flat), scores[head])
    wkv = nn(jnp.concatenate([s.astype(BF16) for s in scores], 1), jnp.concatenate(split_heads(vf, heads), 0))
    state = state_ref[...]
    wkv = wkv + nt(rf * jnp.exp(before), state) + head_sum(rf * own_ref[1:2, :] * kf, ones) * vf
    wkv_ref[c, :] = wkv
    state = state * jnp.exp(total[0:1, :]) + tn(v, kf * jnp.exp(after)) * ones.astype(F32)
    state_ref[...] = state
    end_ref[...] = compact(state)

    center = wkv - head_sum(wkv, ones) / HEAD
    variance = head_sum(center * center, ones) / HEAD
    grouped = center * lax.rsqrt(variance + GROUP_EPSILON) * own_ref[2:3, :] + own_ref[3:4, :]
    gated_ref[c, :] = (grouped * graw * jax.nn.sigmoid(graw)).astype(BF16)


def state_cotangent(place_ref, mine_ref, other_ref, own):
    if mine_ref.dtype == F32:
        return mine_ref[0]
    tile = pl.num_programs(0) - 1 - pl.program_id(0)
    is_mine = tile // (pl.num_programs(0) // 2) == place_ref[1]
    wide = 2 * own
    parts = []
    for at in range(0, mine_ref.shape[2], wide):
        q = pl.ds(pl.multiple_of(place_ref[1] * own + at, own), own)
        parts.append(jnp.where(is_mine, mine_ref[0, :, q].astype(F32), other_ref[0, :, q].astype(F32)))
    both = jnp.concatenate(parts, 0)
    return both[:HEAD] + both[HEAD:]


def wkv_backward(
    place_ref, d_ref, r_ref, k_ref, v_ref, w_ref, graw_ref, wkv_ref, dm_ref, w_out_ref, own_ref, ones_ref, sums_ref,
    start_ref, ends_ref, adj_ref, *refs,
):
    own_sums_ref, decay_up_ref, dr_ref, dk_ref, dv_ref, dg_ref, dpre_ref, state_ref = refs[-8:]
    step = pl.program_id(0)
    length, own = r_ref.shape
    heads = own // HEAD
    ones = ones_ref[...]

    @pl.when(step == 0)
    def _():
        for ref in (state_ref, own_sums_ref, decay_up_ref):
            ref[...] = jnp.zeros_like(ref)

    reward, gain, bias = own_ref[1:2, :], own_ref[2:3, :], own_ref[3:4, :]
    wkv, graw, d_gated = wkv_ref[...], graw_ref[...], nt(d_ref[...], w_out_ref[...])
    center = wkv - head_sum(wkv, ones) / HEAD
    scale = lax.rsqrt(head_sum(center * center, ones) / HEAD + GROUP_EPSILON)
    normed = center * scale
    sigma = jax.nn.sigmoid(graw)
    d_grouped = d_gated * graw * sigma
    dg_ref[...] = (d_gated * (normed * gain + bias) * sigma * (1.0 + graw * (1.0 - sigma))).astype(BF16)
    d_normed = d_grouped * gain
    do = scale * (d_normed - head_sum(d_normed, ones) / HEAD - normed * (head_sum(d_normed * normed, ones) / HEAD))

    rb, kb, vb, dob = r_ref[...], k_ref[...], v_ref[...], do.astype(BF16)
    r, k, v, w = rb.astype(F32), kb.astype(F32), vb.astype(F32), w_ref[...]
    levels, before, after, total = pyramid(w)
    same = ones.astype(F32)
    d_state = state_ref[...] + spread(state_cotangent(place_ref, adj_ref, refs[0], own), same)
    state = spread(jnp.where(step == pl.num_programs(0) - 1, start_ref[...], ends_ref[0]), same)
    d_flat, flat = d_state.astype(BF16), state.astype(BF16)
    from_start, to_end, decay = jnp.exp(before), jnp.exp(after), jnp.exp(total[0:1, :])
    dr = from_start * nn(dob, flat)
    dk = to_end * nn(vb, d_flat)
    dv = nt(k * to_end, d_flat)
    through = [r * dr, k * dk]
    state_ref[...] = d_state * decay + tn(dob, r * from_start) * same
    whole = decay * jnp.sum(state * d_state, 0, keepdims=True)

    row, col = iota((length, length), 0), iota((length, length), 1)
    apart = row ^ col
    do_heads, v_heads = split_heads(do, heads), split_heads(v, heads)
    d_scores = [
        jnp.where(row > col, nt(do_heads[h], vb), jnp.where(row < col, nt(v_heads[h], dob), 0.0)).astype(BF16)
        for h in range(heads)
    ]
    scores = [jnp.zeros((length, length), F32)] * heads
    for half, upper, exponent in levels:
        factor = jnp.exp(exponent)
        scaled = jnp.where(upper, r, k) * factor
        mine = split_heads(scaled, heads)
        here = (apart >= half) & (apart < 2 * half)
        late = here & (row < col)
        for h in range(heads):
            scores[h] = jnp.where(late, nt(mine[h], scaled), scores[h])
        pulled = nn(
            jnp.concatenate([jnp.where(here, d, 0.0).astype(BF16) for d in d_scores], 1), jnp.concatenate(mine, 0)
        )
        if half > 1:
            through.append(scaled * pulled)
        pulled = pulled * factor
        dr = dr + jnp.where(upper, pulled, 0.0)
        dk = dk + jnp.where(upper, 0.0, pulled)
    dv = dv + nn(jnp.concatenate([s.astype(BF16) for s in scores], 1), jnp.concatenate(do_heads, 0))
    met = head_sum(v * do, ones)
    dr = dr + reward * k * met
    dk = dk + reward * r * met
    dv = dv + head_sum(r * reward * k, ones) * do
    d_log = whole + nn(sums_ref[...], jnp.concatenate([q.astype(BF16) for q in through], 0))
    d_pre = d_log * w
    dr_ref[...], dk_ref[...], dv_ref[...] = dr.astype(BF16), dk.astype(BF16), dv.astype(BF16)
    dpre_ref[...] = d_pre
    decay_up_ref[...] += tn(dm_ref[...], d_pre)
    for i, part in enumerate((d_pre, r * k * met, d_grouped * normed, d_grouped)):
        own_sums_ref[8 * i : 8 * i + 8, :] += fold(part)


def sum_table(length):
    row, col = np.arange(length)[:, None], np.arange(length)[None, :]
    tables = [col > row, col < row]
    half = 2
    while half < length:
        inside = (row // half) == (col // half)
        upper = (row // half) % 2 == 1
        tables.append(inside & np.where(upper, col > row, col < row))
        half *= 2
    return jnp.asarray(np.concatenate(tables, 1), BF16)


def mix_backward(rank, halves, *refs):
    (
        place_ref, x_ref, edge_ref, rows_ref, lm_ref, dm_ref, dr_ref, dk_ref, dv_ref, dg_ref, dpre_ref,
        wn_ref, ww_ref, fn_ref, fw_ref, more_ref, part0, part1, part2, part3,
    ) = refs[:20]
    packed_ref = refs[-13 - halves]
    outs = refs[-12 - halves : -12]
    (
        row_sums_ref, up_ref, down_ref, decay_down_ref, dx_ref, carry_ref, sum_ref, coef_ref, normed_ref, delta_ref,
        four_ref, sem,
    ) = refs[-12:]
    step = pl.program_id(0)
    from_first = pl.num_programs(0) - 1 - step
    length, width = x_ref.shape

    @pl.when(step == 0)
    def _():
        load_parts(place_ref, (part0, part1, part2, part3), four_ref, sem)
        for ref in (carry_ref, row_sums_ref, up_ref, down_ref, decay_down_ref):
            ref[...] = jnp.zeros_like(ref)

    own = dr_ref.shape[1]
    mean, scale = row_stats(x_ref)
    edge = edge_ref.shape[0]
    edge_mean, edge_scale = row_stats(edge_ref)
    middle, decay_mid = lm_ref[...], dm_ref[...]
    blocks = rank_blocks(middle, rank)
    d_pre = dpre_ref[...]
    d_decay = (nt(d_pre, fw_ref[...]) * (1.0 - decay_mid * decay_mid)).astype(BF16)
    sources = ((d_decay, None), (dk_ref[...], own), (dv_ref[...], 2 * own), (dr_ref[...], 0), (dg_ref[...], 3 * own))
    first = iota((length, CHUNK), 0) == 0
    last = iota((length, CHUNK), 0) == length - 1
    d_mid = jnp.zeros((5 * length, wn_ref.shape[0]), F32)
    wait_parts(place_ref, (part0, part1, part2, part3), four_ref, sem)
    for at in range(0, width, CHUNK):
        c = slice(at, at + CHUNK)
        gain, bias = rows_ref[GAIN : GAIN + 1, c], rows_ref[BIAS : BIAS + 1, c]
        normed = (x_ref[:, c].astype(F32) - mean) * scale * gain + bias
        edge_normed = (edge_ref[:, c].astype(F32) - edge_mean) * edge_scale * gain + bias
        before = jnp.where(from_first == 0, rows_ref[FIRST : FIRST + 1, c], edge_normed[edge - 1 : edge, :])
        delta = jnp.where(first, before, pltpu.roll(normed, 1, 0)) - normed
        normed_ref[:, c] = normed
        delta_ref[:, c] = delta
        modifiers = nn(blocks, ww_ref[:, c])
        total = jnp.zeros_like(normed)
        by_coef = jnp.zeros_like(normed)
        d_mods = []
        for j, (d, begin) in enumerate(sources):
            d_mixed = nt(d, four_ref[c, begin : begin + own]) if j else nn(d, fn_ref[:, c])
            coef = rows_ref[MIX + 1 + j : MIX + 2 + j, c] + modifiers[j * length : (j + 1) * length, :]
            if j == 0:
                decay_down_ref[:, c] += tn(d_decay, normed + delta * coef)
            d_mod = delta * d_mixed
            row_sums_ref[8 * (MIX + 1 + j) : 8 * (MIX + 2 + j), c] += fold(d_mod)
            d_mods.append(d_mod.astype(BF16))
            total = total + d_mixed
            by_coef = by_coef + d_mixed * coef
        d_mods = jnp.concatenate(d_mods, 0)
        up_ref[:, c] += tn(blocks, d_mods)
        d_mid = d_mid + nt(d_mods, ww_ref[:, c])
        sum_ref[:, c] = total
        coef_ref[:, c] = by_coef
    lane = iota(middle.shape, 1) // rank
    d_low = jnp.zeros_like(middle)
    for j in range(5):
        d_low = jnp.where(lane == j, d_mid[j * length : (j + 1) * length, :], d_low)
    d_low = (d_low * (1.0 - middle * middle)).astype(BF16)
    sum_g = jnp.zeros((length, CHUNK), F32)
    sum_gn = jnp.zeros((length, CHUNK), F32)
    for at in range(0, width, CHUNK):
        c = slice(at, at + CHUNK)
        normed, delta = normed_ref[:, c], delta_ref[:, c]
        mix = rows_ref[MIX : MIX + 1, c]
        d_in = nn(d_low, wn_ref[:, c])
        down_ref[:, c] += tn(d_low, normed + delta * mix)
        row_sums_ref[8 * MIX : 8 * MIX + 8, c] += fold(delta * d_in)
        d_delta = coef_ref[:, c] + d_in * mix
        above = jnp.where(last, carry_ref[0:1, c], pltpu.roll(d_delta, length - 1, 0))
        carry_ref[0:1, c] = d_delta[0:1, :]
        d_normed = sum_ref[:, c] + d_in - d_delta + above
        unit = (x_ref[:, c].astype(F32) - mean) * scale
        row_sums_ref[8 * GAIN : 8 * GAIN + 8, c] += fold(d_normed * unit)
        row_sums_ref[8 * BIAS : 8 * BIAS + 8, c] += fold(d_normed)
        g = d_normed * rows_ref[GAIN : GAIN + 1, c]
        sum_g = sum_g + g
        sum_gn = sum_gn + g * unit
        sum_ref[:, c] = g
    mean_g = jnp.sum(sum_g, 1, keepdims=True) / width
    mean_gn = jnp.sum(sum_gn, 1, keepdims=True) / width
    for at in range(0, width, CHUNK):
        c = slice(at, at + CHUNK)
        unit = (x_ref[:, c].astype(F32) - mean) * scale
        dx_ref[:, c] = (scale * (sum_ref[:, c] - mean_g - unit * mean_gn)).astype(BF16)
    store_half(place_ref, dx_ref, outs, from_first)

    @pl.when(step == pl.num_programs(0) - 1)
    def _():
        at = 16
        packed_ref[0:at, :] = jnp.zeros((at, width), BF16)
        for i in range(8):
            packed_ref[i : i + 1, :] = jnp.sum(row_sums_ref[8 * i : 8 * i + 8, :], 0, keepdims=True).astype(BF16)
        more = more_ref.shape[0]
        decays = packed_ref.shape[0] - at - 10 * rank - more
        for ref, size in ((down_ref, 5 * rank), (up_ref, 5 * rank), (decay_down_ref, decays), (more_ref, more)):
            packed_ref[at : at + size, :] = ref[0:size, :].astype(BF16)
            at += size


def whole(a):
    return pl.BlockSpec(a.shape, lambda t: (0,) * a.ndim)


def params(**more):
    return pltpu.CompilerParams(
        dimension_semantics=("arbitrary",), vmem_limit_bytes=VMEM, **more
    )


def light():
    return pl.CostEstimate(flops=0, bytes_accessed=0, transcendentals=0)


def pinned(pins):
    return [pl.BlockSpec(memory_space=pl.ANY)] * len(pins)


def part_specs(parts):
    return [pl.BlockSpec(memory_space=pltpu.SMEM)] + [pl.BlockSpec(memory_space=pl.ANY)] * len(parts)


def part_scratch(parts):
    rows, columns = parts[0].shape
    return [pltpu.VMEM((len(parts) * rows, columns), BF16), pltpu.SemaphoreType.DMA((len(parts),))]


def call_forward(rank, length, x, rows, own, wn, ww, fn, fw, ones, start, place, parts, pins):
    tokens, width = x.shape
    cw = own.shape[1]
    count = tokens // length
    tile = lambda n: pl.BlockSpec((length, n), lambda t: (t, 0))
    shape = lambda n, dtype: jax.ShapeDtypeStruct((tokens, n), dtype)
    fixed = (rows, own, wn, ww, fn, fw, ones, start)
    return pl.pallas_call(
        lambda *refs: mix_forward(rank, *refs),
        grid=(count,),
        in_specs=[tile(width)] + [whole(a) for a in fixed] + part_specs(parts) + pinned(pins),
        out_specs=[tile(cw)] + [tile(width)] * 4 + [tile(cw)] * 6 + [tile(wn.shape[0]), tile(fn.shape[0])]
        + [pl.BlockSpec((length // TOKENS, HEAD, cw), lambda t: (t, 0, 0))],
        out_shape=[shape(cw, BF16)] + [shape(width, BF16)] * 4 + [shape(cw, BF16)] * 3 + [shape(cw, F32)] * 3
        + [shape(wn.shape[0], F32), shape(fn.shape[0], F32), jax.ShapeDtypeStruct((tokens // TOKENS, HEAD, cw), F32)],
        scratch_shapes=[
            pltpu.VMEM((length, width), F32), pltpu.VMEM((length, width), F32), pltpu.VMEM((8, width), F32),
            pltpu.VMEM((cw, cw), F32),
        ]
        + part_scratch(parts),
        compiler_params=params(),
        cost_estimate=light(),
        name="mix_forward",
    )(x, *fixed, place, *parts, *pins)


def two_halves(tokens, width, length, seqs, backward=False):
    half = tokens // length // 2
    order = (lambda t: tokens // length - 1 - t) if backward else (lambda t: t)
    if seqs != 2:
        return [pl.BlockSpec((length, width), lambda t, place: (order(t), 0))], [jax.ShapeDtypeStruct((tokens, width), BF16)]
    mine = lambda t, place: (jnp.clip(order(t) - place[1] * half, 0, half - 1), 0)
    other = lambda t, place: (jnp.clip(order(t) - (1 - place[1]) * half, 0, half - 1), 0)
    return (
        [pl.BlockSpec((length, width), mine), pl.BlockSpec((length, width), other)],
        [jax.ShapeDtypeStruct((tokens // 2, width), BF16)] * 2,
    )


def store_half(place_ref, value_ref, outs, tile=None):
    if len(outs) == 1:
        outs[0][...] = value_ref[...]
        return
    tile = pl.program_id(0) if tile is None else tile
    is_mine = tile // (pl.num_programs(0) // 2) == place_ref[1]

    @pl.when(is_mine)
    def _():
        outs[0][...] = value_ref[...]

    @pl.when(jnp.logical_not(is_mine))
    def _():
        outs[1][...] = value_ref[...]


def ffn_forward(halves, place_ref, x_ref, edge_ref, rows_ref, w_all, *refs):
    key_ref, recept_ref, hidden_ref, squared_ref = refs[-7 - halves : -3 - halves]
    outs = refs[-3 - halves : -3]
    w_ref, value_ref, sem = refs[-3:]
    length, width = x_ref.shape
    units = hidden_ref.shape[1]
    edge = edge_ref.shape[0]
    load = pltpu.make_async_copy(w_all, w_ref, sem)

    @pl.when(pl.program_id(0) == 0)
    def _():
        load.start()

    first = iota((length, CHUNK), 0) == 0
    for at in range(0, width, CHUNK):
        c = slice(at, at + CHUNK)
        normed = x_ref[:, c].astype(F32)
        before = jnp.where(pl.program_id(0) == 0, rows_ref[2:3, c], edge_ref[edge - 1 : edge, c].astype(F32))
        delta = jnp.where(first, before, pltpu.roll(normed, 1, 0)) - normed
        key_ref[:, c] = (normed + delta * rows_ref[3:4, c]).astype(BF16)
        recept_ref[:, c] = (normed + delta * rows_ref[4:5, c]).astype(BF16)

    @pl.when(pl.program_id(0) == 0)
    def _():
        load.wait()

    hidden = jnp.maximum(nn(key_ref[...], w_ref[:, :units]), 0.0)
    hidden_ref[...] = hidden
    squared = (hidden * hidden).astype(BF16)
    squared_ref[...] = squared
    for at in range(0, width, CHUNK):
        c = slice(at, at + CHUNK)
        value_ref[:, c] = nt(squared, w_ref[c, units:]).astype(BF16)
    store_half(place_ref, value_ref, outs)


def call_ffn_forward(x, rows, w, place, seqs, pins):
    tokens, width = x.shape
    length, edge = 256, 16
    units = w.shape[1] // 2
    tile = lambda n: pl.BlockSpec((length, n), lambda t, place: (t, 0))
    shape = lambda n, dtype: jax.ShapeDtypeStruct((tokens, n), dtype)
    specs, shapes = two_halves(tokens, width, length, seqs)
    return pl.pallas_call(
        lambda *refs: ffn_forward(len(specs), *refs),
        grid_spec=pltpu.PrefetchScalarGridSpec(
            num_scalar_prefetch=1,
            grid=(tokens // length,),
            in_specs=[
                tile(width),
                pl.BlockSpec((edge, width), lambda t, place: (jnp.maximum(t * (length // edge) - 1, 0), 0)),
                pl.BlockSpec(rows.shape, lambda t, place: (0, 0)),
            ]
            + pinned([w]) + pinned(pins),
            out_specs=[tile(width)] * 2 + [tile(units)] * 2 + specs,
            scratch_shapes=[
                pltpu.VMEM(w.shape, BF16), pltpu.VMEM((length, width), BF16), pltpu.SemaphoreType.DMA,
            ],
        ),
        out_shape=[shape(width, BF16)] * 2 + [shape(units, F32), shape(units, BF16)] + shapes,
        compiler_params=params(),
        cost_estimate=light(),
        name="ffn_forward",
    )(place, x, x, rows, w, *pins)


def call_ffn_gate(recept, cot_mine, cot_other, gate, place, pins):
    tokens, width = recept.shape
    length = 256
    half = gate.shape[1]
    step = min(CHUNK, half)
    rows = 128
    tiles, per = tokens // length, length // rows
    split = cot_mine.shape[0] < tiles * per

    def kernel(place_ref, recept_ref, mine_ref, other_ref, gate_ref, *refs):
        recept = recept_ref[...]
        is_mine = pl.program_id(0) // (tiles // 2) == place_ref[1]
        for at in range(0, half, step):
            c = slice(at, at + step)
            gate = jax.nn.sigmoid(nn(recept, gate_ref[:, c]))
            for i in range(per):
                r = slice(i * rows, (i + 1) * rows)
                cot = jnp.where(is_mine, mine_ref[i, :, c].astype(F32), other_ref[i, :, c].astype(F32))
                refs[-1][r, c] = (cot * gate[r, :]).astype(BF16)

    column = (lambda place: place[1]) if half < width else (lambda place: 0)

    def cot_spec(core):
        if not split:
            return pl.BlockSpec((per, rows, half), lambda t, place: (t, 0, column(place)))
        at = lambda t, place: jnp.clip(t - core(place) * (tiles // 2), 0, tiles // 2 - 1)
        return pl.BlockSpec((per, rows, half), lambda t, place: (at(t, place), 0, column(place)))

    return pl.pallas_call(
        kernel,
        grid_spec=pltpu.PrefetchScalarGridSpec(
            num_scalar_prefetch=1,
            grid=(tiles,),
            in_specs=[
                pl.BlockSpec((length, width), lambda t, place: (t, 0)),
                cot_spec(lambda place: place[1]), cot_spec(lambda place: 1 - place[1]),
                pl.BlockSpec(gate.shape, lambda t, place: (0, 0), pipeline_mode=pl.Buffered(1)),
            ]
            + pinned(pins),
            out_specs=pl.BlockSpec((length, half), lambda t, place: (t, 0)),
        ),
        out_shape=jax.ShapeDtypeStruct((tokens, half), BF16),
        compiler_params=params(),
        cost_estimate=light(),
        name="ffn_gate",
    )(place, recept, cot_mine, cot_other, gate, *pins)


def ffn_backward(halves, place_ref, mine_ref, other_ref, hidden_ref, w_all, *refs):
    d_hidden_ref = refs[-5 - halves]
    outs = refs[-4 - halves : -4]
    w_ref, d_values_ref, value_ref, sem = refs[-4:]
    width = d_values_ref.shape[1]
    half = mine_ref.shape[1]
    units = hidden_ref.shape[1]
    load = pltpu.make_async_copy(w_all, w_ref, sem)

    @pl.when(pl.program_id(0) == 0)
    def _():
        load.start()

    cores = ((mine_ref, place_ref[1]), (other_ref, 1 - place_ref[1])) if half < width else ((mine_ref, 0),)
    for ref, core in cores:
        d_values_ref[:, pl.ds(pl.multiple_of(core * half, half), half)] = ref[...]

    @pl.when(pl.program_id(0) == 0)
    def _():
        load.wait()

    d_hidden = (nn(d_values_ref[...], w_ref[:, units:]) * 2.0 * hidden_ref[...]).astype(BF16)
    d_hidden_ref[...] = d_hidden
    for at in range(0, width, CHUNK):
        c = slice(at, at + CHUNK)
        value_ref[:, c] = nt(d_hidden, w_ref[c, :units]).astype(BF16)
    store_half(place_ref, value_ref, outs)


def call_ffn_backward(mine, other, hidden, w, place, seqs, pins):
    tokens, half = mine.shape
    width = w.shape[0]
    length = 256
    units = hidden.shape[1]
    tile = lambda n: pl.BlockSpec((length, n), lambda t, place: (t, 0))
    shape = lambda n: jax.ShapeDtypeStruct((tokens, n), BF16)
    specs, shapes = two_halves(tokens, width, length, seqs)
    return pl.pallas_call(
        lambda *refs: ffn_backward(len(specs), *refs),
        grid_spec=pltpu.PrefetchScalarGridSpec(
            num_scalar_prefetch=1,
            grid=(tokens // length,),
            in_specs=[tile(half), tile(half), tile(units)] + pinned([w]) + pinned(pins),
            out_specs=[tile(units)] + specs,
            scratch_shapes=[
                pltpu.VMEM(w.shape, BF16), pltpu.VMEM((length, width), BF16), pltpu.VMEM((length, width), BF16),
                pltpu.SemaphoreType.DMA,
            ],
        ),
        out_shape=[shape(units)] + shapes,
        compiler_params=params(),
        cost_estimate=light(),
        name="ffn_backward",
    )(place, mine, other, hidden, w, *pins)


def call_grad(x, d, pins):
    tokens, width = x.shape
    units = d.shape[1]
    columns = 512 if tokens <= 1024 else 256

    def kernel(x_ref, d_ref, *refs):
        refs[-1][...] = tn(x_ref[...], d_ref[...]).astype(BF16)

    return pl.pallas_call(
        kernel,
        grid=(width // columns,),
        in_specs=[
            pl.BlockSpec((tokens, columns), lambda t: (0, t)),
            pl.BlockSpec(d.shape, lambda t: (0, 0), pipeline_mode=pl.Buffered(1)),
        ]
        + pinned(pins),
        out_specs=pl.BlockSpec((columns, units), lambda t: (t, 0)),
        out_shape=jax.ShapeDtypeStruct((width, units), BF16),
        compiler_params=params(),
        cost_estimate=light(),
        name="grad",
    )(x, d, *pins)


def call_grad_halves(place, mine, other, d):
    tokens, half = mine.shape
    units = d.shape[1]
    columns = 512
    per = half // columns

    def kernel(place_ref, mine_ref, other_ref, d_ref, out_ref):
        @pl.when(pl.program_id(0) < per)
        def _():
            out_ref[...] = tn(mine_ref[...], d_ref[...]).astype(BF16)

        @pl.when(pl.program_id(0) >= per)
        def _():
            out_ref[...] = tn(other_ref[...], d_ref[...]).astype(BF16)

    def to(t, place):
        return (jnp.where(t < per, place[1] * per + t, (1 - place[1]) * per + t - per), 0)

    return pl.pallas_call(
        kernel,
        grid_spec=pltpu.PrefetchScalarGridSpec(
            num_scalar_prefetch=1,
            grid=(2 * per,),
            in_specs=[
                pl.BlockSpec((tokens, columns), lambda t, place: (0, jnp.minimum(t, per - 1))),
                pl.BlockSpec((tokens, columns), lambda t, place: (0, jnp.maximum(t - per, 0))),
                pl.BlockSpec(d.shape, lambda t, place: (0, 0), pipeline_mode=pl.Buffered(1)),
            ],
            out_specs=pl.BlockSpec((columns, units), to),
        ),
        out_shape=jax.ShapeDtypeStruct((2 * half, units), BF16),
        compiler_params=params(),
        cost_estimate=light(),
        name="grad_halves",
    )(place, mine, other, d)


def call_grads(xs, ds, gated, d_att, segs, pins):
    tokens, width = d_att.shape
    cw = gated.shape[1]
    rows, count = width // segs, len(xs)
    columns = 512 if tokens <= 1024 else 128
    per, cut = rows // columns, cw // segs

    def kernel(*refs):
        x_refs, d_refs, gated_ref, att_ref, out_ref = refs[:count], refs[count : 2 * count], refs[-3 - len(pins)], refs[-2 - len(pins)], refs[-1]
        s, at = pl.program_id(0) // per, pl.program_id(0) % per
        for j in range(count):
            out_ref[s, j, pl.ds(pl.multiple_of(at * columns, columns), columns), :] = tn(
                x_refs[j][...], d_refs[j][...]
            ).astype(BF16)
        result = tn(gated_ref[...], att_ref[...]).astype(BF16)
        each = columns // cw
        for i in range(each):
            to = pl.multiple_of((pl.program_id(0) * each + i) * cut, cut)
            for m in range(segs):
                out_ref[m, count, pl.ds(to, cut), :] = result[m * cut : (m + 1) * cut, i * cw : (i + 1) * cw]

    block = pl.BlockSpec((tokens, columns), lambda t: (0, t))
    fixed = pl.BlockSpec((tokens, cw), lambda t: (0, 0), pipeline_mode=pl.Buffered(1))
    shape = (segs, count + 1, rows, cw)
    return pl.pallas_call(
        kernel,
        grid=(width // columns,),
        in_specs=[block] * count + [fixed] * count + [fixed, block] + pinned(pins),
        out_specs=pl.BlockSpec(shape, lambda t: (0, 0, 0, 0)),
        out_shape=jax.ShapeDtypeStruct(shape, BF16),
        compiler_params=params(),
        cost_estimate=light(),
        name="grads",
    )(*xs, *ds, gated, d_att, *pins)


def call_ffn_norm(x, blocks, rows, pins):
    length, width = x.shape
    count = blocks.shape[0]

    def kernel(x_ref, blocks_ref, rows_ref, *refs):
        sum_ref, unit_ref, scale_ref, normed_ref, low_ref = refs[-5:]
        lanes = 128
        total = jnp.zeros((length, lanes), F32)
        for at in range(0, width, lanes):
            c = slice(at, at + lanes)
            value = x_ref[:, c].astype(F32)
            for i in range(count):
                value = value + blocks_ref[i, :, c].astype(F32)
            sum_ref[:, c] = value
            total = total + value
        mean = jnp.sum(total, 1, keepdims=True) / width
        total = jnp.zeros((length, lanes), F32)
        for at in range(0, width, lanes):
            center = sum_ref[:, at : at + lanes] - mean
            total = total + center * center
        scale = lax.rsqrt(jnp.sum(total, 1, keepdims=True) / width + LAYER_EPSILON)
        scale_ref[...] = jnp.broadcast_to(scale, scale_ref.shape)
        for at in range(0, width, lanes):
            c = slice(at, at + lanes)
            unit = (sum_ref[:, c] - mean) * scale
            unit_ref[:, c] = unit
            normed = unit * rows_ref[0:1, c] + rows_ref[1:2, c]
            normed_ref[:, c] = normed
            low_ref[:, c] = normed.astype(BF16)

    shape = lambda n, dtype: jax.ShapeDtypeStruct((length, n), dtype)
    return pl.pallas_call(
        kernel,
        grid=(1,),
        in_specs=[whole(x), whole(blocks), whole(rows)] + pinned(pins),
        out_specs=[pl.BlockSpec((length, n), lambda t: (0, 0)) for n in (width, width, 128, width, width)],
        out_shape=[shape(width, F32), shape(width, F32), shape(128, F32), shape(width, F32), shape(width, BF16)],
        compiler_params=params(),
        cost_estimate=light(),
        name="ffn_norm",
    )(x, blocks, rows, *pins)


def call_ffn_local(place, recept_in, blocks, cot, residual, gate_mine, gate_other, group, pins):
    length, width = recept_in.shape
    count, half = blocks.shape[0], gate_mine.shape[1]
    cw = width // group
    step = min(CHUNK, half)

    def kernel(place_ref, recept_ref, blocks_ref, cot_ref, residual_ref, mine_ref, other_ref, *refs):
        out_ref, cut_ref, d_ref, gate_ref = refs[-4:]
        recept = recept_ref[...]
        cores = ((mine_ref, place_ref[1]), (other_ref, 1 - place_ref[1])) if half < width else ((mine_ref, 0),)
        for ref, core in cores:
            for at in range(0, half, step):
                c = pl.ds(pl.multiple_of(core * half + at, step), step)
                gate = jax.nn.sigmoid(nn(recept, ref[:, at : at + step]))
                values = sum(blocks_ref[i, :, c].astype(F32) for i in range(count))
                out_ref[:, c] = (residual_ref[:, c] + gate * values).astype(BF16)
                gate_ref[:, c] = (cot_ref[:, c].astype(F32) * values * gate * (1.0 - gate)).astype(BF16)
        for i in range(group):
            cut_ref[i] = gate_ref[:, i * cw : (i + 1) * cw]
        for at in range(0, width, CHUNK):
            c = slice(at, at + CHUNK)
            d = jnp.zeros((length, CHUNK), F32)
            for ref, core in cores:
                d = d + nt(gate_ref[:, pl.ds(pl.multiple_of(core * half, half), half)], ref[c, :])
            d_ref[:, c] = d

    fixed = lambda a: pl.BlockSpec(a.shape, lambda t, place: (0,) * a.ndim)
    shapes = [(length, width), (group, length, cw), (length, width)]
    return pl.pallas_call(
        kernel,
        grid_spec=pltpu.PrefetchScalarGridSpec(
            num_scalar_prefetch=1,
            grid=(1,),
            in_specs=[fixed(a) for a in (recept_in, blocks, cot, residual, gate_mine, gate_other)] + pinned(pins),
            out_specs=[pl.BlockSpec(s, lambda t, place, n=len(s): (0,) * n) for s in shapes],
            scratch_shapes=[pltpu.VMEM((length, width), BF16)],
        ),
        out_shape=[jax.ShapeDtypeStruct(s, dtype) for s, dtype in zip(shapes, (BF16, BF16, F32))],
        compiler_params=params(),
        cost_estimate=light(),
        name="ffn_local",
    )(place, recept_in, blocks, cot, residual, gate_mine, gate_other, *pins)


def call_out(place, gated, own, parts, sender, seqs, pins):
    tokens, cw = gated.shape
    width = own.shape[1]
    length = 256
    specs, shapes = two_halves(tokens, width, length, seqs)

    def kernel(place_ref, gated_ref, own_ref, *refs):
        w_ref, value_ref = refs[-2:]

        @pl.when(pl.program_id(0) == 0)
        def _():
            received = refs[0][...]
            for ref in refs[1 : len(parts)]:
                received = received + ref[...]
            w_ref[...] = jnp.where(place_ref[2] == 1, own_ref[...], received)

        for at in range(0, width, CHUNK):
            c = slice(at, at + CHUNK)
            value_ref[:, c] = nn(gated_ref[...], w_ref[:, c]).astype(BF16)
        store_half(place_ref, value_ref, refs[-2 - len(specs) : -2])

    fixed = lambda a: pl.BlockSpec(a.shape, lambda t, place: (0, 0))

    return pl.pallas_call(
        kernel,
        grid_spec=pltpu.PrefetchScalarGridSpec(
            num_scalar_prefetch=1,
            grid=(tokens // length,),
            in_specs=[pl.BlockSpec((length, cw), lambda t, place: (t, 0))] + [fixed(a) for a in (own, *parts)]
            + pinned(pins),
            out_specs=specs + [pl.BlockSpec((cw, width), lambda t, place: (0, 0))],
            scratch_shapes=[pltpu.VMEM((length, width), BF16)],
        ),
        out_shape=shapes + [jax.ShapeDtypeStruct((cw, width), BF16)],
        compiler_params=params(),
        cost_estimate=light(),
        name="out_projection",
    )(jnp.concatenate([place, sender.reshape(1)]), gated, own, *parts, *pins)


def call_add(mine, other, pins):
    rows, width = mine.shape
    length = 256

    def kernel(a_ref, b_ref, *refs):
        refs[-1][...] = (a_ref[...].astype(F32) + b_ref[...].astype(F32)).astype(BF16)

    tile = pl.BlockSpec((length, width), lambda t: (t, 0))
    return pl.pallas_call(
        kernel,
        grid=(rows // length,),
        in_specs=[tile, tile] + pinned(pins),
        out_specs=tile,
        out_shape=jax.ShapeDtypeStruct((rows, width), BF16),
        compiler_params=params(),
        cost_estimate=light(),
        name="add",
    )(mine, other, *pins)


def call_combine(order, mine, other):
    count, rows, width = mine.shape

    def kernel(order_ref, mine_ref, other_ref, *outs):
        total = mine_ref[0].astype(F32) + other_ref[0].astype(F32)
        for k in range(count):

            @pl.when(pl.program_id(0) == k)
            def _():
                outs[k][...] = total.astype(outs[k].dtype)

    block = pl.BlockSpec((1, rows, width), lambda k, order: (order[k], 0, 0))
    return pl.pallas_call(
        kernel,
        grid_spec=pltpu.PrefetchScalarGridSpec(
            num_scalar_prefetch=1,
            grid=(count,),
            in_specs=[block, block],
            out_specs=[pl.BlockSpec((rows, width), lambda k, order: (0, 0))] * count,
        ),
        out_shape=[jax.ShapeDtypeStruct((rows, width), F32 if k == 0 else BF16) for k in range(count)],
        compiler_params=params(),
        cost_estimate=light(),
        name="combine",
    )(order, mine, other)


def call_wkv_backward(
    length, d, r, k, v, w, graw, wkv, dm, w_out, own, ones, sums, start, ends, adjoints, place, pins
):
    tokens, cw = r.shape
    count = tokens // length
    tile = lambda n: pl.BlockSpec((length, n), lambda t, place: (count - 1 - t, 0))
    fixed = lambda a: pl.BlockSpec(a.shape, lambda t, place: (0, 0))
    shape = lambda dtype: jax.ShapeDtypeStruct((tokens, cw), dtype)
    wide = dm.shape[1]

    def folded(a, core):
        rows = a.shape[1] - length
        at = lambda t, place: jnp.clip(count - 1 - t - core(place) * (count // 2), 0, count // 2 - 1)
        return pl.BlockSpec((1, rows, a.shape[2]), lambda t, place: (at(t, place), length // rows, 0))

    if len(adjoints) == 2:
        states = [folded(adjoints[0], lambda place: place[1]), folded(adjoints[1], lambda place: 1 - place[1])]
    else:
        states = [pl.BlockSpec((1, HEAD, cw), lambda t, place: (count - 1 - t, 0, 0))]
    return pl.pallas_call(
        wkv_backward,
        grid_spec=pltpu.PrefetchScalarGridSpec(
            num_scalar_prefetch=1,
            grid=(count,),
            in_specs=[tile(d.shape[1])] + [tile(cw)] * 6 + [tile(wide)]
            + [fixed(a) for a in (w_out, own, ones, sums, start)]
            + [pl.BlockSpec((1, HEAD, cw), lambda t, place: (jnp.maximum(count - 2 - t, 0), 0, 0))]
            + states + pinned(pins),
            out_specs=[pl.BlockSpec((32, cw), lambda t, place: (0, 0)), pl.BlockSpec((wide, cw), lambda t, place: (0, 0))]
            + [tile(cw)] * 5,
            scratch_shapes=[pltpu.VMEM((cw, cw), F32)],
        ),
        out_shape=[jax.ShapeDtypeStruct((32, cw), F32), jax.ShapeDtypeStruct((wide, cw), F32)]
        + [shape(BF16)] * 4 + [shape(F32)],
        compiler_params=params(),
        cost_estimate=light(),
        name="wkv_backward",
    )(place, d, r, k, v, w, graw, wkv, dm, w_out, own, ones, sums, start, ends, *adjoints, *pins)


def call_mix_backward(
    rank, length, x, rows, lm, dm, dr, dk, dv, dg, dpre, wn, ww, fn, fw, more, place, parts, decays, seqs, pins
):
    tokens, width = x.shape
    cw = dr.shape[1]
    count = tokens // length
    edge = 16
    tile = lambda n: pl.BlockSpec((length, n), lambda t, place: (count - 1 - t, 0))
    before = pl.BlockSpec((edge, width), lambda t, place: (jnp.maximum((count - 1 - t) * (length // edge) - 1, 0), 0))
    fixed = lambda a: pl.BlockSpec(a.shape, lambda t, place: (0, 0))
    packed = 16 + 10 * rank + decays + more.shape[0]
    specs, shapes = two_halves(tokens, width, length, seqs, backward=True)
    return pl.pallas_call(
        lambda *refs: mix_backward(rank, len(specs), *refs),
        grid_spec=pltpu.PrefetchScalarGridSpec(
            num_scalar_prefetch=1,
            grid=(count,),
            in_specs=[tile(width), before, fixed(rows), tile(lm.shape[1]), tile(dm.shape[1])] + [tile(cw)] * 5
            + [fixed(a) for a in (wn, ww, fn, fw, more)] + pinned(parts) + pinned(pins),
            out_specs=[pl.BlockSpec((packed, width), lambda t, place: (0, 0))] + specs,
            scratch_shapes=[pltpu.VMEM((n, width), F32) for n in (8 * 8, wn.shape[0], wn.shape[0], fn.shape[0])]
            + [pltpu.VMEM((length, width), BF16), pltpu.VMEM((8, width), F32)]
            + [pltpu.VMEM((length, width), F32)] * 4 + part_scratch(parts),
        ),
        out_shape=[jax.ShapeDtypeStruct((packed, width), BF16)] + shapes,
        compiler_params=params(),
        cost_estimate=light(),
        name="mix_backward",
    )(place, x, x, rows, lm, dm, dr, dk, dv, dg, dpre, wn, ww, fn, fw, more, *parts, *pins)


def gather_group(block):
    return lax.all_gather(block, TP, axis=0, tiled=True)


SWAP = [(0, 1), (1, 0)]


def reduce_halves(mine, other, pins):
    total = call_add(mine, lax.ppermute(other, "seq", SWAP), pins)
    return reduce_chan(total), total


def reduce_chan(total):
    chans = lax.axis_size("chan")
    return lax.all_to_all(total.reshape(chans, -1, total.shape[1]), "chan", 0, 0, tiled=True)


def reduce_apart(parts):
    chans, at = lax.axis_size("chan"), lax.axis_index("chan")
    if len(parts) == 2:
        mine, other = parts[0], lax.ppermute(parts[1], "seq", SWAP)
    else:
        mine = lax.psum_scatter(parts[0], "seq", scatter_dimension=0, tiled=True)
        other = jnp.zeros_like(mine)
    order = ((at + jnp.arange(chans)) % chans).astype(jnp.int32)
    cut = lambda a: a.reshape(chans, -1, a.shape[1])
    total, *sent = call_combine(order, cut(mine), cut(other))
    came = [
        lax.ppermute(a, "chan", [(i, (i + k + 1) % chans) for i in range(chans)]) for k, a in enumerate(sent)
    ]
    return sum((a.astype(F32) for a in came), total), came


def add_up(blocks):
    return jnp.sum(blocks.astype(F32), 0)


def reduce_group(parts, pins=()):
    if len(parts) == 2:
        return reduce_halves(*parts, pins)
    total = lax.psum_scatter(parts[0], "seq", scatter_dimension=0, tiled=True)
    return reduce_chan(total), total


def after(a, before):
    corner = before[(slice(0, 1),) * before.ndim].reshape((1,) * a.ndim)
    return a + (corner.astype(F32) * 0.0).astype(a.dtype)


def after_all(a, others):
    for other in others:
        a = after(a, other)
    return a


def next_row(row, by):
    count = lax.axis_size(TP)
    return lax.ppermute(row, TP, [(i, i + by) for i in range(count) if 0 <= i + by < count])


def shift_down(values, first_row):
    return jnp.concatenate([first_row, values[:-1]], 0)


def unit_rows(values):
    center = values - jnp.mean(values, -1, keepdims=True)
    scale = lax.rsqrt(jnp.mean(center * center, -1, keepdims=True) + LAYER_EPSILON)
    return center * scale, scale


def on_device(
    sequence_elements,
    segment_predecessor_entries,
    opening_recurrences,
    first_layernorm_gain,
    first_layernorm_shift_term,
    lag_blend_coefficients,
    lag_narrowing_factor,
    lag_widening_factors,
    fading_exponent_baseline,
    fading_narrowing_factor,
    fading_widening_factor,
    present_reward,
    acceptor_projection,
    address_projection,
    content_projection,
    valve_projection,
    timemix_result_projection,
    subspace_cluster_gain,
    subspace_cluster_shift_term,
    second_layernorm_gain,
    second_layernorm_shift_term,
    feedforward_lag_blends,
    feedforward_address_projection,
    feedforward_acceptor_projection,
    feedforward_content_projection,
    result_adjoint,
    final_recurrence_adjoint,
):
    segs, seqs, chans = lax.axis_size("seg"), lax.axis_size("seq"), lax.axis_size("chan")
    group = seqs * chans
    p = lax.axis_index(TP)
    x = sequence_elements[0]
    length, width = x.shape
    tokens = group * length
    cw = width // group
    heads = cw // HEAD
    rank = lag_widening_factors.shape[1] // 5
    ranks, decays = 5 * rank, fading_widening_factor.shape[1]

    def columns(a, axis=-1):
        return lax.dynamic_slice_in_dim(a, p * cw, cw, axis % a.ndim)

    me, seg = lax.axis_index("seq"), lax.axis_index("seg")
    block = width // (segs * group)
    rows_seg = width // segs
    flips = [[(s, s ^ m) for s in range(segs)] for m in range(segs)]

    def seg_parts(a):
        return [a] + [lax.ppermute(a, "seg", flips[m]) for m in range(1, segs)]

    def own_part(a, axis):
        size = a.shape[axis] // seqs
        return lax.dynamic_slice_in_dim(a, me * size, size, axis)

    def reduce_segs(piece):
        sent = [piece(seg ^ m) for m in range(1, segs)]
        return sum((lax.ppermute(a, "seg", flips[m + 1]).astype(F32) for m, a in enumerate(sent)), piece(seg).astype(F32)), sent

    def reduce_rows(a):
        return lax.psum_scatter(a, "seg", scatter_dimension=0, tiled=True)

    x_all = gather_group(x)
    four = seg_parts(
        jnp.concatenate(
            [columns(a) for a in (acceptor_projection, address_projection, content_projection, valve_projection)], 1
        )
    )
    share = group // segs
    out_rows = after(lax.dynamic_slice_in_dim(timemix_result_projection, (p % share) * cw, cw, 0), four[-1])
    out_parts = [
        lax.ppermute(out_rows, ALL, [((j // share) * group + j, ((j // share) ^ m) * group + j) for j in range(group)])
        for m in range(1, segs)
    ]
    ffn_part = jnp.concatenate([own_part(a, 1) for a in (feedforward_address_projection, feedforward_content_projection)], 1)
    w_ffn = lax.all_gather(after_all(ffn_part, four[1:]), "seg", axis=0, tiled=True)
    cot = after(result_adjoint[0], x_all)
    adjoints = final_recurrence_adjoint[0, 0]
    if seqs == 2:
        adjoints = adjoints.reshape(HEAD, seqs, chans, cw).transpose(2, 0, 1, 3).reshape(chans, HEAD, seqs * cw)
        high = adjoints.astype(BF16)
        adjoints = jnp.concatenate([high, (adjoints - high.astype(F32)).astype(BF16)], 1)
        fold_rows = 2 * HEAD * seqs * cw // width
        adjoints = adjoints.reshape(chans, -1, fold_rows, seqs * cw).transpose(0, 2, 1, 3).reshape(chans, fold_rows, width)
        sent = jnp.concatenate([jnp.broadcast_to(cot[None], (chans, length, width)), adjoints], 1)
        cot_mine = lax.all_to_all(sent, "chan", 0, 0, tiled=True)
        cot_other = lax.ppermute(cot_mine, "seq", SWAP)

        adjoints = (cot_mine, cot_other)
    else:
        cot_mine = cot_other = gather_group(cot).reshape(group, length, width)
        adjoints = (lax.all_to_all(adjoints.reshape(HEAD, group, cw).transpose(1, 0, 2), TP, 0, 0, tiled=True),)

    rows = jnp.concatenate(
        [
            first_layernorm_gain[None], first_layernorm_shift_term[None], lag_blend_coefficients.T,
            segment_predecessor_entries[0, 0][None], fading_exponent_baseline[None], present_reward[None],
            subspace_cluster_gain[None], subspace_cluster_shift_term[None], jnp.zeros((11, width), F32),
        ]
    )
    own = lax.dynamic_slice(rows, (FIRST + 1, p * cw), (8, cw))
    wn, ww, fn = lag_narrowing_factor.T, lag_widening_factors.T, fading_narrowing_factor.T
    fw = columns(fading_widening_factor.T)
    head_of = np.arange(cw) // HEAD
    ones = jnp.asarray(head_of[:, None] == head_of[None, :], BF16)
    start = columns(opening_recurrences[0])
    place = jnp.stack([seg, me]).astype(jnp.int32)

    gated, xk, xv, xr, xg, r, k, v, w, graw, wkv, lm, dm, ends = call_forward(
        rank, 2 * length, x_all, rows, own, wn, ww, fn, fw, ones, start, place, four, ()
    )
    *out, w_out = call_out(
        place, gated, out_rows, out_parts, (seg == p // share).astype(jnp.int32), seqs, [cot_mine]
    )
    out_blocks, _ = reduce_group(out)

    mix_key, mix_recept = feedforward_lag_blends[:, 0], feedforward_lag_blends[:, 1]
    first_row = segment_predecessor_entries[0, 1][None]
    ffn_rows = jnp.concatenate(
        [second_layernorm_gain[None], second_layernorm_shift_term[None], first_row, feedforward_lag_blends.T, jnp.zeros((3, width), F32)]
    )
    residual, ffn_unit, ffn_scale, ffn_normed, normed_low = call_ffn_norm(
        x, out_blocks, ffn_rows, [w_ffn]
    )
    ffn_scale = ffn_scale[:, :1]
    normed_all = gather_group(normed_low)
    gate_part = after(own_part(feedforward_acceptor_projection, 1), normed_all)
    gate_mine = lax.all_gather(gate_part, "seg", axis=0, tiled=True)
    before = lax.dynamic_slice_in_dim(normed_all, jnp.maximum(p * length - 1, 0), 1, 0).astype(F32)
    previous = jnp.where(p == 0, first_row, before)
    ffn_delta = shift_down(ffn_normed, previous) - ffn_normed
    recept_in = (ffn_normed + ffn_delta * mix_recept).astype(BF16)
    cot = result_adjoint[0].astype(F32)
    if seqs == 2:
        gate_other = lax.ppermute(gate_mine, "seq", SWAP)
    else:
        gate_mine = gate_other = lax.all_gather(gate_mine, "seq", axis=1, tiled=True)

    key_in, recept_all, hidden, squared, *values = call_ffn_forward(normed_all, ffn_rows, w_ffn, place, seqs, ())
    value_blocks, sent = reduce_group(values)
    d_mine = call_ffn_gate(recept_all, cot_mine, cot_other, gate_mine, place, [sent])
    d_other = lax.ppermute(d_mine, "seq", SWAP) if seqs == 2 else d_mine
    if seqs == 2:
        grad_ffn_value = call_grad_halves(place, d_mine, d_other, squared)
    else:
        grad_ffn_value = call_grad(d_mine, squared, ())
    d_hidden, *d_key = call_ffn_backward(
        d_mine, d_other, hidden, w_ffn, place, seqs, [value_blocks, grad_ffn_value]
    )
    grad_ffn_value = reduce_rows(grad_ffn_value)
    key_blocks, _ = reduce_group(d_key)

    output, d_gate_cut, d_fr = call_ffn_local(
        place, recept_in, value_blocks, result_adjoint[0], residual, gate_mine, gate_other, group, ()
    )
    d_fk = add_up(key_blocks)
    d_fdelta = d_fk * mix_key + d_fr * mix_recept
    d_normed = d_fk + d_fr - d_fdelta + jnp.concatenate([d_fdelta[1:], next_row(d_fdelta[:1], -1)], 0)
    g = d_normed * second_layernorm_gain
    d_residual = cot + ffn_scale * (
        g - jnp.mean(g, -1, keepdims=True) - ffn_unit * jnp.mean(g * ffn_unit, -1, keepdims=True)
    )
    d_att_own = after(d_residual.astype(BF16), grad_ffn_value)
    d_att = gather_group(d_att_own)
    grad_ffn_key = call_grad(key_in, d_hidden, [d_att_own])
    ffn_sums = jnp.stack(
        [
            jnp.sum(d_normed * ffn_unit, 0), jnp.sum(d_normed, 0),
            jnp.sum(ffn_delta * d_fk, 0), jnp.sum(ffn_delta * d_fr, 0),
        ]
    )

    def join_hidden(a):
        if seqs != 2:
            return lax.all_to_all(a, "seq", 0, 1, tiled=True).astype(F32)
        part = a.shape[0] // 2
        kept = lax.dynamic_slice_in_dim(a, me * part, part, 0).astype(F32)
        came = lax.ppermute(lax.dynamic_slice_in_dim(a, (1 - me) * part, part, 0), "seq", SWAP).astype(F32)
        return jnp.where(me == 0, jnp.concatenate([kept, came], 1), jnp.concatenate([came, kept], 1))

    ends_high = ends.astype(BF16)
    ends_low = (ends - ends_high.astype(F32)).astype(BF16)
    moved = after_all(jnp.concatenate([d_gate_cut, ends_high, ends_low], 1), [d_att, grad_ffn_key])
    moved = lax.all_to_all(moved, TP, 0, 0, tiled=True)
    d_gate_own = moved[:, :length].reshape(tokens, cw)
    end_states = moved[:, length : length + HEAD].astype(F32) + moved[:, length + HEAD :].astype(F32)
    own_sums, decay_up, dr, dk, dv, dg, d_pre = call_wkv_backward(
        length, d_att, r, k, v, w, graw, wkv, dm, w_out, own, ones, sum_table(length), start, ends, adjoints, place,
        [grad_ffn_key],
    )
    grads = call_grads([xr, xk, xv, xg, recept_all], [dr, dk, dv, dg, d_gate_own], gated, d_att, segs, ())
    summed = reduce_rows(grads.reshape(-1, cw)).reshape(6, rows_seg, cw)
    more = jnp.concatenate([jnp.sum(own_sums.reshape(4, 8, cw), 1), decay_up[:decays]], 0)
    more = lax.dynamic_update_slice(jnp.zeros((16 * -(-(8 + decays) // 16), width), F32), more, (4, p * cw))
    more = lax.dynamic_update_slice(more, ffn_sums, (0, 0)).astype(BF16)
    packed, *dx = call_mix_backward(
        rank, 2 * length, x_all, rows, lm, dm, dr, dk, dv, dg, d_pre, wn, ww, fn, fw, more, place, four, decays, seqs,
        [grads],
    )
    dx_total, dx_came = reduce_apart(dx)
    input_grad = d_residual + dx_total

    five = summed[:5].reshape(5, group, block, cw).transpose(1, 0, 2, 3).reshape(group, -1, cw)
    grad_ffn_value = join_hidden(grad_ffn_value)
    grad_ffn_key = join_hidden(reduce_rows(grad_ffn_key))
    grad_out = summed[5].reshape(group, cw // segs, cw).transpose(1, 0, 2).reshape(cw // segs, width)
    grad_out = lax.ppermute(
        grad_out, ALL, [(i * group + j, segs * j + i) for i in range(segs) for j in range(group)]
    ).astype(F32)
    small, _ = reduce_segs(lambda s: lax.dynamic_slice_in_dim(packed, s * rows_seg, rows_seg, 1))
    count = small.shape[0]
    small = small.astype(BF16).reshape(count, group, block).transpose(1, 0, 2).reshape(group, -1, cw)
    five = lax.all_to_all(five, TP, 0, 0, tiled=True)
    small = lax.all_to_all(after_all(small, dx_came), TP, 0, 0, tiled=True)
    five = five.reshape(group, 5, block, cw).transpose(1, 2, 0, 3).reshape(5, block, width).astype(F32)
    small = jnp.sum(small.astype(F32).reshape(group, count, block), 0)
    norm_gain, norm_bias, shift_mix = small[0], small[1], small[2:8].T
    at = 16
    shift_down_grad, at = small[at : at + ranks].T, at + ranks
    shift_up_grad, at = small[at : at + ranks].T, at + ranks
    d_down, at = small[at : at + decays].T, at + decays
    ffn_gain, ffn_bias, ffn_shift_mix = small[at], small[at + 1], small[at + 2 : at + 4].T
    decay_base, reward, group_gain, group_bias = (small[at + 4 + i] for i in range(4))
    d_up = small[at + 8 : at + 8 + decays].T
    end_states = end_states.transpose(1, 0, 2).reshape(HEAD, width)
    return (
        output[None],
        end_states[None, None],
        input_grad[None],
        norm_gain,
        norm_bias,
        shift_mix,
        shift_down_grad,
        shift_up_grad,
        decay_base,
        d_down,
        d_up,
        reward,
        five[0],
        five[1],
        five[2],
        five[3],
        grad_out,
        group_gain,
        group_bias,
        ffn_gain,
        ffn_bias,
        ffn_shift_mix,
        grad_ffn_key,
        five[4],
        grad_ffn_value,
    )


def solution(mesh):
    rows, tokens = P("seg", None), P("seg", TP, None)
    matrix = P("seg", "chan")
    vector_out, matrix_out = P(ALL), P(ALL, None)
    ffn_out = P(("seg", "seq"), "chan")
    return jax.shard_map(
        on_device,
        mesh=mesh,
        in_specs=(tokens, P("seg", None, None), P("seg", None, None)) + (P(),) * 9 + (rows,) * 5 + (P(),) * 5
        + (matrix, rows, matrix, tokens, P("seg", TP, None, None)),
        out_specs=(tokens, P("seg", TP, None, None), tokens) + (vector_out,) * 2 + (matrix_out,) * 3 + (vector_out,)
        + (matrix_out,) * 2 + (vector_out,) + (matrix_out,) * 5 + (vector_out,) * 4
        + (matrix_out, ffn_out, matrix_out, ffn_out),
        check_vma=False,
    )
```

```python
import jax
import jax.numpy as jnp
import numpy as np
from jax import lax
from jax.experimental import pallas as pl
from jax.experimental.pallas import tpu as pltpu
from jax.sharding import PartitionSpec as P

HEAD = 64
TP = ("seq", "chan")
ALL = ("seg", "seq", "chan")
LAYER_EPSILON = 1e-05
GROUP_EPSILON = 0.00064
F32 = jnp.float32
BF16 = jnp.bfloat16
CHUNK = 256
TOKENS = 128
VMEM = 62 * 2**20


def dot(a, b, dims):
    return lax.dot_general(
        a.astype(BF16), b.astype(BF16), (dims, ((), ())), preferred_element_type=F32
    )


def nn(a, b):
    return dot(a, b, ((1,), (0,)))


def nt(a, b):
    return dot(a, b, ((1,), (1,)))


def tn(a, b):
    return dot(a, b, ((0,), (0,)))


def iota(shape, axis):
    return lax.broadcasted_iota(jnp.int32, shape, axis)


def head_sum(values, ones):
    high = values.astype(BF16)
    low = (values - high.astype(F32)).astype(BF16)
    return nn(high, ones) + nn(low, ones)


def pyramid(w):
    length = w.shape[0]
    row = iota(w.shape, 0)
    before, after, total = jnp.zeros_like(w), jnp.zeros_like(w), w
    levels = []
    half = 1
    while half < length:
        upper = (row & half) != 0
        levels.append((half, upper, jnp.where(upper, before, after)))
        sibling = jnp.where(upper, pltpu.roll(total, half, 0), pltpu.roll(total, length - half, 0))
        before = jnp.where(upper, before + sibling, before)
        after = jnp.where(upper, after, after + sibling)
        total = total + sibling
        half *= 2
    return levels, before, after, total


def split_heads(values, heads):
    if heads == 1:
        return [values.astype(BF16)]
    lane = iota(values.shape, 1) // HEAD
    return [jnp.where(lane == head, values, 0.0).astype(BF16) for head in range(heads)]


def row_stats(x_ref):
    rows, width = x_ref.shape
    step = 128
    total = jnp.zeros((rows, step), F32)
    for at in range(0, width, step):
        total = total + x_ref[:, at : at + step].astype(F32)
    mean = jnp.sum(total, 1, keepdims=True) / width
    total = jnp.zeros((rows, step), F32)
    for at in range(0, width, step):
        center = x_ref[:, at : at + step].astype(F32) - mean
        total = total + center * center
    return mean, lax.rsqrt(jnp.sum(total, 1, keepdims=True) / width + LAYER_EPSILON)


def fold(values):
    rows, width = values.shape
    return jnp.sum(values.reshape(rows // 8, 8, width), 0)


def rank_blocks(values, rank):
    lane = iota(values.shape, 1) // rank
    return jnp.concatenate([jnp.where(lane == j, values, 0.0).astype(BF16) for j in range(5)], 0)


def spread(states, same):
    flat = states.T
    return jnp.concatenate([flat] * (flat.shape[0] // HEAD), 1) * same


def compact(state):
    return sum(state[:, at : at + HEAD] for at in range(0, state.shape[1], HEAD)).T


def part_copies(place_ref, parts, full_ref, sem):
    rows = parts[0].shape[0]
    copies = []
    for m, part in enumerate(parts):
        at = pl.multiple_of((place_ref[0] ^ m) * rows, rows)
        copies.append(pltpu.make_async_copy(part, full_ref.at[pl.ds(at, rows), :], sem.at[m]))
    return copies


def load_parts(place_ref, parts, full_ref, sem):
    for copy in part_copies(place_ref, parts, full_ref, sem):
        copy.start()


def wait_parts(place_ref, parts, full_ref, sem):
    @pl.when(pl.program_id(0) == 0)
    def _():
        for copy in part_copies(place_ref, parts, full_ref, sem):
            copy.wait()


GAIN, BIAS, MIX, FIRST = 0, 1, 2, 8


def mix_forward(
    rank, x_ref, rows_ref, own_ref, wn_ref, ww_ref, fn_ref, fw_ref,
    ones_ref, start_ref, place_ref, part0, part1, part2, part3, *refs,
):
    (
        gated_ref, xk_ref, xv_ref, xr_ref, xg_ref, r_ref, k_ref, v_ref, w_ref, graw_ref, wkv_ref, lm_ref, dm_ref,
        ends_ref, normed_ref, delta_ref, carry_ref, state_ref, four_ref, sem,
    ) = refs[-20:]
    step = pl.program_id(0)
    length, width = x_ref.shape
    own = own_ref.shape[1]
    heads = own // HEAD

    @pl.when(step == 0)
    def _():
        carry_ref[...] = jnp.broadcast_to(rows_ref[FIRST : FIRST + 1, :], carry_ref.shape)
        state_ref[...] = spread(start_ref[...], ones_ref[...].astype(F32))
        load_parts(place_ref, (part0, part1, part2, part3), four_ref, sem)

    mean, scale = row_stats(x_ref)
    first = iota((length, CHUNK), 0) == 0
    narrow = jnp.zeros((length, wn_ref.shape[0]), F32)
    for at in range(0, width, CHUNK):
        c = slice(at, at + CHUNK)
        normed = (x_ref[:, c].astype(F32) - mean) * scale * rows_ref[GAIN : GAIN + 1, c] + rows_ref[BIAS : BIAS + 1, c]
        delta = jnp.where(first, carry_ref[0:1, c], pltpu.roll(normed, 1, 0)) - normed
        carry_ref[0:1, c] = normed[length - 1 : length, :]
        normed_ref[:, c] = normed
        delta_ref[:, c] = delta
        narrow = narrow + nt(normed + delta * rows_ref[MIX : MIX + 1, c], wn_ref[:, c])
    middle = jnp.tanh(narrow)
    lm_ref[...] = middle
    blocks = rank_blocks(middle, rank)
    decay_in = jnp.zeros((length, fn_ref.shape[0]), F32)
    for at in range(0, width, CHUNK):
        c = slice(at, at + CHUNK)
        normed, delta = normed_ref[:, c], delta_ref[:, c]
        modifiers = nn(blocks, ww_ref[:, c])
        for j, ref in enumerate((None, xk_ref, xv_ref, xr_ref, xg_ref)):
            modifier = modifiers[j * length : (j + 1) * length, :]
            mixed = (normed + delta * (rows_ref[MIX + 1 + j : MIX + 2 + j, c] + modifier)).astype(BF16)
            if ref is None:
                decay_in = decay_in + nt(mixed, fn_ref[:, c])
            else:
                ref[:, c] = mixed
    decay_mid = jnp.tanh(decay_in)
    dm_ref[...] = decay_mid
    w = -jnp.exp(own_ref[0:1, :] + nn(decay_mid, fw_ref[...]))
    w_ref[...] = w
    wait_parts(place_ref, (part0, part1, part2, part3), four_ref, sem)
    r = nn(xr_ref[...], four_ref[:, :own]).astype(BF16)
    k = nn(xk_ref[...], four_ref[:, own : 2 * own]).astype(BF16)
    v = nn(xv_ref[...], four_ref[:, 2 * own : 3 * own]).astype(BF16)
    graw = nn(xg_ref[...], four_ref[:, 3 * own :])
    r_ref[...], k_ref[...], v_ref[...], graw_ref[...] = r, k, v, graw

    ones = ones_ref[...]
    for at in range(0, length, TOKENS):
        one_chunk(
            slice(at, at + TOKENS), r, k, v, w, graw, heads, ones, own_ref, wkv_ref, gated_ref, ends_ref.at[at // TOKENS],
            state_ref,
        )


def one_chunk(c, r, k, v, w, graw, heads, ones, own_ref, wkv_ref, gated_ref, end_ref, state_ref):
    v, w, graw = v[c, :], w[c, :], graw[c, :]
    rf, kf, vf = r[c, :].astype(F32), k[c, :].astype(F32), v.astype(F32)
    length = w.shape[0]
    levels, before, after, total = pyramid(w)
    row, col = iota((length, length), 0), iota((length, length), 1)
    apart = jnp.where(row > col, row ^ col, 0)
    scores = [jnp.zeros((length, length), F32)] * heads
    for half, upper, exponent in levels:
        scaled = jnp.where(upper, rf, kf) * jnp.exp(exponent)
        flat = scaled.astype(BF16)
        here = (apart >= half) & (apart < 2 * half)
        for head, one in enumerate(split_heads(scaled, heads)):
            scores[head] = jnp.where(here, nt(one, flat), scores[head])
    wkv = nn(jnp.concatenate([s.astype(BF16) for s in scores], 1), jnp.concatenate(split_heads(vf, heads), 0))
    state = state_ref[...]
    wkv = wkv + nt(rf * jnp.exp(before), state) + head_sum(rf * own_ref[1:2, :] * kf, ones) * vf
    wkv_ref[c, :] = wkv
    state = state * jnp.exp(total[0:1, :]) + tn(v, kf * jnp.exp(after)) * ones.astype(F32)
    state_ref[...] = state
    end_ref[...] = compact(state)

    center = wkv - head_sum(wkv, ones) / HEAD
    variance = head_sum(center * center, ones) / HEAD
    grouped = center * lax.rsqrt(variance + GROUP_EPSILON) * own_ref[2:3, :] + own_ref[3:4, :]
    gated_ref[c, :] = (grouped * graw * jax.nn.sigmoid(graw)).astype(BF16)


def state_cotangent(place_ref, mine_ref, other_ref, own, i):
    if mine_ref.dtype == F32:
        return mine_ref[i]
    tile = pl.num_programs(0) - 1 - pl.program_id(0)
    is_mine = tile // (pl.num_programs(0) // 2) == place_ref[1]
    wide = 2 * own
    parts = []
    for at in range(0, mine_ref.shape[2], wide):
        q = pl.ds(pl.multiple_of(place_ref[1] * own + at, own), own)
        parts.append(jnp.where(is_mine, mine_ref[i, :, q].astype(F32), other_ref[i, :, q].astype(F32)))
    both = jnp.concatenate(parts, 0)
    return both[:HEAD] + both[HEAD:]


def wkv_backward(
    place_ref, d_ref, r_ref, k_ref, v_ref, w_ref, graw_ref, wkv_ref, dm_ref, w_out_ref, own_ref, ones_ref, sums_ref,
    start_ref, ends_ref, earlier_ref, adj_ref, *refs,
):
    own_sums_ref, decay_up_ref, dr_ref, dk_ref, dv_ref, dg_ref, dpre_ref, state_ref = refs[-8:]
    step = pl.program_id(0)
    length, own = r_ref.shape
    heads = own // HEAD
    ones = ones_ref[...]

    @pl.when(step == 0)
    def _():
        for ref in (state_ref, own_sums_ref, decay_up_ref):
            ref[...] = jnp.zeros_like(ref)

    reward, gain, bias = own_ref[1:2, :], own_ref[2:3, :], own_ref[3:4, :]
    wkv, graw, d_gated = wkv_ref[...], graw_ref[...], nt(d_ref[...], w_out_ref[...])
    center = wkv - head_sum(wkv, ones) / HEAD
    scale = lax.rsqrt(head_sum(center * center, ones) / HEAD + GROUP_EPSILON)
    normed = center * scale
    sigma = jax.nn.sigmoid(graw)
    d_grouped = d_gated * graw * sigma
    dg_ref[...] = (d_gated * (normed * gain + bias) * sigma * (1.0 + graw * (1.0 - sigma))).astype(BF16)
    d_normed = d_grouped * gain
    do = scale * (d_normed - head_sum(d_normed, ones) / HEAD - normed * (head_sum(d_normed * normed, ones) / HEAD))

    dob = do.astype(BF16)
    for i in reversed(range(length // TOKENS)):
        c = slice(i * TOKENS, (i + 1) * TOKENS)
        before = ends_ref[i - 1] if i else jnp.where(
            step == pl.num_programs(0) - 1, start_ref[...], earlier_ref[length // TOKENS - 1]
        )
        d_end = spread(state_cotangent(place_ref, adj_ref, refs[0], own, i), ones.astype(F32))
        one_chunk_backward(
            c, r_ref, k_ref, v_ref, w_ref, do[c, :], dob[c, :], before, d_end, heads, ones, reward, sums_ref,
            dr_ref, dk_ref, dv_ref, dpre_ref, own_sums_ref, state_ref,
        )
    decay_up_ref[...] += tn(dm_ref[...], dpre_ref[...])
    for i, part in enumerate((d_grouped * normed, d_grouped)):
        own_sums_ref[8 * i + 16 : 8 * i + 24, :] += fold(part)


def one_chunk_backward(
    c, r_ref, k_ref, v_ref, w_ref, do, dob, before_state, d_end, heads, ones, reward, sums_ref,
    dr_ref, dk_ref, dv_ref, dpre_ref, own_sums_ref, state_ref,
):
    rb, kb, vb = r_ref[c, :], k_ref[c, :], v_ref[c, :]
    length = rb.shape[0]
    same = ones.astype(F32)
    r, k, v, w = rb.astype(F32), kb.astype(F32), vb.astype(F32), w_ref[c, :]
    levels, before, after, total = pyramid(w)
    d_state = state_ref[...] + d_end
    state = spread(before_state, same)
    d_flat, flat = d_state.astype(BF16), state.astype(BF16)
    from_start, to_end, decay = jnp.exp(before), jnp.exp(after), jnp.exp(total[0:1, :])
    dr = from_start * nn(dob, flat)
    dk = to_end * nn(vb, d_flat)
    dv = nt(k * to_end, d_flat)
    through = [r * dr, k * dk]
    state_ref[...] = d_state * decay + tn(dob, r * from_start) * same
    whole = decay * jnp.sum(state * d_state, 0, keepdims=True)

    row, col = iota((length, length), 0), iota((length, length), 1)
    apart = row ^ col
    do_heads, v_heads = split_heads(do, heads), split_heads(v, heads)
    d_scores = [
        jnp.where(row > col, nt(do_heads[h], vb), jnp.where(row < col, nt(v_heads[h], dob), 0.0)).astype(BF16)
        for h in range(heads)
    ]
    scores = [jnp.zeros((length, length), F32)] * heads
    for half, upper, exponent in levels:
        factor = jnp.exp(exponent)
        scaled = jnp.where(upper, r, k) * factor
        mine = split_heads(scaled, heads)
        here = (apart >= half) & (apart < 2 * half)
        late = here & (row < col)
        for h in range(heads):
            scores[h] = jnp.where(late, nt(mine[h], scaled), scores[h])
        pulled = nn(
            jnp.concatenate([jnp.where(here, d, 0.0).astype(BF16) for d in d_scores], 1), jnp.concatenate(mine, 0)
        )
        if half > 1:
            through.append(scaled * pulled)
        pulled = pulled * factor
        dr = dr + jnp.where(upper, pulled, 0.0)
        dk = dk + jnp.where(upper, 0.0, pulled)
    dv = dv + nn(jnp.concatenate([s.astype(BF16) for s in scores], 1), jnp.concatenate(do_heads, 0))
    met = head_sum(v * do, ones)
    dr = dr + reward * k * met
    dk = dk + reward * r * met
    dv = dv + head_sum(r * reward * k, ones) * do
    d_log = whole + nn(sums_ref[...], jnp.concatenate([q.astype(BF16) for q in through], 0))
    d_pre = d_log * w
    dr_ref[c, :], dk_ref[c, :], dv_ref[c, :] = dr.astype(BF16), dk.astype(BF16), dv.astype(BF16)
    dpre_ref[c, :] = d_pre
    for i, part in enumerate((d_pre, r * k * met)):
        own_sums_ref[8 * i : 8 * i + 8, :] += fold(part)


def sum_table(length):
    row, col = np.arange(length)[:, None], np.arange(length)[None, :]
    tables = [col > row, col < row]
    half = 2
    while half < length:
        inside = (row // half) == (col // half)
        upper = (row // half) % 2 == 1
        tables.append(inside & np.where(upper, col > row, col < row))
        half *= 2
    return jnp.asarray(np.concatenate(tables, 1), BF16)


def mix_backward(rank, halves, *refs):
    (
        place_ref, x_ref, edge_ref, rows_ref, lm_ref, dm_ref, dr_ref, dk_ref, dv_ref, dg_ref, dpre_ref,
        wn_ref, ww_ref, fn_ref, fw_ref, more_ref, part0, part1, part2, part3,
    ) = refs[:20]
    packed_ref = refs[-13 - halves]
    outs = refs[-12 - halves : -12]
    (
        row_sums_ref, up_ref, down_ref, decay_down_ref, dx_ref, carry_ref, sum_ref, coef_ref, normed_ref, delta_ref,
        four_ref, sem,
    ) = refs[-12:]
    step = pl.program_id(0)
    from_first = pl.num_programs(0) - 1 - step
    length, width = x_ref.shape

    @pl.when(step == 0)
    def _():
        load_parts(place_ref, (part0, part1, part2, part3), four_ref, sem)
        for ref in (carry_ref, row_sums_ref, up_ref, down_ref, decay_down_ref):
            ref[...] = jnp.zeros_like(ref)

    own = dr_ref.shape[1]
    mean, scale = row_stats(x_ref)
    edge = edge_ref.shape[0]
    edge_mean, edge_scale = row_stats(edge_ref)
    middle, decay_mid = lm_ref[...], dm_ref[...]
    blocks = rank_blocks(middle, rank)
    d_pre = dpre_ref[...]
    d_decay = (nt(d_pre, fw_ref[...]) * (1.0 - decay_mid * decay_mid)).astype(BF16)
    sources = ((d_decay, None), (dk_ref[...], own), (dv_ref[...], 2 * own), (dr_ref[...], 0), (dg_ref[...], 3 * own))
    first = iota((length, CHUNK), 0) == 0
    last = iota((length, CHUNK), 0) == length - 1
    d_mid = jnp.zeros((5 * length, wn_ref.shape[0]), F32)
    wait_parts(place_ref, (part0, part1, part2, part3), four_ref, sem)
    for at in range(0, width, CHUNK):
        c = slice(at, at + CHUNK)
        gain, bias = rows_ref[GAIN : GAIN + 1, c], rows_ref[BIAS : BIAS + 1, c]
        normed = (x_ref[:, c].astype(F32) - mean) * scale * gain + bias
        edge_normed = (edge_ref[:, c].astype(F32) - edge_mean) * edge_scale * gain + bias
        before = jnp.where(from_first == 0, rows_ref[FIRST : FIRST + 1, c], edge_normed[edge - 1 : edge, :])
        delta = jnp.where(first, before, pltpu.roll(normed, 1, 0)) - normed
        normed_ref[:, c] = normed
        delta_ref[:, c] = delta
        modifiers = nn(blocks, ww_ref[:, c])
        total = jnp.zeros_like(normed)
        by_coef = jnp.zeros_like(normed)
        d_mods = []
        for j, (d, begin) in enumerate(sources):
            d_mixed = nt(d, four_ref[c, begin : begin + own]) if j else nn(d, fn_ref[:, c])
            coef = rows_ref[MIX + 1 + j : MIX + 2 + j, c] + modifiers[j * length : (j + 1) * length, :]
            if j == 0:
                decay_down_ref[:, c] += tn(d_decay, normed + delta * coef)
            d_mod = delta * d_mixed
            row_sums_ref[8 * (MIX + 1 + j) : 8 * (MIX + 2 + j), c] += fold(d_mod)
            d_mods.append(d_mod.astype(BF16))
            total = total + d_mixed
            by_coef = by_coef + d_mixed * coef
        d_mods = jnp.concatenate(d_mods, 0)
        up_ref[:, c] += tn(blocks, d_mods)
        d_mid = d_mid + nt(d_mods, ww_ref[:, c])
        sum_ref[:, c] = total
        coef_ref[:, c] = by_coef
    lane = iota(middle.shape, 1) // rank
    d_low = jnp.zeros_like(middle)
    for j in range(5):
        d_low = jnp.where(lane == j, d_mid[j * length : (j + 1) * length, :], d_low)
    d_low = (d_low * (1.0 - middle * middle)).astype(BF16)
    sum_g = jnp.zeros((length, CHUNK), F32)
    sum_gn = jnp.zeros((length, CHUNK), F32)
    for at in range(0, width, CHUNK):
        c = slice(at, at + CHUNK)
        normed, delta = normed_ref[:, c], delta_ref[:, c]
        mix = rows_ref[MIX : MIX + 1, c]
        d_in = nn(d_low, wn_ref[:, c])
        down_ref[:, c] += tn(d_low, normed + delta * mix)
        row_sums_ref[8 * MIX : 8 * MIX + 8, c] += fold(delta * d_in)
        d_delta = coef_ref[:, c] + d_in * mix
        above = jnp.where(last, carry_ref[0:1, c], pltpu.roll(d_delta, length - 1, 0))
        carry_ref[0:1, c] = d_delta[0:1, :]
        d_normed = sum_ref[:, c] + d_in - d_delta + above
        unit = (x_ref[:, c].astype(F32) - mean) * scale
        row_sums_ref[8 * GAIN : 8 * GAIN + 8, c] += fold(d_normed * unit)
        row_sums_ref[8 * BIAS : 8 * BIAS + 8, c] += fold(d_normed)
        g = d_normed * rows_ref[GAIN : GAIN + 1, c]
        sum_g = sum_g + g
        sum_gn = sum_gn + g * unit
        sum_ref[:, c] = g
    mean_g = jnp.sum(sum_g, 1, keepdims=True) / width
    mean_gn = jnp.sum(sum_gn, 1, keepdims=True) / width
    for at in range(0, width, CHUNK):
        c = slice(at, at + CHUNK)
        unit = (x_ref[:, c].astype(F32) - mean) * scale
        dx_ref[:, c] = (scale * (sum_ref[:, c] - mean_g - unit * mean_gn)).astype(BF16)
    store_half(place_ref, dx_ref, outs, from_first)

    @pl.when(step == pl.num_programs(0) - 1)
    def _():
        at = 16
        packed_ref[0:at, :] = jnp.zeros((at, width), BF16)
        for i in range(8):
            packed_ref[i : i + 1, :] = jnp.sum(row_sums_ref[8 * i : 8 * i + 8, :], 0, keepdims=True).astype(BF16)
        more = more_ref.shape[0]
        decays = packed_ref.shape[0] - at - 10 * rank - more
        for ref, size in ((down_ref, 5 * rank), (up_ref, 5 * rank), (decay_down_ref, decays), (more_ref, more)):
            packed_ref[at : at + size, :] = ref[0:size, :].astype(BF16)
            at += size


def whole(a):
    return pl.BlockSpec(a.shape, lambda t: (0,) * a.ndim)


def params(**more):
    return pltpu.CompilerParams(
        dimension_semantics=("arbitrary",), vmem_limit_bytes=VMEM, **more
    )


def light():
    return pl.CostEstimate(flops=0, bytes_accessed=0, transcendentals=0)


def pinned(pins):
    return [pl.BlockSpec(memory_space=pl.ANY)] * len(pins)


def part_specs(parts):
    return [pl.BlockSpec(memory_space=pltpu.SMEM)] + [pl.BlockSpec(memory_space=pl.ANY)] * len(parts)


def part_scratch(parts):
    rows, columns = parts[0].shape
    return [pltpu.VMEM((len(parts) * rows, columns), BF16), pltpu.SemaphoreType.DMA((len(parts),))]


def call_forward(rank, length, x, rows, own, wn, ww, fn, fw, ones, start, place, parts, pins):
    tokens, width = x.shape
    cw = own.shape[1]
    count = tokens // length
    tile = lambda n: pl.BlockSpec((length, n), lambda t: (t, 0))
    shape = lambda n, dtype: jax.ShapeDtypeStruct((tokens, n), dtype)
    fixed = (rows, own, wn, ww, fn, fw, ones, start)
    return pl.pallas_call(
        lambda *refs: mix_forward(rank, *refs),
        grid=(count,),
        in_specs=[tile(width)] + [whole(a) for a in fixed] + part_specs(parts) + pinned(pins),
        out_specs=[tile(cw)] + [tile(width)] * 4 + [tile(cw)] * 6 + [tile(wn.shape[0]), tile(fn.shape[0])]
        + [pl.BlockSpec((length // TOKENS, HEAD, cw), lambda t: (t, 0, 0))],
        out_shape=[shape(cw, BF16)] + [shape(width, BF16)] * 4 + [shape(cw, BF16)] * 3 + [shape(cw, F32)] * 3
        + [shape(wn.shape[0], F32), shape(fn.shape[0], F32), jax.ShapeDtypeStruct((tokens // TOKENS, HEAD, cw), F32)],
        scratch_shapes=[
            pltpu.VMEM((length, width), F32), pltpu.VMEM((length, width), F32), pltpu.VMEM((8, width), F32),
            pltpu.VMEM((cw, cw), F32),
        ]
        + part_scratch(parts),
        compiler_params=params(),
        cost_estimate=light(),
        name="mix_forward",
    )(x, *fixed, place, *parts, *pins)


def two_halves(tokens, width, length, seqs, backward=False):
    half = tokens // length // 2
    order = (lambda t: tokens // length - 1 - t) if backward else (lambda t: t)
    if seqs != 2:
        return [pl.BlockSpec((length, width), lambda t, place: (order(t), 0))], [jax.ShapeDtypeStruct((tokens, width), BF16)]
    mine = lambda t, place: (jnp.clip(order(t) - place[1] * half, 0, half - 1), 0)
    other = lambda t, place: (jnp.clip(order(t) - (1 - place[1]) * half, 0, half - 1), 0)
    return (
        [pl.BlockSpec((length, width), mine), pl.BlockSpec((length, width), other)],
        [jax.ShapeDtypeStruct((tokens // 2, width), BF16)] * 2,
    )


def store_half(place_ref, value_ref, outs, tile=None):
    if len(outs) == 1:
        outs[0][...] = value_ref[...]
        return
    tile = pl.program_id(0) if tile is None else tile
    is_mine = tile // (pl.num_programs(0) // 2) == place_ref[1]

    @pl.when(is_mine)
    def _():
        outs[0][...] = value_ref[...]

    @pl.when(jnp.logical_not(is_mine))
    def _():
        outs[1][...] = value_ref[...]


def ffn_forward(halves, place_ref, x_ref, edge_ref, rows_ref, w_all, *refs):
    key_ref, recept_ref, hidden_ref, squared_ref = refs[-7 - halves : -3 - halves]
    outs = refs[-3 - halves : -3]
    w_ref, value_ref, sem = refs[-3:]
    length, width = x_ref.shape
    units = hidden_ref.shape[1]
    edge = edge_ref.shape[0]
    load = pltpu.make_async_copy(w_all, w_ref, sem)

    @pl.when(pl.program_id(0) == 0)
    def _():
        load.start()

    first = iota((length, CHUNK), 0) == 0
    for at in range(0, width, CHUNK):
        c = slice(at, at + CHUNK)
        normed = x_ref[:, c].astype(F32)
        before = jnp.where(pl.program_id(0) == 0, rows_ref[2:3, c], edge_ref[edge - 1 : edge, c].astype(F32))
        delta = jnp.where(first, before, pltpu.roll(normed, 1, 0)) - normed
        key_ref[:, c] = (normed + delta * rows_ref[3:4, c]).astype(BF16)
        recept_ref[:, c] = (normed + delta * rows_ref[4:5, c]).astype(BF16)

    @pl.when(pl.program_id(0) == 0)
    def _():
        load.wait()

    hidden = jnp.maximum(nn(key_ref[...], w_ref[:, :units]), 0.0)
    hidden_ref[...] = hidden
    squared = (hidden * hidden).astype(BF16)
    squared_ref[...] = squared
    for at in range(0, width, CHUNK):
        c = slice(at, at + CHUNK)
        value_ref[:, c] = nt(squared, w_ref[c, units:]).astype(BF16)
    store_half(place_ref, value_ref, outs)


def call_ffn_forward(x, rows, w, place, seqs, pins):
    tokens, width = x.shape
    length, edge = 256, 16
    units = w.shape[1] // 2
    tile = lambda n: pl.BlockSpec((length, n), lambda t, place: (t, 0))
    shape = lambda n, dtype: jax.ShapeDtypeStruct((tokens, n), dtype)
    specs, shapes = two_halves(tokens, width, length, seqs)
    return pl.pallas_call(
        lambda *refs: ffn_forward(len(specs), *refs),
        grid_spec=pltpu.PrefetchScalarGridSpec(
            num_scalar_prefetch=1,
            grid=(tokens // length,),
            in_specs=[
                tile(width),
                pl.BlockSpec((edge, width), lambda t, place: (jnp.maximum(t * (length // edge) - 1, 0), 0)),
                pl.BlockSpec(rows.shape, lambda t, place: (0, 0)),
            ]
            + pinned([w]) + pinned(pins),
            out_specs=[tile(width)] * 2 + [tile(units)] * 2 + specs,
            scratch_shapes=[
                pltpu.VMEM(w.shape, BF16), pltpu.VMEM((length, width), BF16), pltpu.SemaphoreType.DMA,
            ],
        ),
        out_shape=[shape(width, BF16)] * 2 + [shape(units, F32), shape(units, BF16)] + shapes,
        compiler_params=params(),
        cost_estimate=light(),
        name="ffn_forward",
    )(place, x, x, rows, w, *pins)


def call_ffn_gate(recept, cot_mine, cot_other, gate, place, pins):
    tokens, width = recept.shape
    length = 256
    half = gate.shape[1]
    step = min(CHUNK, half)
    rows = 128
    tiles, per = tokens // length, length // rows
    split = cot_mine.shape[0] < tiles * per

    def kernel(place_ref, recept_ref, mine_ref, other_ref, gate_ref, *refs):
        recept = recept_ref[...]
        is_mine = pl.program_id(0) // (tiles // 2) == place_ref[1]
        for at in range(0, half, step):
            c = slice(at, at + step)
            gate = jax.nn.sigmoid(nn(recept, gate_ref[:, c]))
            for i in range(per):
                r = slice(i * rows, (i + 1) * rows)
                cot = jnp.where(is_mine, mine_ref[i, :, c].astype(F32), other_ref[i, :, c].astype(F32))
                refs[-1][r, c] = (cot * gate[r, :]).astype(BF16)

    column = (lambda place: place[1]) if half < width else (lambda place: 0)

    def cot_spec(core):
        if not split:
            return pl.BlockSpec((per, rows, half), lambda t, place: (t, 0, column(place)))
        at = lambda t, place: jnp.clip(t - core(place) * (tiles // 2), 0, tiles // 2 - 1)
        return pl.BlockSpec((per, rows, half), lambda t, place: (at(t, place), 0, column(place)))

    return pl.pallas_call(
        kernel,
        grid_spec=pltpu.PrefetchScalarGridSpec(
            num_scalar_prefetch=1,
            grid=(tiles,),
            in_specs=[
                pl.BlockSpec((length, width), lambda t, place: (t, 0)),
                cot_spec(lambda place: place[1]), cot_spec(lambda place: 1 - place[1]),
                pl.BlockSpec(gate.shape, lambda t, place: (0, 0), pipeline_mode=pl.Buffered(1)),
            ]
            + pinned(pins),
            out_specs=pl.BlockSpec((length, half), lambda t, place: (t, 0)),
        ),
        out_shape=jax.ShapeDtypeStruct((tokens, half), BF16),
        compiler_params=params(),
        cost_estimate=light(),
        name="ffn_gate",
    )(place, recept, cot_mine, cot_other, gate, *pins)


def ffn_backward(halves, place_ref, mine_ref, other_ref, hidden_ref, w_all, *refs):
    d_hidden_ref = refs[-5 - halves]
    outs = refs[-4 - halves : -4]
    w_ref, d_values_ref, value_ref, sem = refs[-4:]
    width = d_values_ref.shape[1]
    half = mine_ref.shape[1]
    units = hidden_ref.shape[1]
    load = pltpu.make_async_copy(w_all, w_ref, sem)

    @pl.when(pl.program_id(0) == 0)
    def _():
        load.start()

    cores = ((mine_ref, place_ref[1]), (other_ref, 1 - place_ref[1])) if half < width else ((mine_ref, 0),)
    for ref, core in cores:
        d_values_ref[:, pl.ds(pl.multiple_of(core * half, half), half)] = ref[...]

    @pl.when(pl.program_id(0) == 0)
    def _():
        load.wait()

    d_hidden = (nn(d_values_ref[...], w_ref[:, units:]) * 2.0 * hidden_ref[...]).astype(BF16)
    d_hidden_ref[...] = d_hidden
    for at in range(0, width, CHUNK):
        c = slice(at, at + CHUNK)
        value_ref[:, c] = nt(d_hidden, w_ref[c, :units]).astype(BF16)
    store_half(place_ref, value_ref, outs)


def call_ffn_backward(mine, other, hidden, w, place, seqs, pins):
    tokens, half = mine.shape
    width = w.shape[0]
    length = 256
    units = hidden.shape[1]
    tile = lambda n: pl.BlockSpec((length, n), lambda t, place: (t, 0))
    shape = lambda n: jax.ShapeDtypeStruct((tokens, n), BF16)
    specs, shapes = two_halves(tokens, width, length, seqs)
    return pl.pallas_call(
        lambda *refs: ffn_backward(len(specs), *refs),
        grid_spec=pltpu.PrefetchScalarGridSpec(
            num_scalar_prefetch=1,
            grid=(tokens // length,),
            in_specs=[tile(half), tile(half), tile(units)] + pinned([w]) + pinned(pins),
            out_specs=[tile(units)] + specs,
            scratch_shapes=[
                pltpu.VMEM(w.shape, BF16), pltpu.VMEM((length, width), BF16), pltpu.VMEM((length, width), BF16),
                pltpu.SemaphoreType.DMA,
            ],
        ),
        out_shape=[shape(units)] + shapes,
        compiler_params=params(),
        cost_estimate=light(),
        name="ffn_backward",
    )(place, mine, other, hidden, w, *pins)


def call_grad(x, d, pins):
    tokens, width = x.shape
    units = d.shape[1]
    columns = 512 if tokens <= 1024 else 256

    def kernel(x_ref, d_ref, *refs):
        refs[-1][...] = tn(x_ref[...], d_ref[...]).astype(BF16)

    return pl.pallas_call(
        kernel,
        grid=(width // columns,),
        in_specs=[
            pl.BlockSpec((tokens, columns), lambda t: (0, t)),
            pl.BlockSpec(d.shape, lambda t: (0, 0), pipeline_mode=pl.Buffered(1)),
        ]
        + pinned(pins),
        out_specs=pl.BlockSpec((columns, units), lambda t: (t, 0)),
        out_shape=jax.ShapeDtypeStruct((width, units), BF16),
        compiler_params=params(),
        cost_estimate=light(),
        name="grad",
    )(x, d, *pins)


def call_grad_halves(place, mine, other, d):
    tokens, half = mine.shape
    units = d.shape[1]
    columns = 512
    per = half // columns

    def kernel(place_ref, mine_ref, other_ref, d_ref, out_ref):
        @pl.when(pl.program_id(0) < per)
        def _():
            out_ref[...] = tn(mine_ref[...], d_ref[...]).astype(BF16)

        @pl.when(pl.program_id(0) >= per)
        def _():
            out_ref[...] = tn(other_ref[...], d_ref[...]).astype(BF16)

    def to(t, place):
        return (jnp.where(t < per, place[1] * per + t, (1 - place[1]) * per + t - per), 0)

    return pl.pallas_call(
        kernel,
        grid_spec=pltpu.PrefetchScalarGridSpec(
            num_scalar_prefetch=1,
            grid=(2 * per,),
            in_specs=[
                pl.BlockSpec((tokens, columns), lambda t, place: (0, jnp.minimum(t, per - 1))),
                pl.BlockSpec((tokens, columns), lambda t, place: (0, jnp.maximum(t - per, 0))),
                pl.BlockSpec(d.shape, lambda t, place: (0, 0), pipeline_mode=pl.Buffered(1)),
            ],
            out_specs=pl.BlockSpec((columns, units), to),
        ),
        out_shape=jax.ShapeDtypeStruct((2 * half, units), BF16),
        compiler_params=params(),
        cost_estimate=light(),
        name="grad_halves",
    )(place, mine, other, d)


def call_grads(xs, ds, gated, d_att, segs, pins):
    tokens, width = d_att.shape
    cw = gated.shape[1]
    rows, count = width // segs, len(xs)
    columns = 512 if tokens <= 1024 else 128
    per, cut = rows // columns, cw // segs

    def kernel(*refs):
        x_refs, d_refs, gated_ref, att_ref, out_ref = refs[:count], refs[count : 2 * count], refs[-3 - len(pins)], refs[-2 - len(pins)], refs[-1]
        s, at = pl.program_id(0) // per, pl.program_id(0) % per
        for j in range(count):
            out_ref[s, j, pl.ds(pl.multiple_of(at * columns, columns), columns), :] = tn(
                x_refs[j][...], d_refs[j][...]
            ).astype(BF16)
        result = tn(gated_ref[...], att_ref[...]).astype(BF16)
        each = columns // cw
        for i in range(each):
            to = pl.multiple_of((pl.program_id(0) * each + i) * cut, cut)
            for m in range(segs):
                out_ref[m, count, pl.ds(to, cut), :] = result[m * cut : (m + 1) * cut, i * cw : (i + 1) * cw]

    block = pl.BlockSpec((tokens, columns), lambda t: (0, t))
    fixed = pl.BlockSpec((tokens, cw), lambda t: (0, 0), pipeline_mode=pl.Buffered(1))
    shape = (segs, count + 1, rows, cw)
    return pl.pallas_call(
        kernel,
        grid=(width // columns,),
        in_specs=[block] * count + [fixed] * count + [fixed, block] + pinned(pins),
        out_specs=pl.BlockSpec(shape, lambda t: (0, 0, 0, 0)),
        out_shape=jax.ShapeDtypeStruct(shape, BF16),
        compiler_params=params(),
        cost_estimate=light(),
        name="grads",
    )(*xs, *ds, gated, d_att, *pins)


def call_ffn_norm(x, blocks, rows, pins):
    length, width = x.shape
    count = blocks.shape[0]

    def kernel(x_ref, blocks_ref, rows_ref, *refs):
        sum_ref, unit_ref, scale_ref, normed_ref, low_ref = refs[-5:]
        lanes = 128
        total = jnp.zeros((length, lanes), F32)
        for at in range(0, width, lanes):
            c = slice(at, at + lanes)
            value = x_ref[:, c].astype(F32)
            for i in range(count):
                value = value + blocks_ref[i, :, c].astype(F32)
            sum_ref[:, c] = value
            total = total + value
        mean = jnp.sum(total, 1, keepdims=True) / width
        total = jnp.zeros((length, lanes), F32)
        for at in range(0, width, lanes):
            center = sum_ref[:, at : at + lanes] - mean
            total = total + center * center
        scale = lax.rsqrt(jnp.sum(total, 1, keepdims=True) / width + LAYER_EPSILON)
        scale_ref[...] = jnp.broadcast_to(scale, scale_ref.shape)
        for at in range(0, width, lanes):
            c = slice(at, at + lanes)
            unit = (sum_ref[:, c] - mean) * scale
            unit_ref[:, c] = unit
            normed = unit * rows_ref[0:1, c] + rows_ref[1:2, c]
            normed_ref[:, c] = normed
            low_ref[:, c] = normed.astype(BF16)

    shape = lambda n, dtype: jax.ShapeDtypeStruct((length, n), dtype)
    return pl.pallas_call(
        kernel,
        grid=(1,),
        in_specs=[whole(x), whole(blocks), whole(rows)] + pinned(pins),
        out_specs=[pl.BlockSpec((length, n), lambda t: (0, 0)) for n in (width, width, 128, width, width)],
        out_shape=[shape(width, F32), shape(width, F32), shape(128, F32), shape(width, F32), shape(width, BF16)],
        compiler_params=params(),
        cost_estimate=light(),
        name="ffn_norm",
    )(x, blocks, rows, *pins)


def call_ffn_local(place, recept_in, blocks, cot, residual, gate_mine, gate_other, group, pins):
    length, width = recept_in.shape
    count, half = blocks.shape[0], gate_mine.shape[1]
    cw = width // group
    step = min(CHUNK, half)

    def kernel(place_ref, recept_ref, blocks_ref, cot_ref, residual_ref, mine_ref, other_ref, *refs):
        out_ref, cut_ref, d_ref, gate_ref = refs[-4:]
        recept = recept_ref[...]
        cores = ((mine_ref, place_ref[1]), (other_ref, 1 - place_ref[1])) if half < width else ((mine_ref, 0),)
        for ref, core in cores:
            for at in range(0, half, step):
                c = pl.ds(pl.multiple_of(core * half + at, step), step)
                gate = jax.nn.sigmoid(nn(recept, ref[:, at : at + step]))
                values = sum(blocks_ref[i, :, c].astype(F32) for i in range(count))
                out_ref[:, c] = (residual_ref[:, c] + gate * values).astype(BF16)
                gate_ref[:, c] = (cot_ref[:, c].astype(F32) * values * gate * (1.0 - gate)).astype(BF16)
        for i in range(group):
            cut_ref[i] = gate_ref[:, i * cw : (i + 1) * cw]
        for at in range(0, width, CHUNK):
            c = slice(at, at + CHUNK)
            d = jnp.zeros((length, CHUNK), F32)
            for ref, core in cores:
                d = d + nt(gate_ref[:, pl.ds(pl.multiple_of(core * half, half), half)], ref[c, :])
            d_ref[:, c] = d

    fixed = lambda a: pl.BlockSpec(a.shape, lambda t, place: (0,) * a.ndim)
    shapes = [(length, width), (group, length, cw), (length, width)]
    return pl.pallas_call(
        kernel,
        grid_spec=pltpu.PrefetchScalarGridSpec(
            num_scalar_prefetch=1,
            grid=(1,),
            in_specs=[fixed(a) for a in (recept_in, blocks, cot, residual, gate_mine, gate_other)] + pinned(pins),
            out_specs=[pl.BlockSpec(s, lambda t, place, n=len(s): (0,) * n) for s in shapes],
            scratch_shapes=[pltpu.VMEM((length, width), BF16)],
        ),
        out_shape=[jax.ShapeDtypeStruct(s, dtype) for s, dtype in zip(shapes, (BF16, BF16, F32))],
        compiler_params=params(),
        cost_estimate=light(),
        name="ffn_local",
    )(place, recept_in, blocks, cot, residual, gate_mine, gate_other, *pins)


def call_out(place, gated, own, parts, sender, seqs, pins):
    tokens, cw = gated.shape
    width = own.shape[1]
    length = 256
    specs, shapes = two_halves(tokens, width, length, seqs)

    def kernel(place_ref, gated_ref, own_ref, *refs):
        w_ref, value_ref = refs[-2:]

        @pl.when(pl.program_id(0) == 0)
        def _():
            received = refs[0][...]
            for ref in refs[1 : len(parts)]:
                received = received + ref[...]
            w_ref[...] = jnp.where(place_ref[2] == 1, own_ref[...], received)

        for at in range(0, width, CHUNK):
            c = slice(at, at + CHUNK)
            value_ref[:, c] = nn(gated_ref[...], w_ref[:, c]).astype(BF16)
        store_half(place_ref, value_ref, refs[-2 - len(specs) : -2])

    fixed = lambda a: pl.BlockSpec(a.shape, lambda t, place: (0, 0))

    return pl.pallas_call(
        kernel,
        grid_spec=pltpu.PrefetchScalarGridSpec(
            num_scalar_prefetch=1,
            grid=(tokens // length,),
            in_specs=[pl.BlockSpec((length, cw), lambda t, place: (t, 0))] + [fixed(a) for a in (own, *parts)]
            + pinned(pins),
            out_specs=specs + [pl.BlockSpec((cw, width), lambda t, place: (0, 0))],
            scratch_shapes=[pltpu.VMEM((length, width), BF16)],
        ),
        out_shape=shapes + [jax.ShapeDtypeStruct((cw, width), BF16)],
        compiler_params=params(),
        cost_estimate=light(),
        name="out_projection",
    )(jnp.concatenate([place, sender.reshape(1)]), gated, own, *parts, *pins)


def call_add(mine, other, pins):
    rows, width = mine.shape
    length = 256

    def kernel(a_ref, b_ref, *refs):
        refs[-1][...] = (a_ref[...].astype(F32) + b_ref[...].astype(F32)).astype(BF16)

    tile = pl.BlockSpec((length, width), lambda t: (t, 0))
    return pl.pallas_call(
        kernel,
        grid=(rows // length,),
        in_specs=[tile, tile] + pinned(pins),
        out_specs=tile,
        out_shape=jax.ShapeDtypeStruct((rows, width), BF16),
        compiler_params=params(),
        cost_estimate=light(),
        name="add",
    )(mine, other, *pins)


def call_combine(order, mine, other):
    count, rows, width = mine.shape

    def kernel(order_ref, mine_ref, other_ref, *outs):
        total = mine_ref[0].astype(F32) + other_ref[0].astype(F32)
        for k in range(count):

            @pl.when(pl.program_id(0) == k)
            def _():
                outs[k][...] = total.astype(outs[k].dtype)

    block = pl.BlockSpec((1, rows, width), lambda k, order: (order[k], 0, 0))
    return pl.pallas_call(
        kernel,
        grid_spec=pltpu.PrefetchScalarGridSpec(
            num_scalar_prefetch=1,
            grid=(count,),
            in_specs=[block, block],
            out_specs=[pl.BlockSpec((rows, width), lambda k, order: (0, 0))] * count,
        ),
        out_shape=[jax.ShapeDtypeStruct((rows, width), F32 if k == 0 else BF16) for k in range(count)],
        compiler_params=params(),
        cost_estimate=light(),
        name="combine",
    )(order, mine, other)


def call_wkv_backward(
    length, d, r, k, v, w, graw, wkv, dm, w_out, own, ones, sums, start, ends, adjoints, place, pins
):
    tokens, cw = r.shape
    count = tokens // length
    tile = lambda n: pl.BlockSpec((length, n), lambda t, place: (count - 1 - t, 0))
    fixed = lambda a: pl.BlockSpec(a.shape, lambda t, place: (0, 0))
    shape = lambda dtype: jax.ShapeDtypeStruct((tokens, cw), dtype)
    wide, per = dm.shape[1], length // TOKENS

    def folded(a, core):
        rows = a.shape[1] - TOKENS
        at = lambda t, place: jnp.clip(count - 1 - t - core(place) * (count // 2), 0, count // 2 - 1)
        return pl.BlockSpec((per, rows, a.shape[2]), lambda t, place: (at(t, place), TOKENS // rows, 0))

    if len(adjoints) == 2:
        states = [folded(adjoints[0], lambda place: place[1]), folded(adjoints[1], lambda place: 1 - place[1])]
    else:
        states = [pl.BlockSpec((per, HEAD, cw), lambda t, place: (count - 1 - t, 0, 0))]
    return pl.pallas_call(
        wkv_backward,
        grid_spec=pltpu.PrefetchScalarGridSpec(
            num_scalar_prefetch=1,
            grid=(count,),
            in_specs=[tile(d.shape[1])] + [tile(cw)] * 6 + [tile(wide)]
            + [fixed(a) for a in (w_out, own, ones, sums, start)]
            + [pl.BlockSpec((per, HEAD, cw), lambda t, place: (count - 1 - t, 0, 0))]
            + [pl.BlockSpec((per, HEAD, cw), lambda t, place: (jnp.maximum(count - 2 - t, 0), 0, 0))]
            + states + pinned(pins),
            out_specs=[pl.BlockSpec((32, cw), lambda t, place: (0, 0)), pl.BlockSpec((wide, cw), lambda t, place: (0, 0))]
            + [tile(cw)] * 5,
            scratch_shapes=[pltpu.VMEM((cw, cw), F32)],
        ),
        out_shape=[jax.ShapeDtypeStruct((32, cw), F32), jax.ShapeDtypeStruct((wide, cw), F32)]
        + [shape(BF16)] * 4 + [shape(F32)],
        compiler_params=params(),
        cost_estimate=light(),
        name="wkv_backward",
    )(place, d, r, k, v, w, graw, wkv, dm, w_out, own, ones, sums, start, ends, ends, *adjoints, *pins)


def call_mix_backward(
    rank, length, x, rows, lm, dm, dr, dk, dv, dg, dpre, wn, ww, fn, fw, more, place, parts, decays, seqs, pins
):
    tokens, width = x.shape
    cw = dr.shape[1]
    count = tokens // length
    edge = 16
    tile = lambda n: pl.BlockSpec((length, n), lambda t, place: (count - 1 - t, 0))
    before = pl.BlockSpec((edge, width), lambda t, place: (jnp.maximum((count - 1 - t) * (length // edge) - 1, 0), 0))
    fixed = lambda a: pl.BlockSpec(a.shape, lambda t, place: (0, 0))
    packed = 16 + 10 * rank + decays + more.shape[0]
    specs, shapes = two_halves(tokens, width, length, seqs, backward=True)
    return pl.pallas_call(
        lambda *refs: mix_backward(rank, len(specs), *refs),
        grid_spec=pltpu.PrefetchScalarGridSpec(
            num_scalar_prefetch=1,
            grid=(count,),
            in_specs=[tile(width), before, fixed(rows), tile(lm.shape[1]), tile(dm.shape[1])] + [tile(cw)] * 5
            + [fixed(a) for a in (wn, ww, fn, fw, more)] + pinned(parts) + pinned(pins),
            out_specs=[pl.BlockSpec((packed, width), lambda t, place: (0, 0))] + specs,
            scratch_shapes=[pltpu.VMEM((n, width), F32) for n in (8 * 8, wn.shape[0], wn.shape[0], fn.shape[0])]
            + [pltpu.VMEM((length, width), BF16), pltpu.VMEM((8, width), F32)]
            + [pltpu.VMEM((length, width), F32)] * 4 + part_scratch(parts),
        ),
        out_shape=[jax.ShapeDtypeStruct((packed, width), BF16)] + shapes,
        compiler_params=params(),
        cost_estimate=light(),
        name="mix_backward",
    )(place, x, x, rows, lm, dm, dr, dk, dv, dg, dpre, wn, ww, fn, fw, more, *parts, *pins)


def gather_group(block):
    return lax.all_gather(block, TP, axis=0, tiled=True)


SWAP = [(0, 1), (1, 0)]


def reduce_halves(mine, other, pins):
    total = call_add(mine, lax.ppermute(other, "seq", SWAP), pins)
    return reduce_chan(total), total


def reduce_chan(total):
    chans = lax.axis_size("chan")
    return lax.all_to_all(total.reshape(chans, -1, total.shape[1]), "chan", 0, 0, tiled=True)


def reduce_apart(parts):
    chans, at = lax.axis_size("chan"), lax.axis_index("chan")
    if len(parts) == 2:
        mine, other = parts[0], lax.ppermute(parts[1], "seq", SWAP)
    else:
        mine = lax.psum_scatter(parts[0], "seq", scatter_dimension=0, tiled=True)
        other = jnp.zeros_like(mine)
    order = ((at + jnp.arange(chans)) % chans).astype(jnp.int32)
    cut = lambda a: a.reshape(chans, -1, a.shape[1])
    total, *sent = call_combine(order, cut(mine), cut(other))
    came = [
        lax.ppermute(a, "chan", [(i, (i + k + 1) % chans) for i in range(chans)]) for k, a in enumerate(sent)
    ]
    return sum((a.astype(F32) for a in came), total), came


def add_up(blocks):
    return jnp.sum(blocks.astype(F32), 0)


def reduce_group(parts, pins=()):
    if len(parts) == 2:
        return reduce_halves(*parts, pins)
    total = lax.psum_scatter(parts[0], "seq", scatter_dimension=0, tiled=True)
    return reduce_chan(total), total


def after(a, before):
    corner = before[(slice(0, 1),) * before.ndim].reshape((1,) * a.ndim)
    return a + (corner.astype(F32) * 0.0).astype(a.dtype)


def after_all(a, others):
    for other in others:
        a = after(a, other)
    return a


def next_row(row, by):
    count = lax.axis_size(TP)
    return lax.ppermute(row, TP, [(i, i + by) for i in range(count) if 0 <= i + by < count])


def shift_down(values, first_row):
    return jnp.concatenate([first_row, values[:-1]], 0)


def unit_rows(values):
    center = values - jnp.mean(values, -1, keepdims=True)
    scale = lax.rsqrt(jnp.mean(center * center, -1, keepdims=True) + LAYER_EPSILON)
    return center * scale, scale


def on_device(
    sequence_elements,
    segment_predecessor_entries,
    opening_recurrences,
    first_layernorm_gain,
    first_layernorm_shift_term,
    lag_blend_coefficients,
    lag_narrowing_factor,
    lag_widening_factors,
    fading_exponent_baseline,
    fading_narrowing_factor,
    fading_widening_factor,
    present_reward,
    acceptor_projection,
    address_projection,
    content_projection,
    valve_projection,
    timemix_result_projection,
    subspace_cluster_gain,
    subspace_cluster_shift_term,
    second_layernorm_gain,
    second_layernorm_shift_term,
    feedforward_lag_blends,
    feedforward_address_projection,
    feedforward_acceptor_projection,
    feedforward_content_projection,
    result_adjoint,
    final_recurrence_adjoint,
):
    segs, seqs, chans = lax.axis_size("seg"), lax.axis_size("seq"), lax.axis_size("chan")
    group = seqs * chans
    p = lax.axis_index(TP)
    x = sequence_elements[0]
    length, width = x.shape
    tokens = group * length
    cw = width // group
    heads = cw // HEAD
    rank = lag_widening_factors.shape[1] // 5
    ranks, decays = 5 * rank, fading_widening_factor.shape[1]

    def columns(a, axis=-1):
        return lax.dynamic_slice_in_dim(a, p * cw, cw, axis % a.ndim)

    me, seg = lax.axis_index("seq"), lax.axis_index("seg")
    block = width // (segs * group)
    rows_seg = width // segs
    flips = [[(s, s ^ m) for s in range(segs)] for m in range(segs)]

    def seg_parts(a):
        return [a] + [lax.ppermute(a, "seg", flips[m]) for m in range(1, segs)]

    def own_part(a, axis):
        size = a.shape[axis] // seqs
        return lax.dynamic_slice_in_dim(a, me * size, size, axis)

    def reduce_segs(piece):
        sent = [piece(seg ^ m) for m in range(1, segs)]
        return sum((lax.ppermute(a, "seg", flips[m + 1]).astype(F32) for m, a in enumerate(sent)), piece(seg).astype(F32)), sent

    def reduce_rows(a):
        return lax.psum_scatter(a, "seg", scatter_dimension=0, tiled=True)

    x_all = gather_group(x)
    four = seg_parts(
        jnp.concatenate(
            [columns(a) for a in (acceptor_projection, address_projection, content_projection, valve_projection)], 1
        )
    )
    share = group // segs
    out_rows = after(lax.dynamic_slice_in_dim(timemix_result_projection, (p % share) * cw, cw, 0), four[-1])
    out_parts = [
        lax.ppermute(out_rows, ALL, [((j // share) * group + j, ((j // share) ^ m) * group + j) for j in range(group)])
        for m in range(1, segs)
    ]
    ffn_part = jnp.concatenate([own_part(a, 1) for a in (feedforward_address_projection, feedforward_content_projection)], 1)
    w_ffn = lax.all_gather(after_all(ffn_part, four[1:]), "seg", axis=0, tiled=True)
    cot = after(result_adjoint[0], x_all)
    adjoints = final_recurrence_adjoint[0, 0]
    if seqs == 2:
        adjoints = adjoints.reshape(HEAD, seqs, chans, cw).transpose(2, 0, 1, 3).reshape(chans, HEAD, seqs * cw)
        high = adjoints.astype(BF16)
        adjoints = jnp.concatenate([high, (adjoints - high.astype(F32)).astype(BF16)], 1)
        fold_rows = 2 * HEAD * seqs * cw // width
        adjoints = adjoints.reshape(chans, -1, fold_rows, seqs * cw).transpose(0, 2, 1, 3).reshape(chans, fold_rows, width)
        sent = jnp.concatenate([jnp.broadcast_to(cot[None], (chans, length, width)), adjoints], 1)
        cot_mine = lax.all_to_all(sent, "chan", 0, 0, tiled=True)
        cot_other = lax.ppermute(cot_mine, "seq", SWAP)

        adjoints = (cot_mine, cot_other)
    else:
        cot_mine = cot_other = gather_group(cot).reshape(group, length, width)
        adjoints = (lax.all_to_all(adjoints.reshape(HEAD, group, cw).transpose(1, 0, 2), TP, 0, 0, tiled=True),)

    rows = jnp.concatenate(
        [
            first_layernorm_gain[None], first_layernorm_shift_term[None], lag_blend_coefficients.T,
            segment_predecessor_entries[0, 0][None], fading_exponent_baseline[None], present_reward[None],
            subspace_cluster_gain[None], subspace_cluster_shift_term[None], jnp.zeros((11, width), F32),
        ]
    )
    own = lax.dynamic_slice(rows, (FIRST + 1, p * cw), (8, cw))
    wn, ww, fn = lag_narrowing_factor.T, lag_widening_factors.T, fading_narrowing_factor.T
    fw = columns(fading_widening_factor.T)
    head_of = np.arange(cw) // HEAD
    ones = jnp.asarray(head_of[:, None] == head_of[None, :], BF16)
    start = columns(opening_recurrences[0])
    place = jnp.stack([seg, me]).astype(jnp.int32)

    gated, xk, xv, xr, xg, r, k, v, w, graw, wkv, lm, dm, ends = call_forward(
        rank, 2 * length, x_all, rows, own, wn, ww, fn, fw, ones, start, place, four, ()
    )
    *out, w_out = call_out(
        place, gated, out_rows, out_parts, (seg == p // share).astype(jnp.int32), seqs, [cot_mine]
    )
    out_blocks, _ = reduce_group(out)

    mix_key, mix_recept = feedforward_lag_blends[:, 0], feedforward_lag_blends[:, 1]
    first_row = segment_predecessor_entries[0, 1][None]
    ffn_rows = jnp.concatenate(
        [second_layernorm_gain[None], second_layernorm_shift_term[None], first_row, feedforward_lag_blends.T, jnp.zeros((3, width), F32)]
    )
    residual, ffn_unit, ffn_scale, ffn_normed, normed_low = call_ffn_norm(
        x, out_blocks, ffn_rows, [w_ffn]
    )
    ffn_scale = ffn_scale[:, :1]
    normed_all = gather_group(normed_low)
    gate_part = after(own_part(feedforward_acceptor_projection, 1), normed_all)
    gate_mine = lax.all_gather(gate_part, "seg", axis=0, tiled=True)
    before = lax.dynamic_slice_in_dim(normed_all, jnp.maximum(p * length - 1, 0), 1, 0).astype(F32)
    previous = jnp.where(p == 0, first_row, before)
    ffn_delta = shift_down(ffn_normed, previous) - ffn_normed
    recept_in = (ffn_normed + ffn_delta * mix_recept).astype(BF16)
    cot = result_adjoint[0].astype(F32)
    if seqs == 2:
        gate_other = lax.ppermute(gate_mine, "seq", SWAP)
    else:
        gate_mine = gate_other = lax.all_gather(gate_mine, "seq", axis=1, tiled=True)

    key_in, recept_all, hidden, squared, *values = call_ffn_forward(normed_all, ffn_rows, w_ffn, place, seqs, ())
    value_blocks, sent = reduce_group(values)
    d_mine = call_ffn_gate(recept_all, cot_mine, cot_other, gate_mine, place, [sent])
    d_other = lax.ppermute(d_mine, "seq", SWAP) if seqs == 2 else d_mine
    if seqs == 2:
        grad_ffn_value = call_grad_halves(place, d_mine, d_other, squared)
    else:
        grad_ffn_value = call_grad(d_mine, squared, ())
    d_hidden, *d_key = call_ffn_backward(
        d_mine, d_other, hidden, w_ffn, place, seqs, [value_blocks, grad_ffn_value]
    )
    grad_ffn_value = reduce_rows(grad_ffn_value)
    key_blocks, _ = reduce_group(d_key)

    output, d_gate_cut, d_fr = call_ffn_local(
        place, recept_in, value_blocks, result_adjoint[0], residual, gate_mine, gate_other, group, ()
    )
    d_fk = add_up(key_blocks)
    d_fdelta = d_fk * mix_key + d_fr * mix_recept
    d_normed = d_fk + d_fr - d_fdelta + jnp.concatenate([d_fdelta[1:], next_row(d_fdelta[:1], -1)], 0)
    g = d_normed * second_layernorm_gain
    d_residual = cot + ffn_scale * (
        g - jnp.mean(g, -1, keepdims=True) - ffn_unit * jnp.mean(g * ffn_unit, -1, keepdims=True)
    )
    d_att_own = after(d_residual.astype(BF16), grad_ffn_value)
    d_att = gather_group(d_att_own)
    grad_ffn_key = call_grad(key_in, d_hidden, [d_att_own])
    ffn_sums = jnp.stack(
        [
            jnp.sum(d_normed * ffn_unit, 0), jnp.sum(d_normed, 0),
            jnp.sum(ffn_delta * d_fk, 0), jnp.sum(ffn_delta * d_fr, 0),
        ]
    )

    def join_hidden(a):
        if seqs != 2:
            return lax.all_to_all(a, "seq", 0, 1, tiled=True).astype(F32)
        part = a.shape[0] // 2
        kept = lax.dynamic_slice_in_dim(a, me * part, part, 0).astype(F32)
        came = lax.ppermute(lax.dynamic_slice_in_dim(a, (1 - me) * part, part, 0), "seq", SWAP).astype(F32)
        return jnp.where(me == 0, jnp.concatenate([kept, came], 1), jnp.concatenate([came, kept], 1))

    ends_high = ends.astype(BF16)
    ends_low = (ends - ends_high.astype(F32)).astype(BF16)
    moved = after_all(jnp.concatenate([d_gate_cut, ends_high, ends_low], 1), [d_att, grad_ffn_key])
    moved = lax.all_to_all(moved, TP, 0, 0, tiled=True)
    d_gate_own = moved[:, :length].reshape(tokens, cw)
    end_states = moved[:, length : length + HEAD].astype(F32) + moved[:, length + HEAD :].astype(F32)
    own_sums, decay_up, dr, dk, dv, dg, d_pre = call_wkv_backward(
        2 * length, d_att, r, k, v, w, graw, wkv, dm, w_out, own, ones, sum_table(length), start, ends, adjoints, place,
        [grad_ffn_key],
    )
    grads = call_grads([xr, xk, xv, xg, recept_all], [dr, dk, dv, dg, d_gate_own], gated, d_att, segs, ())
    summed = reduce_rows(grads.reshape(-1, cw)).reshape(6, rows_seg, cw)
    more = jnp.concatenate([jnp.sum(own_sums.reshape(4, 8, cw), 1), decay_up[:decays]], 0)
    more = lax.dynamic_update_slice(jnp.zeros((16 * -(-(8 + decays) // 16), width), F32), more, (4, p * cw))
    more = lax.dynamic_update_slice(more, ffn_sums, (0, 0)).astype(BF16)
    packed, *dx = call_mix_backward(
        rank, 2 * length, x_all, rows, lm, dm, dr, dk, dv, dg, d_pre, wn, ww, fn, fw, more, place, four, decays, seqs,
        [grads],
    )
    dx_total, dx_came = reduce_apart(dx)
    input_grad = d_residual + dx_total

    five = summed[:5].reshape(5, group, block, cw).transpose(1, 0, 2, 3).reshape(group, -1, cw)
    grad_ffn_value = join_hidden(grad_ffn_value)
    grad_ffn_key = join_hidden(reduce_rows(grad_ffn_key))
    grad_out = summed[5].reshape(group, cw // segs, cw).transpose(1, 0, 2).reshape(cw // segs, width)
    grad_out = lax.ppermute(
        grad_out, ALL, [(i * group + j, segs * j + i) for i in range(segs) for j in range(group)]
    ).astype(F32)
    small, _ = reduce_segs(lambda s: lax.dynamic_slice_in_dim(packed, s * rows_seg, rows_seg, 1))
    count = small.shape[0]
    small = small.astype(BF16).reshape(count, group, block).transpose(1, 0, 2).reshape(group, -1, cw)
    five = lax.all_to_all(five, TP, 0, 0, tiled=True)
    small = lax.all_to_all(after_all(small, dx_came), TP, 0, 0, tiled=True)
    five = five.reshape(group, 5, block, cw).transpose(1, 2, 0, 3).reshape(5, block, width).astype(F32)
    small = jnp.sum(small.astype(F32).reshape(group, count, block), 0)
    norm_gain, norm_bias, shift_mix = small[0], small[1], small[2:8].T
    at = 16
    shift_down_grad, at = small[at : at + ranks].T, at + ranks
    shift_up_grad, at = small[at : at + ranks].T, at + ranks
    d_down, at = small[at : at + decays].T, at + decays
    ffn_gain, ffn_bias, ffn_shift_mix = small[at], small[at + 1], small[at + 2 : at + 4].T
    decay_base, reward, group_gain, group_bias = (small[at + 4 + i] for i in range(4))
    d_up = small[at + 8 : at + 8 + decays].T
    end_states = end_states.transpose(1, 0, 2).reshape(HEAD, width)
    return (
        output[None],
        end_states[None, None],
        input_grad[None],
        norm_gain,
        norm_bias,
        shift_mix,
        shift_down_grad,
        shift_up_grad,
        decay_base,
        d_down,
        d_up,
        reward,
        five[0],
        five[1],
        five[2],
        five[3],
        grad_out,
        group_gain,
        group_bias,
        ffn_gain,
        ffn_bias,
        ffn_shift_mix,
        grad_ffn_key,
        five[4],
        grad_ffn_value,
    )


def solution(mesh):
    rows, tokens = P("seg", None), P("seg", TP, None)
    matrix = P("seg", "chan")
    vector_out, matrix_out = P(ALL), P(ALL, None)
    ffn_out = P(("seg", "seq"), "chan")
    return jax.shard_map(
        on_device,
        mesh=mesh,
        in_specs=(tokens, P("seg", None, None), P("seg", None, None)) + (P(),) * 9 + (rows,) * 5 + (P(),) * 5
        + (matrix, rows, matrix, tokens, P("seg", TP, None, None)),
        out_specs=(tokens, P("seg", TP, None, None), tokens) + (vector_out,) * 2 + (matrix_out,) * 3 + (vector_out,)
        + (matrix_out,) * 2 + (vector_out,) + (matrix_out,) * 5 + (vector_out,) * 4
        + (matrix_out, ffn_out, matrix_out, ffn_out),
        check_vma=False,
    )
```
